512 devices in a mesh: section: 4 (over y), tm: 4 (over x_lo, core), space: 32 (over z, x_hi).
Axes of the slice: x: 4 (x_hi: 2, x_lo: 2; x = x_hi * 2 + x_lo), y: 4, z: 16, core: 2. Of those that a mesh axis runs over, the one named last changes fastest.
Arguments:
- clip_features: bfloat16 [8, 64, 64, 256], P('tm', 'space'), may hold values from -6 to 6
- conv_kernels: bfloat16 [4, 9, 768, 256], P('section'), may hold values from -0.078125 to 0.078125
- norm_gains: float32 [4, 256], P('section'), may hold values from 0.1 to 1.9
Outputs:
- section_outputs: bfloat16 [4, 8, 64, 64, 256], P('section', 'tm', 'space')
The draws below stay inside these ranges and needn't reach their ends.
All inputs are finite; a program needn't handle non-finite values.
Results may differ from the reference program's by a relative error of at most 0.018.
Values may be sent and summed in bfloat16 or wider, within the bound.
A program may use at most 64 MiB of HBM per device.

```python
import jax
import jax.numpy as jnp
from jax import lax

C = 256
W = 64
SECTIONS = 4
FRAMES = 8
H = 64


def levels(own_key, shape, shards, least, top_value):
    factor_of, own = 1.0, jax.random.fold_in(own_key, 6)
    for dim, parts in shards:
        heights = jnp.exp(jax.random.uniform(jax.random.fold_in(own, dim), (parts,), jnp.float32, least / len(shards), top_value / len(shards)))
        factor_of = factor_of * jnp.repeat(heights, shape[dim] // parts).reshape([-1 if axis == dim else 1 for axis in range(len(shape))])
    return factor_of


def bell_draw(rng, extent, deviation, limit, pieces=(), held_as=jnp.bfloat16):
    values = deviation * jax.random.normal(rng, extent, jnp.float32)
    if pieces:
        values = values * levels(rng, extent, pieces, -0.22, 0.18)
    return jnp.clip(values, -limit, limit).astype(held_as)


def setup_inputs(seed: int = 0) -> dict:
    streams_of = jax.random.split(jax.random.key(seed), 4)
    clip_features = bell_draw(streams_of[0], (FRAMES, H, W, C), 1.0, 6.0, ((0, 4), (1, 32)))
    conv_kernels = bell_draw(streams_of[1], (SECTIONS, 9, 3 * C, C), (27 * C) ** -0.5, 0.078125, ((0, 4),))
    norm_gains = jnp.clip(1.0 + 0.18 * jax.random.normal(streams_of[2], (SECTIONS, C), jnp.float32), 0.1, 1.9)
    return {"clip_features": clip_features, "conv_kernels": conv_kernels, "norm_gains": norm_gains}


def normed(inputs, norm_gain):
    wide = inputs.astype(jnp.float32)
    factor = lax.rsqrt(lax.optimization_barrier(jnp.mean(wide * wide, axis=-1, keepdims=True)) + 1e-06)
    return jax.nn.silu(wide * factor * norm_gain).astype(jnp.bfloat16)

def convolve_frames(hidden, kernel):
    frame_count, row_count, col_count, channels = hidden.shape
    padded = jnp.pad(hidden, ((2, 0), (1, 1), (1, 1), (0, 0)))

    def one_frame(index):
        window = lax.dynamic_slice_in_dim(padded, index, 3, 0)
        summed = jnp.zeros((row_count * col_count, channels), jnp.float32)
        for time_tap in range(3):
            for row_tap in range(3):
                plane = window[time_tap, row_tap:row_tap + row_count]
                stacked = jnp.concatenate([plane[:, 0:col_count], plane[:, 1:col_count + 1], plane[:, 2:col_count + 2]], axis=-1)
                summed = summed + jnp.dot(stacked.reshape(-1, 3 * channels), kernel[3 * time_tap + row_tap], preferred_element_type=jnp.float32)
        return summed.reshape(row_count, col_count, channels)
    return lax.map(one_frame, jnp.arange(frame_count, dtype=jnp.int32))

def reference(clip_features, conv_kernels, norm_gains):
    current = clip_features
    layer_outs = []
    for layer in range(SECTIONS):
        hidden = normed(current, norm_gains[layer])
        current = (current.astype(jnp.float32) + convolve_frames(hidden, conv_kernels[layer])).astype(jnp.bfloat16)
        layer_outs.append(current)
    return jnp.stack(layer_outs, 0)
```

```python
import functools

import jax
import jax.numpy as jnp
from jax import lax
from jax.experimental import pallas as pl
from jax.experimental.pallas import tpu as pltpu
from jax.sharding import PartitionSpec as P

MESH = pl.DeviceIdType.MESH
WORKER = 0
TAPS = 3


def chain_kernel(
    clip, weights, gains, out,
    x_in, hidden, filters, gain, rows_out,
    x_sem, home_sem, init_send, next_send, home_send, load_sem,
):
    section = lax.axis_index("section")
    tm = lax.axis_index("tm")
    space = lax.axis_index("space")
    sections = lax.axis_size("section")
    groups = lax.axis_size("tm")
    bands = lax.axis_size("space")
    run = tm // 2
    row = 2 * space + run
    last_row = 2 * bands - 1
    worker = tm % 2 == WORKER
    frames, _, columns, channels = clip.shape
    cells = frames * columns

    def row_device(at_section, at_row):
        at_section = jnp.clip(at_section, 0, sections - 1)
        at_row = jnp.clip(at_row, 0, last_row)
        return (at_section, 2 * (at_row % 2) + WORKER, at_row // 2)

    load_filters = pltpu.make_async_copy(weights.at[0], filters, load_sem.at[0])
    load_gain = pltpu.make_async_copy(gains, gain, load_sem.at[1])

    @pl.when(worker)
    def _():
        load_gain.start()
        load_filters.start()

    barrier = pltpu.get_barrier_semaphore()

    def greet(device):
        pl.semaphore_signal(barrier, inc=1, device_id=device, device_id_type=MESH)

    def init_targets():
        return (
            (None, 0, 2 * space, 1),
            (None, 1, 2 * space, 2),
            (None, 0, 2 * space + 1, 0),
            (None, 1, 2 * space + 1, 1),
            (space > 0, 0, 2 * space - 1, 2),
            (space < bands - 1, 1, 2 * space + 2, 0),
        )

    for group in range(groups):
        @pl.when((section == 0) & worker & (group != tm))
        def _(group=group):
            greet((0, group, space))

        @pl.when((section == 0) & worker & (run == 0) & (space > 0))
        def _(group=group):
            greet((0, group, jnp.maximum(space - 1, 0)))

        @pl.when((section == 0) & worker & (run == 1) & (space < bands - 1))
        def _(group=group):
            greet((0, group, jnp.minimum(space + 1, bands - 1)))

    for step in (-1, 0, 1):
        @pl.when((section > 0) & worker & (row + step >= 0) & (row + step <= last_row))
        def _(step=step):
            greet(row_device(section - 1, row + step))

    for near in range(2):
        @pl.when(tm != 2 * near + WORKER)
        def _(near=near):
            greet((section, 2 * near + WORKER, space))

    @pl.when(worker)
    def _():
        hidden[0:frames] = jnp.zeros((frames, *hidden.shape[1:]), hidden.dtype)

    @pl.when(worker & (row == 0))
    def _():
        x_in[:, 0] = jnp.zeros((groups, *x_in.shape[2:]), x_in.dtype)

    @pl.when(worker & (row == last_row))
    def _():
        x_in[:, 2] = jnp.zeros((groups, *x_in.shape[2:]), x_in.dtype)

    def has_next(step):
        return (section < sections - 1) & (row + step >= 0) & (row + step <= last_row)

    def one_if(condition):
        return jnp.where(condition, 1, 0)

    from_clip = one_if(section == 0) * (
        2 - one_if(worker) + one_if(space > 0) + one_if(space < bands - 1)
    )
    from_rows = one_if(worker) * (
        groups - 1 + one_if(has_next(-1)) + one_if(has_next(0)) + one_if(has_next(1))
    )
    receivers = from_clip + from_rows

    @pl.when(receivers > 0)
    def _():
        pl.semaphore_wait(barrier, receivers)

    def init_copies():
        copies = []
        for k, (condition, source, target, tap) in enumerate(init_targets()):
            own = (target % 2 == run) & worker & (k < 4)
            remote = pltpu.make_async_remote_copy(
                src_ref=clip.at[:, source],
                dst_ref=x_in.at[tm, tap],
                send_sem=init_send.at[k],
                recv_sem=x_sem.at[tm, tap],
                device_id=row_device(0, target),
                device_id_type=MESH,
            )
            local = pltpu.make_async_copy(clip.at[:, source], x_in.at[tm, tap], x_sem.at[tm, tap])
            copies.append((condition, own, remote, local))
        return copies

    @pl.when(section == 0)
    def _():
        for condition, own, remote, local in init_copies():
            if condition is None:
                @pl.when(own)
                def _(local=local):
                    local.start()

                @pl.when(jnp.logical_not(own))
                def _(remote=remote):
                    remote.start()
            else:
                @pl.when(condition)
                def _(remote=remote):
                    remote.start()

    def next_copy(group, step):
        return pltpu.make_async_remote_copy(
            src_ref=rows_out.at[group],
            dst_ref=x_in.at[group, 1 - step],
            send_sem=next_send.at[group, step + 1],
            recv_sem=x_sem.at[group, 1 - step],
            device_id=row_device(section + 1, row + step),
            device_id_type=MESH,
        )

    def home_copy(group):
        return pltpu.make_async_remote_copy(
            src_ref=rows_out.at[group],
            dst_ref=out.at[0, :, run],
            send_sem=home_send.at[group],
            recv_sem=home_sem.at[run],
            device_id=(section, group, space),
            device_id_type=MESH,
        )

    def own_copy(group):
        return pltpu.make_async_copy(rows_out.at[group], out.at[0, :, run], home_sem.at[run])

    def process(group, carry):
        first = group * frames
        for tap in (1, 0, 2):
            @pl.when((row + tap - 1 >= 0) & (row + tap - 1 <= last_row))
            def _(tap=tap):
                pltpu.make_async_copy(x_in.at[group, tap], x_in.at[group, tap], x_sem.at[group, tap]).wait()

            wide = x_in[group, tap].reshape(cells, channels).astype(jnp.float32)
            factor = lax.rsqrt(jnp.mean(wide * wide, axis=-1, keepdims=True) + 1e-06)
            value = wide * factor * gain[...]
            value = value / (1.0 + jnp.exp(-value))
            column = lax.broadcasted_iota(jnp.int32, value.shape, 0) % columns
            left = jnp.where(column == 0, 0.0, pltpu.roll(value, 1, 0))
            right = jnp.where(column == columns - 1, 0.0, pltpu.roll(value, cells - 1, 0))
            for part, shifted in enumerate((left, value, right)):
                hidden[pl.ds(first + frames, frames), tap, :, part * channels:(part + 1) * channels] = (
                    shifted.astype(jnp.bfloat16).reshape(frames, columns, channels)
                )

        @pl.when(group == 0)
        def _():
            load_filters.wait()

        total = x_in[group, 1].reshape(cells, channels).astype(jnp.float32)
        summed = jnp.zeros((cells, channels), jnp.float32)
        for time_tap in range(TAPS):
            for row_tap in range(TAPS):
                window = hidden[pl.ds(first + frames - 2 + time_tap, frames), row_tap]
                summed = summed + jnp.dot(
                    window.reshape(cells, TAPS * channels),
                    filters[TAPS * time_tap + row_tap],
                    preferred_element_type=jnp.float32,
                )
        rows_out[group] = (total + summed).astype(jnp.bfloat16).reshape(frames, columns, channels)

        for step in (-1, 1, 0):
            @pl.when(has_next(step))
            def _(step=step):
                next_copy(group, step).start()

        @pl.when(group == tm)
        def _():
            own_copy(group).start()

        @pl.when(group != tm)
        def _():
            home_copy(group).start()

        return carry

    @pl.when(worker)
    def _():
        load_gain.wait()
        lax.fori_loop(0, groups, process, 0)

    for near in range(2):
        arrived = out.at[0, :, near]
        pltpu.make_async_copy(arrived, arrived, home_sem.at[near]).wait()

    @pl.when(section == 0)
    def _():
        for condition, own, remote, _ in init_copies():
            needed = jnp.logical_not(own) if condition is None else condition

            @pl.when(needed)
            def _(remote=remote):
                remote.wait_send()

    def drain(group, carry):
        for step in (-1, 1, 0):
            @pl.when(has_next(step))
            def _(step=step):
                next_copy(group, step).wait_send()

        @pl.when(group != tm)
        def _():
            home_copy(group).wait_send()

        return carry

    @pl.when(worker)
    def _():
        lax.fori_loop(0, groups, drain, 0)


def on_device(clip_features, conv_kernels, norm_gains):
    frames, rows, columns, channels = clip_features.shape
    groups = lax.axis_size("tm")
    any_space = pl.BlockSpec(memory_space=pltpu.HBM)
    return pl.pallas_call(
        chain_kernel,
        out_shape=jax.ShapeDtypeStruct((1, frames, rows, columns, channels), jnp.bfloat16),
        in_specs=[any_space] * 3,
        out_specs=any_space,
        scratch_shapes=[
            pltpu.VMEM((groups, TAPS, frames, columns, channels), jnp.bfloat16),
            pltpu.VMEM(((groups + 1) * frames, TAPS, columns, TAPS * channels), jnp.bfloat16),
            pltpu.VMEM(conv_kernels.shape[1:], jnp.bfloat16),
            pltpu.VMEM(norm_gains.shape, jnp.float32),
            pltpu.VMEM((groups, frames, columns, channels), jnp.bfloat16),
            pltpu.SemaphoreType.DMA((groups, TAPS)),
            pltpu.SemaphoreType.DMA((2,)),
            pltpu.SemaphoreType.DMA((6,)),
            pltpu.SemaphoreType.DMA((groups, TAPS)),
            pltpu.SemaphoreType.DMA((groups,)),
            pltpu.SemaphoreType.DMA((2,)),
        ],
        compiler_params=pltpu.CompilerParams(
            collective_id=0, has_side_effects=True, vmem_limit_bytes=56 * 2**20
        ),
        name="chain",
    )(clip_features, conv_kernels, norm_gains)


def solution(mesh):
    return jax.shard_map(
        on_device,
        mesh=mesh,
        in_specs=(P("tm", "space", None, None), P("section", None, None, None), P("section", None)),
        out_specs=P("section", "tm", "space", None, None),
        check_vma=False,
    )
```

```python
import functools

import jax
import jax.numpy as jnp
from jax import lax
from jax.experimental import pallas as pl
from jax.experimental.pallas import tpu as pltpu
from jax.sharding import PartitionSpec as P

MESH = pl.DeviceIdType.MESH
WORKER = 1
TAPS = 3


def chain_kernel(
    clip, weights, gains, out,
    x_in, hidden, filters, gain, rows_out,
    x_sem, home_sem, init_send, next_send, home_send, load_sem,
):
    section = lax.axis_index("section")
    tm = lax.axis_index("tm")
    space = lax.axis_index("space")
    sections = lax.axis_size("section")
    groups = lax.axis_size("tm")
    bands = lax.axis_size("space")
    run = tm // 2
    row = 2 * space + run
    last_row = 2 * bands - 1
    worker = tm % 2 == WORKER
    frames, _, columns, channels = clip.shape
    cells = frames * columns

    def row_device(at_section, at_row):
        at_section = jnp.clip(at_section, 0, sections - 1)
        at_row = jnp.clip(at_row, 0, last_row)
        return (at_section, 2 * (at_row % 2) + WORKER, at_row // 2)

    load_filters = pltpu.make_async_copy(weights.at[0], filters, load_sem.at[0])
    load_gain = pltpu.make_async_copy(gains, gain, load_sem.at[1])

    @pl.when(worker)
    def _():
        load_gain.start()
        load_filters.start()

    barrier = pltpu.get_barrier_semaphore()

    def greet(device):
        pl.semaphore_signal(barrier, inc=1, device_id=device, device_id_type=MESH)

    def init_targets():
        return (
            (None, 0, 2 * space, 1),
            (None, 1, 2 * space, 2),
            (None, 0, 2 * space + 1, 0),
            (None, 1, 2 * space + 1, 1),
            (space > 0, 0, 2 * space - 1, 2),
            (space < bands - 1, 1, 2 * space + 2, 0),
        )

    sender = section == tm % sections
    for group in range(groups):
        source = group % sections

        @pl.when((section == 0) & worker & ((source != 0) | (group != tm)))
        def _(group=group, source=source):
            greet((source, group, space))

        @pl.when((section == 0) & worker & (run == 0) & (space > 0))
        def _(group=group, source=source):
            greet((source, group, jnp.maximum(space - 1, 0)))

        @pl.when((section == 0) & worker & (run == 1) & (space < bands - 1))
        def _(group=group, source=source):
            greet((source, group, jnp.minimum(space + 1, bands - 1)))

    for step in (-1, 0, 1):
        @pl.when((section > 0) & worker & (row + step >= 0) & (row + step <= last_row))
        def _(step=step):
            greet(row_device(section - 1, row + step))

    for near in range(2):
        @pl.when(tm != 2 * near + WORKER)
        def _(near=near):
            greet((section, 2 * near + WORKER, space))

    @pl.when(worker)
    def _():
        hidden[0:frames] = jnp.zeros((frames, *hidden.shape[1:]), hidden.dtype)

    @pl.when(worker & (row == 0))
    def _():
        x_in[:, 0] = jnp.zeros((groups, *x_in.shape[2:]), x_in.dtype)

    @pl.when(worker & (row == last_row))
    def _():
        x_in[:, 2] = jnp.zeros((groups, *x_in.shape[2:]), x_in.dtype)

    def has_next(step):
        return (section < sections - 1) & (row + step >= 0) & (row + step <= last_row)

    def one_if(condition):
        return jnp.where(condition, 1, 0)

    from_clip = one_if(sender) * (
        2 - one_if(worker & (section == 0)) + one_if(space > 0) + one_if(space < bands - 1)
    )
    from_rows = one_if(worker) * (
        groups - 1 + one_if(has_next(-1)) + one_if(has_next(0)) + one_if(has_next(1))
    )
    receivers = from_clip + from_rows

    @pl.when(receivers > 0)
    def _():
        pl.semaphore_wait(barrier, receivers)

    def init_copies():
        copies = []
        for k, (condition, source, target, tap) in enumerate(init_targets()):
            own = (section == 0) & (target % 2 == run) & worker & (k < 4)
            remote = pltpu.make_async_remote_copy(
                src_ref=clip.at[:, source],
                dst_ref=x_in.at[tm, tap],
                send_sem=init_send.at[k],
                recv_sem=x_sem.at[tm, tap],
                device_id=row_device(0, target),
                device_id_type=MESH,
            )
            local = pltpu.make_async_copy(clip.at[:, source], x_in.at[tm, tap], x_sem.at[tm, tap])
            copies.append((condition, own, remote, local))
        return copies

    @pl.when(sender)
    def _():
        for condition, own, remote, local in init_copies():
            if condition is None:
                @pl.when(own)
                def _(local=local):
                    local.start()

                @pl.when(jnp.logical_not(own))
                def _(remote=remote):
                    remote.start()
            else:
                @pl.when(condition)
                def _(remote=remote):
                    remote.start()

    def next_copy(group, step):
        return pltpu.make_async_remote_copy(
            src_ref=rows_out.at[group],
            dst_ref=x_in.at[group, 1 - step],
            send_sem=next_send.at[group, step + 1],
            recv_sem=x_sem.at[group, 1 - step],
            device_id=row_device(section + 1, row + step),
            device_id_type=MESH,
        )

    def home_copy(group):
        return pltpu.make_async_remote_copy(
            src_ref=rows_out.at[group],
            dst_ref=out.at[0, :, run],
            send_sem=home_send.at[group],
            recv_sem=home_sem.at[run],
            device_id=(section, group, space),
            device_id_type=MESH,
        )

    def own_copy(group):
        return pltpu.make_async_copy(rows_out.at[group], out.at[0, :, run], home_sem.at[run])

    def process(group, carry):
        first = group * frames
        for tap in (1, 0, 2):
            @pl.when((row + tap - 1 >= 0) & (row + tap - 1 <= last_row))
            def _(tap=tap):
                pltpu.make_async_copy(x_in.at[group, tap], x_in.at[group, tap], x_sem.at[group, tap]).wait()

            wide = x_in[group, tap].reshape(cells, channels).astype(jnp.float32)
            factor = lax.rsqrt(jnp.mean(wide * wide, axis=-1, keepdims=True) + 1e-06)
            value = wide * factor * gain[...]
            value = value / (1.0 + jnp.exp(-value))
            column = lax.broadcasted_iota(jnp.int32, value.shape, 0) % columns
            left = jnp.where(column == 0, 0.0, pltpu.roll(value, 1, 0))
            right = jnp.where(column == columns - 1, 0.0, pltpu.roll(value, cells - 1, 0))
            for part, shifted in enumerate((left, value, right)):
                hidden[pl.ds(first + frames, frames), tap, :, part * channels:(part + 1) * channels] = (
                    shifted.astype(jnp.bfloat16).reshape(frames, columns, channels)
                )

        @pl.when(group == 0)
        def _():
            load_filters.wait()

        total = x_in[group, 1].reshape(cells, channels).astype(jnp.float32)
        summed = jnp.zeros((cells, channels), jnp.float32)
        for time_tap in range(TAPS):
            for row_tap in range(TAPS):
                window = hidden[pl.ds(first + frames - 2 + time_tap, frames), row_tap]
                summed = summed + jnp.dot(
                    window.reshape(cells, TAPS * channels),
                    filters[TAPS * time_tap + row_tap],
                    preferred_element_type=jnp.float32,
                )
        rows_out[group] = (total + summed).astype(jnp.bfloat16).reshape(frames, columns, channels)

        for step in (-1, 1, 0):
            @pl.when(has_next(step))
            def _(step=step):
                next_copy(group, step).start()

        @pl.when(group == tm)
        def _():
            own_copy(group).start()

        @pl.when(group != tm)
        def _():
            home_copy(group).start()

        return carry

    @pl.when(worker)
    def _():
        load_gain.wait()
        lax.fori_loop(0, groups, process, 0)

    for near in range(2):
        arrived = out.at[0, :, near]
        pltpu.make_async_copy(arrived, arrived, home_sem.at[near]).wait()

    @pl.when(sender)
    def _():
        for condition, own, remote, _ in init_copies():
            needed = jnp.logical_not(own) if condition is None else condition

            @pl.when(needed)
            def _(remote=remote):
                remote.wait_send()

    def drain(group, carry):
        for step in (-1, 1, 0):
            @pl.when(has_next(step))
            def _(step=step):
                next_copy(group, step).wait_send()

        @pl.when(group != tm)
        def _():
            home_copy(group).wait_send()

        return carry

    @pl.when(worker)
    def _():
        lax.fori_loop(0, groups, drain, 0)


def on_device(clip_features, conv_kernels, norm_gains):
    frames, rows, columns, channels = clip_features.shape
    groups = lax.axis_size("tm")
    any_space = pl.BlockSpec(memory_space=pltpu.HBM)
    return pl.pallas_call(
        chain_kernel,
        out_shape=jax.ShapeDtypeStruct((1, frames, rows, columns, channels), jnp.bfloat16),
        in_specs=[any_space] * 3,
        out_specs=any_space,
        scratch_shapes=[
            pltpu.VMEM((groups, TAPS, frames, columns, channels), jnp.bfloat16),
            pltpu.VMEM(((groups + 1) * frames, TAPS, columns, TAPS * channels), jnp.bfloat16),
            pltpu.VMEM(conv_kernels.shape[1:], jnp.bfloat16),
            pltpu.VMEM(norm_gains.shape, jnp.float32),
            pltpu.VMEM((groups, frames, columns, channels), jnp.bfloat16),
            pltpu.SemaphoreType.DMA((groups, TAPS)),
            pltpu.SemaphoreType.DMA((2,)),
            pltpu.SemaphoreType.DMA((6,)),
            pltpu.SemaphoreType.DMA((groups, TAPS)),
            pltpu.SemaphoreType.DMA((groups,)),
            pltpu.SemaphoreType.DMA((2,)),
        ],
        compiler_params=pltpu.CompilerParams(
            collective_id=0, has_side_effects=True, vmem_limit_bytes=56 * 2**20
        ),
        name="chain",
    )(clip_features, conv_kernels, norm_gains)


def solution(mesh):
    return jax.shard_map(
        on_device,
        mesh=mesh,
        in_specs=(P("tm", "space", None, None), P("section", None, None, None), P("section", None)),
        out_specs=P("section", "tm", "space", None, None),
        check_vma=False,
    )
```

```python
import jax
import jax.numpy as jnp
from jax import lax
from jax.experimental import pallas as pl
from jax.experimental.pallas import tpu as pltpu
from jax.sharding import PartitionSpec as P

MESH = pl.DeviceIdType.MESH
WORKER = 1
TAPS = 3
TALL = 4
TILES = 4
LANES = 128


def chain_kernel(
    clip, weights, gains, out,
    own_in, row_in, edge_in, hidden, halo, filters, gain, wide_out, tile_out, edge_out,
    clip_in, clip_wide, clip_edge,
    own_sem, row_sem, edge_sem, home_sem, clip_send, next_send, home_send, load_sem,
):
    section = lax.axis_index("section")
    tm = lax.axis_index("tm")
    space = lax.axis_index("space")
    sections = lax.axis_size("section")
    groups = lax.axis_size("tm")
    bands = lax.axis_size("space") // 2
    band = space // 2
    half = space % 2
    tile = 2 * half + tm // 2
    worker = tm % 2 == WORKER
    sender = section == tm % sections
    frames, pair, columns, channels = clip.shape
    wide = columns // TILES
    cells = frames * TALL * wide
    edge_cells = frames * TALL
    beside = band + 2 * half - 1
    has_beside = (beside >= 0) & (beside < bands)

    def worker_device(at_section, at_tile, at_band):
        at_section = jnp.clip(at_section, 0, sections - 1)
        at_tile = jnp.clip(at_tile, 0, TILES - 1)
        at_band = jnp.clip(at_band, 0, bands - 1)
        return (at_section, 2 * (at_tile % 2) + WORKER, 2 * at_band + at_tile // 2)

    def inside(step_tile, step_band):
        there = None
        for at, step, end in ((tile, step_tile, TILES), (band, step_band, bands)):
            if step:
                here = (at > 0) if step < 0 else (at < end - 1)
                there = here if there is None else there & here
        return there

    def when(condition, action):
        if condition is None:
            action()
        else:
            pl.when(condition)(action)

    barrier = pltpu.get_barrier_semaphore()

    def greet(device):
        pl.semaphore_signal(barrier, inc=1, device_id=device, device_id_type=MESH)

    @pl.when(worker & (section == 0))
    def _():
        for group in range(groups):
            for near in range(2):
                greet((group % sections, group, 2 * band + near))

        @pl.when(band > 0)
        def _():
            for group in range(groups):
                greet((group % sections, group, jnp.maximum(2 * band - 1, 0)))

        @pl.when(band < bands - 1)
        def _():
            for group in range(groups):
                greet((group % sections, group, jnp.minimum(2 * band + 2, 2 * bands - 1)))

    load_filters = pltpu.make_async_copy(weights.at[0], filters, load_sem.at[0])
    load_gain = pltpu.make_async_copy(gains, gain, load_sem.at[1])
    load_clip = pltpu.make_async_copy(clip, clip_in, load_sem.at[2])

    @pl.when(sender)
    def _():
        load_clip.start()

    @pl.when(worker)
    def _():
        load_gain.start()
        load_filters.start()

    steps = [(t, b) for t in (-1, 1, 0) for b in (-1, 1, 0)]

    @pl.when(worker & (section > 0))
    def _():
        for t, b in steps:
            when(inside(t, b), lambda t=t, b=b: greet(worker_device(section - 1, tile + t, band + b)))

    for near in range(TILES):
        @pl.when(jnp.logical_not(worker & (tile == near)))
        def _(near=near):
            greet(worker_device(section, near, band))

    @pl.when(worker)
    def _():
        hidden[0:frames] = jnp.zeros((frames, *hidden.shape[1:]), hidden.dtype)

        @pl.when(band == 0)
        def _():
            row_in[:, 0] = jnp.zeros((groups, *row_in.shape[2:]), row_in.dtype)
            edge_in[:, :, 0] = jnp.zeros((groups, 2, *edge_in.shape[3:]), edge_in.dtype)

        @pl.when(band == bands - 1)
        def _():
            row_in[:, 1] = jnp.zeros((groups, *row_in.shape[2:]), row_in.dtype)
            edge_in[:, :, 3] = jnp.zeros((groups, 2, *edge_in.shape[3:]), edge_in.dtype)

        @pl.when(section > 0)
        def _():
            edge_in[:, :, 2] = jnp.zeros((groups, 2, *edge_in.shape[3:]), edge_in.dtype)

        @pl.when(tile == 0)
        def _():
            edge_in[:, 0] = jnp.zeros((groups, *edge_in.shape[2:]), edge_in.dtype)

        @pl.when(tile == TILES - 1)
        def _():
            edge_in[:, 1] = jnp.zeros((groups, *edge_in.shape[2:]), edge_in.dtype)

    left_edges = [(0, at, at * wide - 1) for at in range(1, TILES)]
    right_edges = [(1, at, at * wide + wide) for at in range(TILES - 1)]
    clip_edges = left_edges + right_edges

    @pl.when(sender)
    def _():
        load_clip.wait()
        for n in range(channels // LANES):
            clip_wide[n] = clip_in[:, :, :, n * LANES:(n + 1) * LANES].reshape(-1, LANES).astype(jnp.float32)
        for n, (_, _, column) in enumerate(clip_edges):
            parts = []
            for lane in range(channels // LANES):
                part = clip_wide[lane, pl.ds(column, frames * pair, stride=columns), :]
                parts += [part, part]
            clip_edge[n] = jnp.concatenate(parts, axis=0).astype(jnp.bfloat16)

    def one_if(condition):
        return jnp.where(condition, 1, 0)

    near_tiles = 1 + one_if(tile > 0) + one_if(tile < TILES - 1)
    near_bands = 1 + one_if(band > 0) + one_if(band < bands - 1)
    receivers = (
        one_if(sender) * TILES * (1 + one_if(has_beside))
        + one_if(worker) * (2 * groups - 1 + one_if(section < sections - 1) * near_tiles * near_bands)
    )

    @pl.when(receivers > 0)
    def _():
        pl.semaphore_wait(barrier, receivers)

    def clip_copies():
        copies = []

        def add(condition, source, target, arrived, at_tile, at_band):
            copies.append((condition, pltpu.make_async_remote_copy(
                src_ref=source,
                dst_ref=target,
                send_sem=clip_send.at[len(copies)],
                recv_sem=arrived,
                device_id=worker_device(0, at_tile, at_band),
                device_id_type=MESH,
            )))

        for n, (side, at, _) in enumerate(clip_edges):
            piece = 3 * (1 - half)
            add(has_beside, clip_edge.at[n], edge_in.at[tm, side, piece], edge_sem.at[tm, side, piece], at, beside)
        for at in range(TILES):
            add(has_beside, clip.at[:, half, at * wide:(at + 1) * wide], row_in.at[tm, 1 - half],
                row_sem.at[tm, 1 - half], at, beside)
        for n, (side, at, _) in enumerate(clip_edges):
            piece = 1 + half
            add(None, clip_edge.at[n], edge_in.at[tm, side, piece], edge_sem.at[tm, side, piece], at, band)
        for at in range(TILES):
            add(None, clip.at[:, :, at * wide:(at + 1) * wide], own_in.at[tm, :, pl.ds(pair * half, pair)],
                own_sem.at[tm, half], at, band)
        return copies

    @pl.when(sender)
    def _():
        for condition, copy in clip_copies():
            when(condition, copy.start)

    def next_copies(group):
        copies = []
        for n, (t, b) in enumerate(steps):
            if t:
                side, piece = (1 if t < 0 else 0), {-1: 3, 0: 1, 1: 0}[b]
                source = edge_out.at[group, 1 - side]
                target, arrived = edge_in.at[group, side, piece], edge_sem.at[group, side, piece]
            elif b:
                source = tile_out.at[group, :, 0 if b < 0 else TALL - 1]
                above = 1 if b < 0 else 0
                target, arrived = row_in.at[group, above], row_sem.at[group, above]
            else:
                source, target, arrived = tile_out.at[group], own_in.at[group], own_sem.at[group, 0]
            copies.append((inside(t, b), pltpu.make_async_remote_copy(
                src_ref=source,
                dst_ref=target,
                send_sem=next_send.at[group, n],
                recv_sem=arrived,
                device_id=worker_device(section + 1, tile + t, band + b),
                device_id_type=MESH,
            )))
        return copies

    def home_target():
        return out.at[0, :, :, pl.ds(pl.multiple_of(tile * wide, wide), wide)]

    def home_copy(group, near):
        return pltpu.make_async_remote_copy(
            src_ref=tile_out.at[group, :, near * pair:(near + 1) * pair],
            dst_ref=home_target(),
            send_sem=home_send.at[group, near],
            recv_sem=home_sem.at[tile],
            device_id=(section, group, 2 * band + near),
            device_id_type=MESH,
        )

    def own_copy(group, near):
        source = tile_out.at[group, :, near * pair:(near + 1) * pair]
        return pltpu.make_async_copy(source, home_target(), home_sem.at[tile])

    def arrived(ref, sem):
        pltpu.make_async_copy(ref, ref, sem).wait()

    def activated(value):
        factor = lax.rsqrt(jnp.mean(value * value, axis=-1, keepdims=True) + 1e-06)
        value = value * factor * gain[...]
        return value / (1.0 + jnp.exp(-value))

    def process(group, carry):
        first = group * frames

        for side, t in ((0, -1), (1, 1)):
            for piece, b in ((0, -1), (1, 0), (3, 1)):
                when(inside(t, b), lambda side=side, piece=piece: arrived(
                    edge_in.at[group, side, piece], edge_sem.at[group, side, piece]))

            @pl.when((section == 0) & inside(t, 0))
            def _(side=side):
                arrived(edge_in.at[group, side, 2], edge_sem.at[group, side, 2])

        for above, b in ((0, -1), (1, 1)):
            when(inside(0, b), lambda above=above: arrived(row_in.at[group, above], row_sem.at[group, above]))

        @pl.when(section == 0)
        def _():
            for near in range(2):
                arrived(own_in.at[group, :, near * pair:(near + 1) * pair], own_sem.at[group, near])

        @pl.when(section > 0)
        def _():
            arrived(own_in.at[group], own_sem.at[group, 0])

        lower = lax.broadcasted_iota(jnp.int32, (edge_cells, channels), 0) >= edge_cells // 2
        pieces = []
        for side in range(2):
            above, middle, under, below = (
                jnp.concatenate(
                    [edge_in[group, side, p][n * edge_cells:(n + 1) * edge_cells].astype(jnp.float32)
                     for n in range(channels // LANES)],
                    axis=1,
                )
                for p in range(4)
            )
            pieces += [above, jnp.where(lower & (section == 0), under, middle), below]
        halo[...] = activated(jnp.concatenate(pieces, axis=0))

        own = own_in[group].reshape(cells, channels).astype(jnp.float32)
        middle = activated(own).reshape(frames, TALL, wide, channels)
        outer = activated(row_in[group].reshape(2 * frames * wide, channels).astype(jnp.float32))
        outer = outer.reshape(2, frames, wide, channels)
        column = lax.broadcasted_iota(jnp.int32, (wide, channels), 0)
        for frame in range(frames):
            for row in range(TALL + 2):
                if row == 0:
                    here, at = outer[0, frame], edge_cells // 2 + pair * frame + pair - 1
                elif row == TALL + 1:
                    here, at = outer[1, frame], 2 * edge_cells + pair * frame
                else:
                    part, within = divmod(row - 1, pair)
                    here = middle[frame, row - 1]
                    at = edge_cells + part * (edge_cells // 2) + pair * frame + within
                left = jnp.where(column == 0, halo[pl.ds(at, 1), :], pltpu.roll(here, 1, 0))
                at += TAPS * edge_cells
                right = jnp.where(column == wide - 1, halo[pl.ds(at, 1), :], pltpu.roll(here, wide - 1, 0))
                for part, shifted in enumerate((left, here, right)):
                    hidden[first + frames + frame, row, :, part * channels:(part + 1) * channels] = (
                        shifted.astype(jnp.bfloat16)
                    )

        @pl.when(group == 0)
        def _():
            load_filters.wait()

        summed = jnp.zeros((cells, channels), jnp.float32)
        for time_tap in range(TAPS):
            for row_tap in range(TAPS):
                window = hidden[pl.ds(first + frames - 2 + time_tap, frames), row_tap:row_tap + TALL]
                summed = summed + jnp.dot(
                    window.reshape(cells, TAPS * channels),
                    filters[TAPS * time_tap + row_tap],
                    preferred_element_type=jnp.float32,
                )
        result = own + summed
        tile_out[group] = result.astype(jnp.bfloat16).reshape(frames, TALL, wide, channels)

        @pl.when(section < sections - 1)
        def _():
            block = pair * wide
            for frame in range(frames):
                for part in range(TALL // pair):
                    source = (frame * (TALL // pair) + part) * block
                    for n in range(channels // LANES):
                        wide_out[n, pl.ds((part * frames + frame) * block, block), :] = (
                            result[source:source + block, n * LANES:(n + 1) * LANES]
                        )
            for side, at in enumerate((0, wide - 1)):
                parts = [
                    wide_out[n, pl.ds(at, edge_cells, stride=wide), :]
                    for n in range(channels // LANES)
                ]
                edge_out[group, side] = jnp.concatenate(parts, axis=0).astype(jnp.bfloat16)
            for condition, copy in next_copies(group):
                when(condition, copy.start)

        for near in range(2):
            own_home = (group == tm) & (near == half)

            @pl.when(own_home)
            def _(near=near):
                own_copy(group, near).start()

            @pl.when(jnp.logical_not(own_home))
            def _(near=near):
                home_copy(group, near).start()

        return carry

    @pl.when(worker)
    def _():
        load_gain.wait()
        lax.fori_loop(0, groups, process, 0)

    for at in range(TILES):
        arrived(out.at[0, :, :, at * wide:(at + 1) * wide], home_sem.at[at])

    @pl.when(sender)
    def _():
        for condition, copy in clip_copies():
            when(condition, copy.wait_send)

    def drain(group, carry):
        @pl.when(section < sections - 1)
        def _():
            for condition, copy in next_copies(group):
                when(condition, copy.wait_send)

        for near in range(2):
            @pl.when(jnp.logical_not((group == tm) & (near == half)))
            def _(near=near):
                home_copy(group, near).wait_send()

        return carry

    @pl.when(worker)
    def _():
        lax.fori_loop(0, groups, drain, 0)


def on_device(clip_features, conv_kernels, norm_gains):
    frames, pair, columns, channels = clip_features.shape
    groups = lax.axis_size("tm")
    wide = columns // TILES
    edge_cells = frames * TALL
    edge = (edge_cells * channels // LANES, LANES)
    edges = 2 * (TILES - 1)
    in_hbm = pl.BlockSpec(memory_space=pltpu.HBM)
    return pl.pallas_call(
        chain_kernel,
        out_shape=jax.ShapeDtypeStruct((1, frames, pair, columns, channels), jnp.bfloat16),
        in_specs=[in_hbm] * 3,
        out_specs=in_hbm,
        scratch_shapes=[
            pltpu.VMEM((groups, frames, TALL, wide, channels), jnp.bfloat16),
            pltpu.VMEM((groups, 2, frames, wide, channels), jnp.bfloat16),
            pltpu.VMEM((groups, 2, 4, *edge), jnp.bfloat16),
            pltpu.VMEM(((groups + 1) * frames, TALL + 2, wide, TAPS * channels), jnp.bfloat16),
            pltpu.VMEM((2 * TAPS * edge_cells, channels), jnp.float32),
            pltpu.VMEM(conv_kernels.shape[1:], jnp.bfloat16),
            pltpu.VMEM(norm_gains.shape, jnp.float32),
            pltpu.VMEM((channels // LANES, frames * TALL * wide, LANES), jnp.float32),
            pltpu.VMEM((groups, frames, TALL, wide, channels), jnp.bfloat16),
            pltpu.VMEM((groups, 2, *edge), jnp.bfloat16),
            pltpu.VMEM((frames, pair, columns, channels), jnp.bfloat16),
            pltpu.VMEM((channels // LANES, frames * pair * columns, LANES), jnp.float32),
            pltpu.VMEM((edges, *edge), jnp.bfloat16),
            pltpu.SemaphoreType.DMA((groups, 2)),
            pltpu.SemaphoreType.DMA((groups, 2)),
            pltpu.SemaphoreType.DMA((groups, 2, 4)),
            pltpu.SemaphoreType.DMA((TILES,)),
            pltpu.SemaphoreType.DMA((2 * edges + 2 * TILES,)),
            pltpu.SemaphoreType.DMA((groups, 9)),
            pltpu.SemaphoreType.DMA((groups, 2)),
            pltpu.SemaphoreType.DMA((3,)),
        ],
        compiler_params=pltpu.CompilerParams(
            collective_id=0, has_side_effects=True, vmem_limit_bytes=56 * 2**20
        ),
        name="chain",
    )(clip_features, conv_kernels, norm_gains)


def solution(mesh):
    return jax.shard_map(
        on_device,
        mesh=mesh,
        in_specs=(P("tm", "space", None, None), P("section", None, None, None), P("section", None)),
        out_specs=P("section", "tm", "space", None, None),
        check_vma=False,
    )
```

```python
import jax
import jax.numpy as jnp
from jax import lax
from jax.experimental import pallas as pl
from jax.experimental.pallas import tpu as pltpu
from jax.sharding import PartitionSpec as P

MESH = pl.DeviceIdType.MESH
WORKER = 1
TAPS = 3
TALL = 4
TILES = 4
LANES = 128


def chain_kernel(
    clip, weights, gains, out,
    own_in, row_in, edge_in, hidden, halo, filters, gain, wide_out, tile_out, edge_out,
    clip_in, clip_wide, clip_edge,
    own_sem, row_sem, edge_sem, home_sem, clip_send, next_send, home_send, load_sem,
):
    section = lax.axis_index("section")
    tm = lax.axis_index("tm")
    space = lax.axis_index("space")
    sections = lax.axis_size("section")
    groups = lax.axis_size("tm")
    bands = lax.axis_size("space") // 2
    band = space // 2
    half = space % 2
    tile = 2 * half + tm // 2
    worker = tm % 2 == WORKER
    sender = section == tm % sections
    frames, pair, columns, channels = clip.shape
    wide = columns // TILES
    cells = frames * TALL * wide
    edge_cells = frames * TALL
    beside = band + 2 * half - 1
    has_beside = (beside >= 0) & (beside < bands)

    def worker_device(at_section, at_tile, at_band):
        at_section = jnp.clip(at_section, 0, sections - 1)
        at_tile = jnp.clip(at_tile, 0, TILES - 1)
        at_band = jnp.clip(at_band, 0, bands - 1)
        return (at_section, 2 * (at_tile % 2) + WORKER, 2 * at_band + at_tile // 2)

    def inside(step_tile, step_band):
        there = None
        for at, step, end in ((tile, step_tile, TILES), (band, step_band, bands)):
            if step:
                here = (at > 0) if step < 0 else (at < end - 1)
                there = here if there is None else there & here
        return there

    def when(condition, action):
        if condition is None:
            action()
        else:
            pl.when(condition)(action)

    barrier = pltpu.get_barrier_semaphore()

    def greet(device):
        pl.semaphore_signal(barrier, inc=1, device_id=device, device_id_type=MESH)

    @pl.when(worker & (section == 0))
    def _():
        for group in range(groups):
            for near in range(2):
                greet((group % sections, group, 2 * band + near))

        @pl.when(band > 0)
        def _():
            for group in range(groups):
                greet((group % sections, group, jnp.maximum(2 * band - 1, 0)))

        @pl.when(band < bands - 1)
        def _():
            for group in range(groups):
                greet((group % sections, group, jnp.minimum(2 * band + 2, 2 * bands - 1)))

    load_filters = pltpu.make_async_copy(weights.at[0], filters, load_sem.at[0])
    load_gain = pltpu.make_async_copy(gains, gain, load_sem.at[1])
    load_clip = pltpu.make_async_copy(clip, clip_in, load_sem.at[2])

    @pl.when(sender)
    def _():
        load_clip.start()

    @pl.when(worker)
    def _():
        load_gain.start()
        load_filters.start()

    steps = [(t, b) for t in (-1, 1, 0) for b in (-1, 1, 0)]

    @pl.when(worker & (section > 0))
    def _():
        for t, b in steps:
            when(inside(t, b), lambda t=t, b=b: greet(worker_device(section - 1, tile + t, band + b)))

    for near in range(TILES):
        @pl.when(jnp.logical_not(worker & (tile == near)))
        def _(near=near):
            greet(worker_device(section, near, band))

    @pl.when(worker)
    def _():
        hidden[0:frames] = jnp.zeros((frames, *hidden.shape[1:]), hidden.dtype)

        @pl.when(band == 0)
        def _():
            row_in[:, 0] = jnp.zeros((groups, *row_in.shape[2:]), row_in.dtype)
            edge_in[:, :, 0] = jnp.zeros((groups, 2, *edge_in.shape[3:]), edge_in.dtype)

        @pl.when(band == bands - 1)
        def _():
            row_in[:, 1] = jnp.zeros((groups, *row_in.shape[2:]), row_in.dtype)
            edge_in[:, :, 3] = jnp.zeros((groups, 2, *edge_in.shape[3:]), edge_in.dtype)

        @pl.when(section > 0)
        def _():
            edge_in[:, :, 2] = jnp.zeros((groups, 2, *edge_in.shape[3:]), edge_in.dtype)

        @pl.when(tile == 0)
        def _():
            edge_in[:, 0] = jnp.zeros((groups, *edge_in.shape[2:]), edge_in.dtype)

        @pl.when(tile == TILES - 1)
        def _():
            edge_in[:, 1] = jnp.zeros((groups, *edge_in.shape[2:]), edge_in.dtype)

    left_edges = [(0, at, at * wide - 1) for at in range(1, TILES)]
    right_edges = [(1, at, at * wide + wide) for at in range(TILES - 1)]
    clip_edges = left_edges + right_edges

    @pl.when(sender)
    def _():
        load_clip.wait()
        for n in range(channels // LANES):
            clip_wide[n] = clip_in[:, :, :, n * LANES:(n + 1) * LANES].reshape(-1, LANES).astype(jnp.float32)
        for n, (_, _, column) in enumerate(clip_edges):
            parts = []
            for lane in range(channels // LANES):
                part = clip_wide[lane, pl.ds(column, frames * pair, stride=columns), :]
                parts += [part, part]
            clip_edge[n] = jnp.concatenate(parts, axis=0).astype(jnp.bfloat16)

    def one_if(condition):
        return jnp.where(condition, 1, 0)

    near_tiles = 1 + one_if(tile > 0) + one_if(tile < TILES - 1)
    near_bands = 1 + one_if(band > 0) + one_if(band < bands - 1)
    receivers = (
        one_if(sender) * TILES * (1 + one_if(has_beside))
        + one_if(worker) * (2 * groups - 1 + one_if(section < sections - 1) * near_tiles * near_bands)
    )

    @pl.when(receivers > 0)
    def _():
        pl.semaphore_wait(barrier, receivers)

    def clip_copies():
        copies = []

        def add(condition, source, target, arrived, at_tile, at_band):
            copies.append((condition, pltpu.make_async_remote_copy(
                src_ref=source,
                dst_ref=target,
                send_sem=clip_send.at[len(copies)],
                recv_sem=arrived,
                device_id=worker_device(0, at_tile, at_band),
                device_id_type=MESH,
            )))

        for n, (side, at, _) in enumerate(clip_edges):
            piece = 3 * (1 - half)
            add(has_beside, clip_edge.at[n], edge_in.at[tm, side, piece], edge_sem.at[tm, side, piece], at, beside)
        for at in range(TILES):
            add(has_beside, clip.at[:, half, at * wide:(at + 1) * wide], row_in.at[tm, 1 - half],
                row_sem.at[tm, 1 - half], at, beside)
        for n, (side, at, _) in enumerate(clip_edges):
            piece = 1 + half
            add(None, clip_edge.at[n], edge_in.at[tm, side, piece], edge_sem.at[tm, side, piece], at, band)
        for at in range(TILES):
            add(None, clip.at[:, :, at * wide:(at + 1) * wide], own_in.at[tm, :, pl.ds(pair * half, pair)],
                own_sem.at[tm, half], at, band)
        return copies

    @pl.when(sender)
    def _():
        for condition, copy in clip_copies():
            when(condition, copy.start)

    def next_copies(group):
        copies = []
        for n, (t, b) in enumerate(steps):
            if t:
                side, piece = (1 if t < 0 else 0), {-1: 3, 0: 1, 1: 0}[b]
                source = edge_out.at[group, 1 - side]
                target, arrived = edge_in.at[group, side, piece], edge_sem.at[group, side, piece]
            elif b:
                source = tile_out.at[group, :, 0 if b < 0 else TALL - 1]
                above = 1 if b < 0 else 0
                target, arrived = row_in.at[group, above], row_sem.at[group, above]
            else:
                source, target, arrived = tile_out.at[group], own_in.at[group], own_sem.at[group, 0]
            copies.append((inside(t, b), pltpu.make_async_remote_copy(
                src_ref=source,
                dst_ref=target,
                send_sem=next_send.at[group, n],
                recv_sem=arrived,
                device_id=worker_device(section + 1, tile + t, band + b),
                device_id_type=MESH,
            )))
        return copies

    def home_target():
        return out.at[0, :, :, pl.ds(pl.multiple_of(tile * wide, wide), wide)]

    def home_copy(group, near):
        return pltpu.make_async_remote_copy(
            src_ref=tile_out.at[group, :, near * pair:(near + 1) * pair],
            dst_ref=home_target(),
            send_sem=home_send.at[group, near],
            recv_sem=home_sem.at[tile],
            device_id=(section, group, 2 * band + near),
            device_id_type=MESH,
        )

    def own_copy(group, near):
        source = tile_out.at[group, :, near * pair:(near + 1) * pair]
        return pltpu.make_async_copy(source, home_target(), home_sem.at[tile])

    def arrived(ref, sem):
        pltpu.make_async_copy(ref, ref, sem).wait()

    def activated(value):
        factor = lax.rsqrt(jnp.mean(value * value, axis=-1, keepdims=True) + 1e-06)
        value = value * factor * gain[...]
        return value / (1.0 + jnp.exp(-value))

    def process(group, carry):
        first = group * frames

        for side, t in ((0, -1), (1, 1)):
            for piece, b in ((0, -1), (1, 0), (3, 1)):
                when(inside(t, b), lambda side=side, piece=piece: arrived(
                    edge_in.at[group, side, piece], edge_sem.at[group, side, piece]))

            @pl.when((section == 0) & inside(t, 0))
            def _(side=side):
                arrived(edge_in.at[group, side, 2], edge_sem.at[group, side, 2])

        for above, b in ((0, -1), (1, 1)):
            when(inside(0, b), lambda above=above: arrived(row_in.at[group, above], row_sem.at[group, above]))

        @pl.when(section == 0)
        def _():
            for near in range(2):
                arrived(own_in.at[group, :, near * pair:(near + 1) * pair], own_sem.at[group, near])

        @pl.when(section > 0)
        def _():
            arrived(own_in.at[group], own_sem.at[group, 0])

        lower = lax.broadcasted_iota(jnp.int32, (edge_cells, channels), 0) >= edge_cells // 2
        pieces = []
        for side in range(2):
            above, middle, under, below = (
                jnp.concatenate(
                    [edge_in[group, side, p][n * edge_cells:(n + 1) * edge_cells].astype(jnp.float32)
                     for n in range(channels // LANES)],
                    axis=1,
                )
                for p in range(4)
            )
            pieces += [above, jnp.where(lower & (section == 0), under, middle), below]
        halo[...] = activated(jnp.concatenate(pieces, axis=0))

        own = own_in[group].reshape(cells, channels).astype(jnp.float32)
        middle = activated(own).reshape(frames, TALL, wide, channels)
        outer = activated(row_in[group].reshape(2 * frames * wide, channels).astype(jnp.float32))
        outer = outer.reshape(2, frames, wide, channels)
        column = lax.broadcasted_iota(jnp.int32, (wide, channels), 0)
        for frame in range(frames):
            for row in range(TALL + 2):
                if row == 0:
                    here, at = outer[0, frame], edge_cells // 2 + pair * frame + pair - 1
                elif row == TALL + 1:
                    here, at = outer[1, frame], 2 * edge_cells + pair * frame
                else:
                    part, within = divmod(row - 1, pair)
                    here = middle[frame, row - 1]
                    at = edge_cells + part * (edge_cells // 2) + pair * frame + within
                left = jnp.where(column == 0, halo[pl.ds(at, 1), :], pltpu.roll(here, 1, 0))
                at += TAPS * edge_cells
                right = jnp.where(column == wide - 1, halo[pl.ds(at, 1), :], pltpu.roll(here, wide - 1, 0))
                for part, shifted in enumerate((left, here, right)):
                    hidden[first + frames + frame, row, :, part * channels:(part + 1) * channels] = (
                        shifted.astype(jnp.bfloat16)
                    )

        @pl.when(group == 0)
        def _():
            load_filters.wait()

        summed = jnp.zeros((cells, channels), jnp.float32)
        for time_tap in range(TAPS):
            for row_tap in range(TAPS):
                window = hidden[pl.ds(first + frames - 2 + time_tap, frames), row_tap:row_tap + TALL]
                summed = summed + jnp.dot(
                    window.reshape(cells, TAPS * channels),
                    filters[TAPS * time_tap + row_tap],
                    preferred_element_type=jnp.float32,
                )
        result = own + summed
        tile_out[group] = result.astype(jnp.bfloat16).reshape(frames, TALL, wide, channels)

        @pl.when(section < sections - 1)
        def _():
            block = pair * wide
            for frame in range(frames):
                for part in range(TALL // pair):
                    source = (frame * (TALL // pair) + part) * block
                    for n in range(channels // LANES):
                        wide_out[n, pl.ds((part * frames + frame) * block, block), :] = (
                            result[source:source + block, n * LANES:(n + 1) * LANES]
                        )
            for side, at in enumerate((0, wide - 1)):
                parts = [
                    wide_out[n, pl.ds(at, edge_cells, stride=wide), :]
                    for n in range(channels // LANES)
                ]
                edge_out[group, side] = jnp.concatenate(parts, axis=0).astype(jnp.bfloat16)
            for condition, copy in next_copies(group):
                when(condition, copy.start)

        for near in range(2):
            own_home = (group == tm) & (near == half)

            @pl.when(own_home)
            def _(near=near):
                own_copy(group, near).start()

            @pl.when(jnp.logical_not(own_home))
            def _(near=near):
                home_copy(group, near).start()

        return carry

    @pl.when(worker)
    def _():
        load_gain.wait()
        lax.fori_loop(0, groups, process, 0)

    for at in range(TILES):
        arrived(out.at[0, :, :, at * wide:(at + 1) * wide], home_sem.at[at])

    @pl.when(sender)
    def _():
        for condition, copy in clip_copies():
            when(condition, copy.wait_send)

    def drain(group, carry):
        @pl.when(section < sections - 1)
        def _():
            for condition, copy in next_copies(group):
                when(condition, copy.wait_send)

        for near in range(2):
            @pl.when(jnp.logical_not((group == tm) & (near == half)))
            def _(near=near):
                home_copy(group, near).wait_send()

        return carry

    @pl.when(worker)
    def _():
        lax.fori_loop(0, groups, drain, 0)


def on_device(clip_features, conv_kernels, norm_gains):
    frames, pair, columns, channels = clip_features.shape
    groups = lax.axis_size("tm")
    wide = columns // TILES
    edge_cells = frames * TALL
    edge = (edge_cells * channels // LANES, LANES)
    edges = 2 * (TILES - 1)
    in_hbm = pl.BlockSpec(memory_space=pltpu.HBM)
    blocks = pl.pallas_call(
        chain_kernel,
        out_shape=jax.ShapeDtypeStruct((1, frames, pair, columns, channels), jnp.bfloat16),
        in_specs=[in_hbm] * 3,
        out_specs=in_hbm,
        scratch_shapes=[
            pltpu.VMEM((groups, frames, TALL, wide, channels), jnp.bfloat16),
            pltpu.VMEM((groups, 2, frames, wide, channels), jnp.bfloat16),
            pltpu.VMEM((groups, 2, 4, *edge), jnp.bfloat16),
            pltpu.VMEM(((groups + 1) * frames, TALL + 2, wide, TAPS * channels), jnp.bfloat16),
            pltpu.VMEM((2 * TAPS * edge_cells, channels), jnp.float32),
            pltpu.VMEM(conv_kernels.shape[1:], jnp.bfloat16),
            pltpu.VMEM(norm_gains.shape, jnp.float32),
            pltpu.VMEM((channels // LANES, frames * TALL * wide, LANES), jnp.float32),
            pltpu.VMEM((groups, frames, TALL, wide, channels), jnp.bfloat16),
            pltpu.VMEM((groups, 2, *edge), jnp.bfloat16),
            pltpu.VMEM((frames, pair, columns, channels), jnp.bfloat16),
            pltpu.VMEM((channels // LANES, frames * pair * columns, LANES), jnp.float32),
            pltpu.VMEM((edges, *edge), jnp.bfloat16),
            pltpu.SemaphoreType.DMA((groups, 2)),
            pltpu.SemaphoreType.DMA((groups, 2)),
            pltpu.SemaphoreType.DMA((groups, 2, 4)),
            pltpu.SemaphoreType.DMA((TILES,)),
            pltpu.SemaphoreType.DMA((2 * edges + 2 * TILES,)),
            pltpu.SemaphoreType.DMA((groups, 9)),
            pltpu.SemaphoreType.DMA((groups, 2)),
            pltpu.SemaphoreType.DMA((3,)),
        ],
        compiler_params=pltpu.CompilerParams(
            collective_id=0, has_side_effects=True, vmem_limit_bytes=56 * 2**20
        ),
        name="chain",
    )(clip_features, conv_kernels, norm_gains)
    return jnp.clip(blocks, jnp.finfo(jnp.bfloat16).min, jnp.finfo(jnp.bfloat16).max)


def solution(mesh):
    return jax.shard_map(
        on_device,
        mesh=mesh,
        in_specs=(P("tm", "space", None, None), P("section", None, None, None), P("section", None)),
        out_specs=P("section", "tm", "space", None, None),
        check_vma=False,
    )
```

```python
import jax
import jax.numpy as jnp
from jax import lax
from jax.experimental import pallas as pl
from jax.experimental.pallas import tpu as pltpu
from jax.sharding import PartitionSpec as P

MESH = pl.DeviceIdType.MESH
WORKER = 1
TAPS = 3
TALL = 4
TILES = 4
LANES = 128


def chain_kernel(
    clip, weights, gains, out,
    own_in, row_in, edge_in, hidden, partial, halo, filters, gain, wide_out, tile_out, edge_out,
    clip_in, clip_wide, clip_edge,
    own_sem, row_sem, edge_sem, home_sem, clip_send, next_send, home_send, load_sem,
):
    section = lax.axis_index("section")
    tm = lax.axis_index("tm")
    space = lax.axis_index("space")
    sections = lax.axis_size("section")
    groups = lax.axis_size("tm")
    bands = lax.axis_size("space") // 2
    band = space // 2
    half = space % 2
    tile = 2 * half + tm // 2
    worker = tm % 2 == WORKER
    sender = section == tm % sections
    frames, pair, columns, channels = clip.shape
    wide = columns // TILES
    cells = TALL * wide
    ahead = TAPS - 1
    last_group = groups - 1
    total_units = last_group + frames
    edge_cells = frames * TALL
    beside = band + 2 * half - 1
    has_beside = (beside >= 0) & (beside < bands)

    def worker_device(at_section, at_tile, at_band):
        at_section = jnp.clip(at_section, 0, sections - 1)
        at_tile = jnp.clip(at_tile, 0, TILES - 1)
        at_band = jnp.clip(at_band, 0, bands - 1)
        return (at_section, 2 * (at_tile % 2) + WORKER, 2 * at_band + at_tile // 2)

    def inside(step_tile, step_band):
        there = None
        for at, step, end in ((tile, step_tile, TILES), (band, step_band, bands)):
            if step:
                here = (at > 0) if step < 0 else (at < end - 1)
                there = here if there is None else there & here
        return there

    def when(condition, action):
        if condition is None:
            action()
        else:
            pl.when(condition)(action)

    barrier = pltpu.get_barrier_semaphore()

    def greet(device):
        pl.semaphore_signal(barrier, inc=1, device_id=device, device_id_type=MESH)

    @pl.when(worker & (section == 0))
    def _():
        for group in range(groups):
            for near in range(2):
                greet((group % sections, group, 2 * band + near))

        @pl.when(band > 0)
        def _():
            for group in range(groups):
                greet((group % sections, group, jnp.maximum(2 * band - 1, 0)))

        @pl.when(band < bands - 1)
        def _():
            for group in range(groups):
                greet((group % sections, group, jnp.minimum(2 * band + 2, 2 * bands - 1)))

    load_filters = pltpu.make_async_copy(weights.at[0], filters, load_sem.at[0])
    load_gain = pltpu.make_async_copy(gains, gain, load_sem.at[1])
    load_clip = pltpu.make_async_copy(clip, clip_in, load_sem.at[2])

    @pl.when(sender)
    def _():
        load_clip.start()

    @pl.when(worker)
    def _():
        load_gain.start()
        load_filters.start()

    steps = [(t, b) for t in (-1, 1, 0) for b in (-1, 1, 0)]

    @pl.when(worker & (section > 0))
    def _():
        for t, b in steps:
            when(inside(t, b), lambda t=t, b=b: greet(worker_device(section - 1, tile + t, band + b)))

    for near in range(TILES):
        @pl.when(jnp.logical_not(worker & (tile == near)))
        def _(near=near):
            greet(worker_device(section, near, band))

    @pl.when(worker)
    def _():
        hidden[0:ahead] = jnp.zeros((ahead, *hidden.shape[1:]), hidden.dtype)
        partial[...] = jnp.zeros_like(partial)

        @pl.when(band == 0)
        def _():
            row_in[0] = jnp.zeros(row_in.shape[1:], row_in.dtype)
            edge_in[:, :, 0] = jnp.zeros((total_units, 2, *edge_in.shape[3:]), edge_in.dtype)

        @pl.when(band == bands - 1)
        def _():
            row_in[1] = jnp.zeros(row_in.shape[1:], row_in.dtype)
            edge_in[:, :, 3] = jnp.zeros((total_units, 2, *edge_in.shape[3:]), edge_in.dtype)

        @pl.when(section > 0)
        def _():
            edge_in[:, :, 2] = jnp.zeros((total_units, 2, *edge_in.shape[3:]), edge_in.dtype)

        @pl.when(tile == 0)
        def _():
            edge_in[:, 0] = jnp.zeros((total_units, *edge_in.shape[2:]), edge_in.dtype)

        @pl.when(tile == TILES - 1)
        def _():
            edge_in[:, 1] = jnp.zeros((total_units, *edge_in.shape[2:]), edge_in.dtype)

    left_edges = [(0, at, at * wide - 1) for at in range(1, TILES)]
    right_edges = [(1, at, at * wide + wide) for at in range(TILES - 1)]
    clip_edges = left_edges + right_edges

    @pl.when(sender)
    def _():
        load_clip.wait()
        for n in range(channels // LANES):
            clip_wide[n] = clip_in[:, :, :, n * LANES:(n + 1) * LANES].reshape(-1, LANES).astype(jnp.float32)
        for n, (_, _, column) in enumerate(clip_edges):
            parts = []
            for lane in range(channels // LANES):
                part = clip_wide[lane, pl.ds(column, frames * pair, stride=columns), :]
                parts += [part, part]
            clip_edge[n] = jnp.concatenate(parts, axis=0).astype(jnp.bfloat16)

    def one_if(condition):
        return jnp.where(condition, 1, 0)

    near_tiles = 1 + one_if(tile > 0) + one_if(tile < TILES - 1)
    near_bands = 1 + one_if(band > 0) + one_if(band < bands - 1)
    receivers = (
        one_if(sender) * TILES * (1 + one_if(has_beside))
        + one_if(worker) * (2 * groups - 1 + one_if(section < sections - 1) * near_tiles * near_bands)
    )

    @pl.when(receivers > 0)
    def _():
        pl.semaphore_wait(barrier, receivers)

    def clip_copies():
        copies = []

        def add(condition, source, target, arrived, at_tile, at_band):
            copies.append((condition, pltpu.make_async_remote_copy(
                src_ref=source,
                dst_ref=target,
                send_sem=clip_send.at[len(copies)],
                recv_sem=arrived,
                device_id=worker_device(0, at_tile, at_band),
                device_id_type=MESH,
            )))

        for n, (side, at, _) in enumerate(clip_edges):
            piece = 3 * (1 - half)
            add(has_beside, clip_edge.at[n], edge_in.at[tm, side, piece], edge_sem.at[tm, side, piece], at, beside)
        for at in range(TILES):
            add(has_beside, clip_in.at[:, half, at * wide:(at + 1) * wide],
                row_in.at[1 - half, pl.ds(tm * frames, frames)],
                row_sem.at[tm, 1 - half], at, beside)
        for n, (side, at, _) in enumerate(clip_edges):
            piece = 1 + half
            add(None, clip_edge.at[n], edge_in.at[tm, side, piece], edge_sem.at[tm, side, piece], at, band)
        for at in range(TILES):
            add(None, clip_in.at[:, :, at * wide:(at + 1) * wide],
                own_in.at[pl.ds(tm * frames, frames), pl.ds(pair * half, pair)],
                own_sem.at[tm, half], at, band)
        return copies

    @pl.when(sender)
    def _():
        for condition, copy in clip_copies():
            when(condition, copy.start)

    def next_copies(unit, first, count):
        copies = []
        for n, (t, b) in enumerate(steps):
            if t:
                side, piece = (1 if t < 0 else 0), {-1: 3, 0: 1, 1: 0}[b]
                source = edge_out.at[unit, 1 - side]
                target, arrived = edge_in.at[unit, side, piece], edge_sem.at[unit, side, piece]
            elif b:
                source = tile_out.at[pl.ds(first, count), 0 if b < 0 else TALL - 1]
                above = 1 if b < 0 else 0
                target, arrived = row_in.at[above, pl.ds(first, count)], row_sem.at[unit, above]
            else:
                source, target = tile_out.at[pl.ds(first, count)], own_in.at[pl.ds(first, count)]
                arrived = own_sem.at[unit, 0]
            copies.append((inside(t, b), pltpu.make_async_remote_copy(
                src_ref=source,
                dst_ref=target,
                send_sem=next_send.at[unit, n],
                recv_sem=arrived,
                device_id=worker_device(section + 1, tile + t, band + b),
                device_id_type=MESH,
            )))
        return copies

    def home_copy(unit, first, count, slot, near, remote):
        source = tile_out.at[pl.ds(first, count), near * pair:(near + 1) * pair]
        target = out.at[0, slot:slot + count, :, pl.ds(pl.multiple_of(tile * wide, wide), wide)]
        if not remote:
            return pltpu.make_async_copy(source, target, home_sem.at[tile, slot])
        return pltpu.make_async_remote_copy(
            src_ref=source,
            dst_ref=target,
            send_sem=home_send.at[unit, near],
            recv_sem=home_sem.at[tile, slot],
            device_id=(section, jnp.minimum(unit, last_group), 2 * band + near),
            device_id_type=MESH,
        )

    def stays(unit, near):
        return (jnp.minimum(unit, last_group) == tm) & (near == half)

    def arrived(ref, sem):
        pltpu.make_async_copy(ref, ref, sem).wait()

    def activated(value):
        factor = lax.rsqrt(jnp.mean(value * value, axis=-1, keepdims=True) + 1e-06)
        value = value * factor * gain[...]
        return value / (1.0 + jnp.exp(-value))

    def taps(first, count, time_tap):
        summed = jnp.zeros((count * cells, channels), jnp.float32)
        for row_tap in range(TAPS):
            window = hidden[pl.ds(first + ahead, count), row_tap:row_tap + TALL]
            summed = summed + jnp.dot(
                window.reshape(count * cells, TAPS * channels),
                filters[TAPS * time_tap + row_tap],
                preferred_element_type=jnp.float32,
            )
        return summed

    def receive(unit, first, count):
        for side, t in ((0, -1), (1, 1)):
            for piece, b in ((0, -1), (1, 0), (3, 1)):
                when(inside(t, b), lambda side=side, piece=piece: arrived(
                    edge_in.at[unit, side, piece], edge_sem.at[unit, side, piece]))
        for above, b in ((0, -1), (1, 1)):
            when(inside(0, b), lambda above=above: arrived(
                row_in.at[above, pl.ds(first, count)], row_sem.at[unit, above]))

    def receive_clip(unit, first):
        for side, t in ((0, -1), (1, 1)):
            @pl.when(inside(t, 0))
            def _(side=side):
                arrived(edge_in.at[unit, side, 2], edge_sem.at[unit, side, 2])
        for near in range(2):
            arrived(own_in.at[pl.ds(first, frames), near * pair:(near + 1) * pair], own_sem.at[unit, near])

    def process(unit, first, count, slot):
        @pl.when(section > 0)
        def _():
            receive(unit, first, count)
            arrived(own_in.at[pl.ds(first, count)], own_sem.at[unit, 0])

        if slot == 0:
            @pl.when(section == 0)
            def _():
                receive(unit, first, frames)
                receive_clip(unit, first)

        at_edge = unit if slot == 0 else jnp.where(section == 0, unit - slot, unit)

        lower = lax.broadcasted_iota(jnp.int32, (edge_cells, channels), 0) >= edge_cells // 2
        pieces = []
        for side in range(2):
            above, middle, under, below = (
                jnp.concatenate(
                    [edge_in[at_edge, side, p][n * edge_cells:(n + 1) * edge_cells].astype(jnp.float32)
                     for n in range(channels // LANES)],
                    axis=1,
                )
                for p in range(4)
            )
            pieces += [above, jnp.where(lower & (section == 0), under, middle), below]
        halo[...] = activated(jnp.concatenate(pieces, axis=0))

        own = own_in[pl.ds(first, count)].reshape(count * cells, channels).astype(jnp.float32)
        middle = activated(own).reshape(count, TALL, wide, channels)
        outer = row_in[:, pl.ds(first, count)].reshape(2 * count * wide, channels).astype(jnp.float32)
        outer = activated(outer).reshape(2, count, wide, channels)
        column = lax.broadcasted_iota(jnp.int32, (wide, channels), 0)
        for n in range(count):
            frame = slot + n
            for row in range(TALL + 2):
                if row == 0:
                    here, at = outer[0, n], edge_cells // 2 + pair * frame + pair - 1
                elif row == TALL + 1:
                    here, at = outer[1, n], 2 * edge_cells + pair * frame
                else:
                    part, within = divmod(row - 1, pair)
                    here = middle[n, row - 1]
                    at = edge_cells + part * (edge_cells // 2) + pair * frame + within
                left = jnp.where(column == 0, halo[pl.ds(at, 1), :], pltpu.roll(here, 1, 0))
                at += TAPS * edge_cells
                right = jnp.where(column == wide - 1, halo[pl.ds(at, 1), :], pltpu.roll(here, wide - 1, 0))
                for part, shifted in enumerate((left, here, right)):
                    hidden[first + ahead + n, row, :, part * channels:(part + 1) * channels] = (
                        shifted.astype(jnp.bfloat16)
                    )

        if count > 1:
            @pl.when(unit == 0)
            def _():
                load_filters.wait()

        summed = partial[slot * cells:(slot + count) * cells]
        for time_tap in range(1 if count > 1 else ahead, TAPS):
            summed = summed + taps(first + time_tap - ahead, count, time_tap)
        result = own + summed
        tile_out[pl.ds(first, count)] = result.astype(jnp.bfloat16).reshape(count, TALL, wide, channels)

        @pl.when(section < sections - 1)
        def _():
            block = pair * wide
            for n in range(count):
                for part in range(TALL // pair):
                    source = (n * (TALL // pair) + part) * block
                    for lane in range(channels // LANES):
                        wide_out[lane, pl.ds((part * frames + slot + n) * block, block), :] = (
                            result[source:source + block, lane * LANES:(lane + 1) * LANES]
                        )
            for side, at in enumerate((0, wide - 1)):
                parts = [
                    wide_out[lane, pl.ds(at, edge_cells, stride=wide), :]
                    for lane in range(channels // LANES)
                ]
                edge_out[unit, side] = jnp.concatenate(parts, axis=0).astype(jnp.bfloat16)
            for condition, copy in next_copies(unit, first, count):
                when(condition, copy.start)

        for near in range(2):
            @pl.when(stays(unit, near))
            def _(near=near):
                home_copy(unit, first, count, slot, near, False).start()

            @pl.when(jnp.logical_not(stays(unit, near)))
            def _(near=near):
                home_copy(unit, first, count, slot, near, True).start()

    def process_group(unit, carry):
        process(unit, unit * frames, frames, 0)
        partial[...] = taps(unit * frames, frames, 0)
        return carry

    @pl.when(worker)
    def _():
        load_gain.wait()
        lax.fori_loop(0, last_group, process_group, 0)
        for slot in range(frames):
            frame = last_group * frames + slot
            for time_tap in range(1, ahead):
                partial[slot * cells:(slot + 1) * cells] += taps(frame + time_tap - ahead, 1, time_tap)
            process(last_group + slot, frame, 1, slot)

    @pl.when(tm < last_group)
    def _():
        for at in range(TILES):
            arrived(out.at[0, :, :, at * wide:(at + 1) * wide], home_sem.at[at, 0])

    @pl.when(tm == last_group)
    def _():
        for slot in range(frames):
            for at in range(TILES):
                arrived(out.at[0, slot:slot + 1, :, at * wide:(at + 1) * wide], home_sem.at[at, slot])

    @pl.when(sender)
    def _():
        for condition, copy in clip_copies():
            when(condition, copy.wait_send)

    def drain(unit, first, count, slot):
        @pl.when(section < sections - 1)
        def _():
            for condition, copy in next_copies(unit, first, count):
                when(condition, copy.wait_send)

        for near in range(2):
            @pl.when(jnp.logical_not(stays(unit, near)))
            def _(near=near):
                home_copy(unit, first, count, slot, near, True).wait_send()

    def drain_group(unit, carry):
        drain(unit, unit * frames, frames, 0)
        return carry

    @pl.when(worker)
    def _():
        lax.fori_loop(0, last_group, drain_group, 0)
        for slot in range(frames):
            drain(last_group + slot, last_group * frames + slot, 1, slot)


def on_device(clip_features, conv_kernels, norm_gains):
    frames, pair, columns, channels = clip_features.shape
    groups = lax.axis_size("tm")
    total = groups * frames
    units = groups - 1 + frames
    wide = columns // TILES
    edge_cells = frames * TALL
    edge = (edge_cells * channels // LANES, LANES)
    edges = 2 * (TILES - 1)
    in_hbm = pl.BlockSpec(memory_space=pltpu.HBM)
    return pl.pallas_call(
        chain_kernel,
        out_shape=jax.ShapeDtypeStruct((1, frames, pair, columns, channels), jnp.bfloat16),
        in_specs=[in_hbm] * 3,
        out_specs=in_hbm,
        scratch_shapes=[
            pltpu.VMEM((total, TALL, wide, channels), jnp.bfloat16),
            pltpu.VMEM((2, total, wide, channels), jnp.bfloat16),
            pltpu.VMEM((units, 2, 4, *edge), jnp.bfloat16),
            pltpu.VMEM((TAPS - 1 + total, TALL + 2, wide, TAPS * channels), jnp.bfloat16),
            pltpu.VMEM((frames * TALL * wide, channels), jnp.float32),
            pltpu.VMEM((2 * TAPS * edge_cells, channels), jnp.float32),
            pltpu.VMEM(conv_kernels.shape[1:], jnp.bfloat16),
            pltpu.VMEM(norm_gains.shape, jnp.float32),
            pltpu.VMEM((channels // LANES, frames * TALL * wide, LANES), jnp.float32),
            pltpu.VMEM((total, TALL, wide, channels), jnp.bfloat16),
            pltpu.VMEM((units, 2, *edge), jnp.bfloat16),
            pltpu.VMEM((frames, pair, columns, channels), jnp.bfloat16),
            pltpu.VMEM((channels // LANES, frames * pair * columns, LANES), jnp.float32),
            pltpu.VMEM((edges, *edge), jnp.bfloat16),
            pltpu.SemaphoreType.DMA((units, 2)),
            pltpu.SemaphoreType.DMA((units, 2)),
            pltpu.SemaphoreType.DMA((units, 2, 4)),
            pltpu.SemaphoreType.DMA((TILES, frames)),
            pltpu.SemaphoreType.DMA((2 * edges + 2 * TILES,)),
            pltpu.SemaphoreType.DMA((units, 9)),
            pltpu.SemaphoreType.DMA((units, 2)),
            pltpu.SemaphoreType.DMA((3,)),
        ],
        compiler_params=pltpu.CompilerParams(
            collective_id=0, has_side_effects=True, vmem_limit_bytes=56 * 2**20
        ),
        name="chain",
    )(clip_features, conv_kernels, norm_gains)


def solution(mesh):
    return jax.shard_map(
        on_device,
        mesh=mesh,
        in_specs=(P("tm", "space", None, None), P("section", None, None, None), P("section", None)),
        out_specs=P("section", "tm", "space", None, None),
        check_vma=False,
    )
```

```python
import jax
import jax.numpy as jnp
from jax import lax
from jax.experimental import pallas as pl
from jax.experimental.pallas import tpu as pltpu
from jax.sharding import PartitionSpec as P

MESH = pl.DeviceIdType.MESH
WORKER = 1
TAPS = 3
TALL = 4
TILES = 4
LANES = 128


def chain_kernel(
    clip, weights, gains, out,
    own_in, row_in, edge_in, hidden, halo, filters, gain, wide_out, tile_out, edge_out,
    clip_in, clip_wide, clip_edge,
    own_sem, row_sem, edge_sem, home_sem, clip_send, next_send, home_send, load_sem,
):
    section = lax.axis_index("section")
    tm = lax.axis_index("tm")
    space = lax.axis_index("space")
    sections = lax.axis_size("section")
    groups = lax.axis_size("tm")
    bands = lax.axis_size("space") // 2
    band = space // 2
    half = space % 2
    tile = 2 * half + tm // 2
    worker = tm % 2 == WORKER
    sender = section == jnp.where(tm == 0, sections - 1, tm % sections)
    sources = [(sections - 1 if group == 0 else group % sections, group) for group in range(groups)]
    frames, pair, columns, channels = clip.shape
    wide = columns // TILES
    cells = frames * TALL * wide
    edge_cells = frames * TALL
    beside = band + 2 * half - 1
    has_beside = (beside >= 0) & (beside < bands)

    def worker_device(at_section, at_tile, at_band):
        at_section = jnp.clip(at_section, 0, sections - 1)
        at_tile = jnp.clip(at_tile, 0, TILES - 1)
        at_band = jnp.clip(at_band, 0, bands - 1)
        return (at_section, 2 * (at_tile % 2) + WORKER, 2 * at_band + at_tile // 2)

    def inside(step_tile, step_band):
        there = None
        for at, step, end in ((tile, step_tile, TILES), (band, step_band, bands)):
            if step:
                here = (at > 0) if step < 0 else (at < end - 1)
                there = here if there is None else there & here
        return there

    def when(condition, action):
        if condition is None:
            action()
        else:
            pl.when(condition)(action)

    barrier = pltpu.get_barrier_semaphore()

    def greet(device):
        pl.semaphore_signal(barrier, inc=1, device_id=device, device_id_type=MESH)

    @pl.when(worker & (section == 0))
    def _():
        for source, group in sources:
            for near in range(2):
                greet((source, group, 2 * band + near))

        @pl.when(band > 0)
        def _():
            for source, group in sources:
                greet((source, group, jnp.maximum(2 * band - 1, 0)))

        @pl.when(band < bands - 1)
        def _():
            for source, group in sources:
                greet((source, group, jnp.minimum(2 * band + 2, 2 * bands - 1)))

    load_filters = pltpu.make_async_copy(weights.at[0], filters, load_sem.at[0])
    load_gain = pltpu.make_async_copy(gains, gain, load_sem.at[1])
    load_clip = pltpu.make_async_copy(clip, clip_in, load_sem.at[2])

    @pl.when(sender)
    def _():
        load_clip.start()

    @pl.when(worker)
    def _():
        load_gain.start()
        load_filters.start()

    steps = [(t, b) for t in (-1, 1, 0) for b in (-1, 1, 0)]

    @pl.when(worker & (section > 0))
    def _():
        for t, b in steps:
            when(inside(t, b), lambda t=t, b=b: greet(worker_device(section - 1, tile + t, band + b)))

    for near in range(TILES):
        @pl.when(jnp.logical_not(worker & (tile == near)))
        def _(near=near):
            greet(worker_device(section, near, band))

    @pl.when(worker)
    def _():
        hidden[0:frames] = jnp.zeros((frames, *hidden.shape[1:]), hidden.dtype)

        @pl.when(band == 0)
        def _():
            row_in[:, 0] = jnp.zeros((groups, *row_in.shape[2:]), row_in.dtype)
            edge_in[:, :, 0] = jnp.zeros((groups, 2, *edge_in.shape[3:]), edge_in.dtype)

        @pl.when(band == bands - 1)
        def _():
            row_in[:, 1] = jnp.zeros((groups, *row_in.shape[2:]), row_in.dtype)
            edge_in[:, :, 3] = jnp.zeros((groups, 2, *edge_in.shape[3:]), edge_in.dtype)

        @pl.when(section > 0)
        def _():
            edge_in[:, :, 2] = jnp.zeros((groups, 2, *edge_in.shape[3:]), edge_in.dtype)

        @pl.when(tile == 0)
        def _():
            edge_in[:, 0] = jnp.zeros((groups, *edge_in.shape[2:]), edge_in.dtype)

        @pl.when(tile == TILES - 1)
        def _():
            edge_in[:, 1] = jnp.zeros((groups, *edge_in.shape[2:]), edge_in.dtype)

    left_edges = [(0, at, at * wide - 1) for at in range(1, TILES)]
    right_edges = [(1, at, at * wide + wide) for at in range(TILES - 1)]
    clip_edges = left_edges + right_edges

    @pl.when(sender)
    def _():
        load_clip.wait()
        for n in range(channels // LANES):
            clip_wide[n] = clip_in[:, :, :, n * LANES:(n + 1) * LANES].reshape(-1, LANES).astype(jnp.float32)
        for n, (_, _, column) in enumerate(clip_edges):
            parts = []
            for lane in range(channels // LANES):
                part = clip_wide[lane, pl.ds(column, frames * pair, stride=columns), :]
                parts += [part, part]
            clip_edge[n] = jnp.concatenate(parts, axis=0).astype(jnp.bfloat16)

    def one_if(condition):
        return jnp.where(condition, 1, 0)

    near_tiles = 1 + one_if(tile > 0) + one_if(tile < TILES - 1)
    near_bands = 1 + one_if(band > 0) + one_if(band < bands - 1)
    receivers = (
        one_if(sender) * TILES * (1 + one_if(has_beside))
        + one_if(worker) * (2 * groups - 1 + one_if(section < sections - 1) * near_tiles * near_bands)
    )

    @pl.when(receivers > 0)
    def _():
        pl.semaphore_wait(barrier, receivers)

    def clip_copies():
        copies = []

        def add(condition, source, target, arrived, at_tile, at_band):
            copies.append((condition, pltpu.make_async_remote_copy(
                src_ref=source,
                dst_ref=target,
                send_sem=clip_send.at[len(copies)],
                recv_sem=arrived,
                device_id=worker_device(0, at_tile, at_band),
                device_id_type=MESH,
            )))

        for n, (side, at, _) in enumerate(clip_edges):
            piece = 3 * (1 - half)
            add(has_beside, clip_edge.at[n], edge_in.at[tm, side, piece], edge_sem.at[tm, side, piece], at, beside)
        for at in range(TILES):
            add(has_beside, clip_in.at[:, half, at * wide:(at + 1) * wide], row_in.at[tm, 1 - half],
                row_sem.at[tm, 1 - half], at, beside)
        for n, (side, at, _) in enumerate(clip_edges):
            piece = 1 + half
            add(None, clip_edge.at[n], edge_in.at[tm, side, piece], edge_sem.at[tm, side, piece], at, band)
        for at in range(TILES):
            add(None, clip_in.at[:, :, at * wide:(at + 1) * wide], own_in.at[tm, :, pl.ds(pair * half, pair)],
                own_sem.at[tm, half], at, band)
        return copies

    @pl.when(sender)
    def _():
        for condition, copy in clip_copies():
            when(condition, copy.start)

    def next_copies(group):
        copies = []
        for n, (t, b) in enumerate(steps):
            if t:
                side, piece = (1 if t < 0 else 0), {-1: 3, 0: 1, 1: 0}[b]
                source = edge_out.at[group, 1 - side]
                target, arrived = edge_in.at[group, side, piece], edge_sem.at[group, side, piece]
            elif b:
                source = tile_out.at[group, :, 0 if b < 0 else TALL - 1]
                above = 1 if b < 0 else 0
                target, arrived = row_in.at[group, above], row_sem.at[group, above]
            else:
                source, target, arrived = tile_out.at[group], own_in.at[group], own_sem.at[group, 0]
            copies.append((inside(t, b), pltpu.make_async_remote_copy(
                src_ref=source,
                dst_ref=target,
                send_sem=next_send.at[group, n],
                recv_sem=arrived,
                device_id=worker_device(section + 1, tile + t, band + b),
                device_id_type=MESH,
            )))
        return copies

    def home_target():
        return out.at[0, :, :, pl.ds(pl.multiple_of(tile * wide, wide), wide)]

    def home_copy(group, near):
        return pltpu.make_async_remote_copy(
            src_ref=tile_out.at[group, :, near * pair:(near + 1) * pair],
            dst_ref=home_target(),
            send_sem=home_send.at[group, near],
            recv_sem=home_sem.at[tile],
            device_id=(section, group, 2 * band + near),
            device_id_type=MESH,
        )

    def own_copy(group, near):
        source = tile_out.at[group, :, near * pair:(near + 1) * pair]
        return pltpu.make_async_copy(source, home_target(), home_sem.at[tile])

    def arrived(ref, sem):
        pltpu.make_async_copy(ref, ref, sem).wait()

    def activated(value):
        factor = lax.rsqrt(jnp.mean(value * value, axis=-1, keepdims=True) + 1e-06)
        value = value * factor * gain[...]
        return value / (1.0 + jnp.exp(-value))

    def process(group, carry):
        first = group * frames

        for side, t in ((0, -1), (1, 1)):
            for piece, b in ((0, -1), (1, 0), (3, 1)):
                when(inside(t, b), lambda side=side, piece=piece: arrived(
                    edge_in.at[group, side, piece], edge_sem.at[group, side, piece]))

            @pl.when((section == 0) & inside(t, 0))
            def _(side=side):
                arrived(edge_in.at[group, side, 2], edge_sem.at[group, side, 2])

        for above, b in ((0, -1), (1, 1)):
            when(inside(0, b), lambda above=above: arrived(row_in.at[group, above], row_sem.at[group, above]))

        @pl.when(section == 0)
        def _():
            for near in range(2):
                arrived(own_in.at[group, :, near * pair:(near + 1) * pair], own_sem.at[group, near])

        @pl.when(section > 0)
        def _():
            arrived(own_in.at[group], own_sem.at[group, 0])

        lower = lax.broadcasted_iota(jnp.int32, (edge_cells, channels), 0) >= edge_cells // 2
        pieces = []
        for side in range(2):
            above, middle, under, below = (
                jnp.concatenate(
                    [edge_in[group, side, p][n * edge_cells:(n + 1) * edge_cells].astype(jnp.float32)
                     for n in range(channels // LANES)],
                    axis=1,
                )
                for p in range(4)
            )
            pieces += [above, jnp.where(lower & (section == 0), under, middle), below]
        halo[...] = activated(jnp.concatenate(pieces, axis=0))

        own = own_in[group].reshape(cells, channels).astype(jnp.float32)
        middle = activated(own).reshape(frames, TALL, wide, channels)
        outer = activated(row_in[group].reshape(2 * frames * wide, channels).astype(jnp.float32))
        outer = outer.reshape(2, frames, wide, channels)
        column = lax.broadcasted_iota(jnp.int32, (wide, channels), 0)
        for frame in range(frames):
            for row in range(TALL + 2):
                if row == 0:
                    here, at = outer[0, frame], edge_cells // 2 + pair * frame + pair - 1
                elif row == TALL + 1:
                    here, at = outer[1, frame], 2 * edge_cells + pair * frame
                else:
                    part, within = divmod(row - 1, pair)
                    here = middle[frame, row - 1]
                    at = edge_cells + part * (edge_cells // 2) + pair * frame + within
                left = jnp.where(column == 0, halo[pl.ds(at, 1), :], pltpu.roll(here, 1, 0))
                at += TAPS * edge_cells
                right = jnp.where(column == wide - 1, halo[pl.ds(at, 1), :], pltpu.roll(here, wide - 1, 0))
                for part, shifted in enumerate((left, here, right)):
                    hidden[first + frames + frame, row, :, part * channels:(part + 1) * channels] = (
                        shifted.astype(jnp.bfloat16)
                    )

        @pl.when(group == 0)
        def _():
            load_filters.wait()

        summed = jnp.zeros((cells, channels), jnp.float32)
        for time_tap in range(TAPS):
            for row_tap in range(TAPS):
                window = hidden[pl.ds(first + frames - 2 + time_tap, frames), row_tap:row_tap + TALL]
                summed = summed + jnp.dot(
                    window.reshape(cells, TAPS * channels),
                    filters[TAPS * time_tap + row_tap],
                    preferred_element_type=jnp.float32,
                )
        result = own + summed
        tile_out[group] = result.astype(jnp.bfloat16).reshape(frames, TALL, wide, channels)

        @pl.when(section < sections - 1)
        def _():
            block = pair * wide
            for frame in range(frames):
                for part in range(TALL // pair):
                    source = (frame * (TALL // pair) + part) * block
                    for n in range(channels // LANES):
                        wide_out[n, pl.ds((part * frames + frame) * block, block), :] = (
                            result[source:source + block, n * LANES:(n + 1) * LANES]
                        )
            for side, at in enumerate((0, wide - 1)):
                parts = [
                    wide_out[n, pl.ds(at, edge_cells, stride=wide), :]
                    for n in range(channels // LANES)
                ]
                edge_out[group, side] = jnp.concatenate(parts, axis=0).astype(jnp.bfloat16)
            for condition, copy in next_copies(group):
                when(condition, copy.start)

        for near in range(2):
            own_home = (group == tm) & (near == half)

            @pl.when(own_home)
            def _(near=near):
                own_copy(group, near).start()

            @pl.when(jnp.logical_not(own_home))
            def _(near=near):
                home_copy(group, near).start()

        return carry

    @pl.when(worker)
    def _():
        load_gain.wait()
        lax.fori_loop(0, groups, process, 0)

    for at in range(TILES):
        arrived(out.at[0, :, :, at * wide:(at + 1) * wide], home_sem.at[at])

    @pl.when(sender)
    def _():
        for condition, copy in clip_copies():
            when(condition, copy.wait_send)

    def drain(group, carry):
        @pl.when(section < sections - 1)
        def _():
            for condition, copy in next_copies(group):
                when(condition, copy.wait_send)

        for near in range(2):
            @pl.when(jnp.logical_not((group == tm) & (near == half)))
            def _(near=near):
                home_copy(group, near).wait_send()

        return carry

    @pl.when(worker)
    def _():
        lax.fori_loop(0, groups, drain, 0)


def on_device(clip_features, conv_kernels, norm_gains):
    frames, pair, columns, channels = clip_features.shape
    groups = lax.axis_size("tm")
    wide = columns // TILES
    edge_cells = frames * TALL
    edge = (edge_cells * channels // LANES, LANES)
    edges = 2 * (TILES - 1)
    in_hbm = pl.BlockSpec(memory_space=pltpu.HBM)
    return pl.pallas_call(
        chain_kernel,
        out_shape=jax.ShapeDtypeStruct((1, frames, pair, columns, channels), jnp.bfloat16),
        in_specs=[in_hbm] * 3,
        out_specs=in_hbm,
        scratch_shapes=[
            pltpu.VMEM((groups, frames, TALL, wide, channels), jnp.bfloat16),
            pltpu.VMEM((groups, 2, frames, wide, channels), jnp.bfloat16),
            pltpu.VMEM((groups, 2, 4, *edge), jnp.bfloat16),
            pltpu.VMEM(((groups + 1) * frames, TALL + 2, wide, TAPS * channels), jnp.bfloat16),
            pltpu.VMEM((2 * TAPS * edge_cells, channels), jnp.float32),
            pltpu.VMEM(conv_kernels.shape[1:], jnp.bfloat16),
            pltpu.VMEM(norm_gains.shape, jnp.float32),
            pltpu.VMEM((channels // LANES, frames * TALL * wide, LANES), jnp.float32),
            pltpu.VMEM((groups, frames, TALL, wide, channels), jnp.bfloat16),
            pltpu.VMEM((groups, 2, *edge), jnp.bfloat16),
            pltpu.VMEM((frames, pair, columns, channels), jnp.bfloat16),
            pltpu.VMEM((channels // LANES, frames * pair * columns, LANES), jnp.float32),
            pltpu.VMEM((edges, *edge), jnp.bfloat16),
            pltpu.SemaphoreType.DMA((groups, 2)),
            pltpu.SemaphoreType.DMA((groups, 2)),
            pltpu.SemaphoreType.DMA((groups, 2, 4)),
            pltpu.SemaphoreType.DMA((TILES,)),
            pltpu.SemaphoreType.DMA((2 * edges + 2 * TILES,)),
            pltpu.SemaphoreType.DMA((groups, 9)),
            pltpu.SemaphoreType.DMA((groups, 2)),
            pltpu.SemaphoreType.DMA((3,)),
        ],
        compiler_params=pltpu.CompilerParams(
            collective_id=0, has_side_effects=True, vmem_limit_bytes=56 * 2**20
        ),
        name="chain",
    )(clip_features, conv_kernels, norm_gains)


def solution(mesh):
    return jax.shard_map(
        on_device,
        mesh=mesh,
        in_specs=(P("tm", "space", None, None), P("section", None, None, None), P("section", None)),
        out_specs=P("section", "tm", "space", None, None),
        check_vma=False,
    )
```

```python
import jax
import jax.numpy as jnp
from jax import lax
from jax.experimental import pallas as pl
from jax.experimental.pallas import tpu as pltpu
from jax.sharding import PartitionSpec as P

MESH = pl.DeviceIdType.MESH
WORKER = 1
TAPS = 3
TALL = 4
TILES = 4
LANES = 128


def chain_kernel(
    clip, weights, gains, out,
    own_in, row_in, edge_in, corner_in, hidden, partial, raw, halo, filters, gain, wide_out, tile_out, edge_out,
    corner_out, clip_in, clip_wide, clip_edge, clip_corner,
    own_sem, row_sem, edge_sem, corner_sem, home_sem, clip_send, next_send, home_send, load_sem,
):
    section = lax.axis_index("section")
    tm = lax.axis_index("tm")
    space = lax.axis_index("space")
    sections = lax.axis_size("section")
    groups = lax.axis_size("tm")
    bands = lax.axis_size("space") // 2
    band = space // 2
    half = space % 2
    tile = 2 * half + tm // 2
    worker = tm % 2 == WORKER
    sender = section == tm % sections
    frames, pair, columns, channels = clip.shape
    wide = columns // TILES
    cells = frames * TALL * wide
    edge_cells = frames * TALL
    ahead = TAPS - 1
    beside = band + 2 * half - 1
    has_beside = (beside >= 0) & (beside < bands)

    def worker_device(at_section, at_tile, at_band):
        at_section = jnp.clip(at_section, 0, sections - 1)
        at_tile = jnp.clip(at_tile, 0, TILES - 1)
        at_band = jnp.clip(at_band, 0, bands - 1)
        return (at_section, 2 * (at_tile % 2) + WORKER, 2 * at_band + at_tile // 2)

    def inside(step_tile, step_band):
        there = None
        for at, step, end in ((tile, step_tile, TILES), (band, step_band, bands)):
            if step:
                here = (at > 0) if step < 0 else (at < end - 1)
                there = here if there is None else there & here
        return there

    def when(condition, action):
        if condition is None:
            action()
        else:
            pl.when(condition)(action)

    barrier = pltpu.get_barrier_semaphore()

    def greet(device):
        pl.semaphore_signal(barrier, inc=1, device_id=device, device_id_type=MESH)

    @pl.when(worker & (section == 0))
    def _():
        for group in range(groups):
            for near in range(2):
                greet((group % sections, group, 2 * band + near))

        @pl.when(band > 0)
        def _():
            for group in range(groups):
                greet((group % sections, group, jnp.maximum(2 * band - 1, 0)))

        @pl.when(band < bands - 1)
        def _():
            for group in range(groups):
                greet((group % sections, group, jnp.minimum(2 * band + 2, 2 * bands - 1)))

    load_filters = pltpu.make_async_copy(weights.at[0], filters, load_sem.at[0])
    load_gain = pltpu.make_async_copy(gains, gain, load_sem.at[1])
    load_clip = pltpu.make_async_copy(clip, clip_in, load_sem.at[2])

    @pl.when(sender)
    def _():
        load_clip.start()

    @pl.when(worker)
    def _():
        load_gain.start()
        load_filters.start()

    steps = [(t, b) for t in (-1, 1, 0) for b in (-1, 1, 0)]

    @pl.when(worker & (section > 0))
    def _():
        for t, b in steps:
            when(inside(t, b), lambda t=t, b=b: greet(worker_device(section - 1, tile + t, band + b)))

    for near in range(TILES):
        @pl.when(jnp.logical_not(worker & (tile == near)))
        def _(near=near):
            greet(worker_device(section, near, band))

    @pl.when(worker)
    def _():
        hidden[0:ahead] = jnp.zeros((ahead, *hidden.shape[1:]), hidden.dtype)
        partial[...] = jnp.zeros_like(partial)

        @pl.when(band == 0)
        def _():
            row_in[:, 0] = jnp.zeros((groups, *row_in.shape[2:]), row_in.dtype)
            corner_in[:, :, 0] = jnp.zeros((groups, 2, *corner_in.shape[3:]), corner_in.dtype)

        @pl.when(band == bands - 1)
        def _():
            row_in[:, 1] = jnp.zeros((groups, *row_in.shape[2:]), row_in.dtype)
            corner_in[:, :, 1] = jnp.zeros((groups, 2, *corner_in.shape[3:]), corner_in.dtype)

        @pl.when(section > 0)
        def _():
            edge_in[:, :, 1] = jnp.zeros((groups, 2, *edge_in.shape[3:]), edge_in.dtype)

        @pl.when(tile == 0)
        def _():
            edge_in[:, 0] = jnp.zeros((groups, *edge_in.shape[2:]), edge_in.dtype)
            corner_in[:, 0] = jnp.zeros((groups, *corner_in.shape[2:]), corner_in.dtype)

        @pl.when(tile == TILES - 1)
        def _():
            edge_in[:, 1] = jnp.zeros((groups, *edge_in.shape[2:]), edge_in.dtype)
            corner_in[:, 1] = jnp.zeros((groups, *corner_in.shape[2:]), corner_in.dtype)

    left_edges = [(0, at, at * wide - 1) for at in range(1, TILES)]
    right_edges = [(1, at, at * wide + wide) for at in range(TILES - 1)]
    clip_edges = left_edges + right_edges

    @pl.when(sender)
    def _():
        load_clip.wait()
        for n in range(channels // LANES):
            clip_wide[n] = clip_in[:, :, :, n * LANES:(n + 1) * LANES].reshape(-1, LANES).astype(jnp.float32)
        for n, (_, _, column) in enumerate(clip_edges):
            parts = []
            for lane in range(channels // LANES):
                part = clip_wide[lane, pl.ds(column, frames * pair, stride=columns), :]
                parts += [part, part]
            clip_edge[n] = jnp.concatenate(parts, axis=0).astype(jnp.bfloat16)
            for lane in range(channels // LANES):
                for row in range(pair):
                    @pl.when(half == row)
                    def _(n=n, column=column, lane=lane, row=row):
                        clip_corner[n, lane * frames:(lane + 1) * frames] = (
                            clip_wide[lane, pl.ds(row * columns + column, frames, stride=pair * columns), :]
                        )

    def one_if(condition):
        return jnp.where(condition, 1, 0)

    near_tiles = 1 + one_if(tile > 0) + one_if(tile < TILES - 1)
    near_bands = 1 + one_if(band > 0) + one_if(band < bands - 1)
    receivers = (
        one_if(sender) * TILES * (1 + one_if(has_beside))
        + one_if(worker) * (2 * groups - 1 + one_if(section < sections - 1) * near_tiles * near_bands)
    )

    @pl.when(receivers > 0)
    def _():
        pl.semaphore_wait(barrier, receivers)

    def clip_copies():
        copies = []

        def add(condition, source, target, arrived, at_tile, at_band):
            copies.append((condition, pltpu.make_async_remote_copy(
                src_ref=source,
                dst_ref=target,
                send_sem=clip_send.at[len(copies)],
                recv_sem=arrived,
                device_id=worker_device(0, at_tile, at_band),
                device_id_type=MESH,
            )))

        for n, (side, at, _) in enumerate(clip_edges):
            add(has_beside, clip_corner.at[n], corner_in.at[tm, side, 1 - half], corner_sem.at[tm, side, 1 - half],
                at, beside)
        for at in range(TILES):
            add(has_beside, clip.at[:, half, at * wide:(at + 1) * wide], row_in.at[tm, 1 - half],
                row_sem.at[tm, 1 - half], at, beside)
        for n, (side, at, _) in enumerate(clip_edges):
            add(None, clip_edge.at[n], edge_in.at[tm, side, half], edge_sem.at[tm, side, half], at, band)
        for at in range(TILES):
            add(None, clip.at[:, :, at * wide:(at + 1) * wide], own_in.at[tm, :, pl.ds(pair * half, pair)],
                own_sem.at[tm, half], at, band)
        return copies

    @pl.when(sender)
    def _():
        for condition, copy in clip_copies():
            when(condition, copy.start)

    def next_copies(group):
        copies = []
        for n, (t, b) in enumerate(steps):
            if t and b:
                side, above = (1 if t < 0 else 0), (1 if b < 0 else 0)
                source = corner_out.at[group, 1 - side, 1 - above]
                target, arrived = corner_in.at[group, side, above], corner_sem.at[group, side, above]
            elif t:
                side = 1 if t < 0 else 0
                source = edge_out.at[group, 1 - side]
                target, arrived = edge_in.at[group, side, 0], edge_sem.at[group, side, 0]
            elif b:
                source = tile_out.at[group, :, 0 if b < 0 else TALL - 1]
                above = 1 if b < 0 else 0
                target, arrived = row_in.at[group, above], row_sem.at[group, above]
            else:
                source, target, arrived = tile_out.at[group], own_in.at[group], own_sem.at[group, 0]
            copies.append((inside(t, b), pltpu.make_async_remote_copy(
                src_ref=source,
                dst_ref=target,
                send_sem=next_send.at[group, n],
                recv_sem=arrived,
                device_id=worker_device(section + 1, tile + t, band + b),
                device_id_type=MESH,
            )))
        return copies

    def home_target():
        return out.at[0, :, :, pl.ds(pl.multiple_of(tile * wide, wide), wide)]

    def home_copy(group, near):
        return pltpu.make_async_remote_copy(
            src_ref=tile_out.at[group, :, near * pair:(near + 1) * pair],
            dst_ref=home_target(),
            send_sem=home_send.at[group, near],
            recv_sem=home_sem.at[tile],
            device_id=(section, group, 2 * band + near),
            device_id_type=MESH,
        )

    def own_copy(group, near):
        source = tile_out.at[group, :, near * pair:(near + 1) * pair]
        return pltpu.make_async_copy(source, home_target(), home_sem.at[tile])

    def arrived(ref, sem):
        pltpu.make_async_copy(ref, ref, sem).wait()

    def activated(value):
        factor = lax.rsqrt(jnp.mean(value * value, axis=-1, keepdims=True) + 1e-06)
        value = value * factor * gain[...]
        value = 0.5 * value
        return value + value * jnp.tanh(value)

    def taps(frame, time_tap):
        summed = jnp.zeros((cells, channels), jnp.float32)
        for row_tap in range(TAPS):
            window = hidden[pl.ds(frame, frames), row_tap:row_tap + TALL]
            summed = summed + jnp.dot(
                window.reshape(cells, TAPS * channels),
                filters[TAPS * time_tap + row_tap],
                preferred_element_type=jnp.float32,
            )
        return summed

    def process(group, carry):
        first = group * frames

        for side, t in ((0, -1), (1, 1)):
            for above, b in ((0, -1), (1, 1)):
                when(inside(t, b), lambda side=side, above=above: arrived(
                    corner_in.at[group, side, above], corner_sem.at[group, side, above]))
            when(inside(t, 0), lambda side=side: arrived(edge_in.at[group, side, 0], edge_sem.at[group, side, 0]))

            @pl.when((section == 0) & inside(t, 0))
            def _(side=side):
                arrived(edge_in.at[group, side, 1], edge_sem.at[group, side, 1])

        for above, b in ((0, -1), (1, 1)):
            when(inside(0, b), lambda above=above: arrived(row_in.at[group, above], row_sem.at[group, above]))

        @pl.when(section == 0)
        def _():
            for near in range(2):
                arrived(own_in.at[group, :, near * pair:(near + 1) * pair], own_sem.at[group, near])

        @pl.when(section > 0)
        def _():
            arrived(own_in.at[group], own_sem.at[group, 0])

        lower = lax.broadcasted_iota(jnp.int32, (edge_cells, channels), 0) >= edge_cells // 2
        stored = edge_cells + 2 * frames
        for side in range(2):
            upper, under = (
                jnp.concatenate(
                    [edge_in[group, side, p][n * edge_cells:(n + 1) * edge_cells].astype(jnp.float32)
                     for n in range(channels // LANES)],
                    axis=1,
                )
                for p in range(2)
            )
            raw[pl.ds(side * stored, edge_cells), :] = jnp.where(lower & (section == 0), under, upper)
            for above in range(2):
                at = side * stored + edge_cells + above * frames
                for n in range(channels // LANES):
                    raw[pl.ds(at, frames), n * LANES:(n + 1) * LANES] = (
                        corner_in[group, side, above, n * frames:(n + 1) * frames]
                    )
        halo[...] = activated(raw[...])

        own = own_in[group].reshape(cells, channels).astype(jnp.float32)
        middle = activated(own).reshape(frames, TALL, wide, channels)
        outer = activated(row_in[group].reshape(2 * frames * wide, channels).astype(jnp.float32))
        outer = outer.reshape(2, frames, wide, channels)
        column = lax.broadcasted_iota(jnp.int32, (wide, channels), 0)
        for frame in range(frames):
            for row in range(TALL + 2):
                if row == 0:
                    here, at = outer[0, frame], edge_cells + frame
                elif row == TALL + 1:
                    here, at = outer[1, frame], edge_cells + frames + frame
                else:
                    part, within = divmod(row - 1, pair)
                    here = middle[frame, row - 1]
                    at = part * (edge_cells // 2) + pair * frame + within
                left = jnp.where(column == 0, halo[pl.ds(at, 1), :], pltpu.roll(here, 1, 0))
                at += stored
                right = jnp.where(column == wide - 1, halo[pl.ds(at, 1), :], pltpu.roll(here, wide - 1, 0))
                for part, shifted in enumerate((left, here, right)):
                    hidden[first + ahead + frame, row, :, part * channels:(part + 1) * channels] = (
                        shifted.astype(jnp.bfloat16)
                    )

        @pl.when(group == 0)
        def _():
            load_filters.wait()

        summed = partial[...]
        for time_tap in range(1, TAPS):
            summed = summed + taps(first + time_tap, time_tap)
        result = own + summed
        tile_out[group] = result.astype(jnp.bfloat16).reshape(frames, TALL, wide, channels)

        @pl.when(section < sections - 1)
        def _():
            block = pair * wide
            for frame in range(frames):
                for part in range(TALL // pair):
                    source = (frame * (TALL // pair) + part) * block
                    for n in range(channels // LANES):
                        wide_out[n, pl.ds((part * frames + frame) * block, block), :] = (
                            result[source:source + block, n * LANES:(n + 1) * LANES]
                        )
            for side, at in enumerate((0, wide - 1)):
                parts = [
                    wide_out[n, pl.ds(at, edge_cells, stride=wide), :]
                    for n in range(channels // LANES)
                ]
                edge_out[group, side] = jnp.concatenate(parts, axis=0).astype(jnp.bfloat16)
                for above, start in enumerate((0, frames * block + (pair - 1) * wide)):
                    for lane in range(channels // LANES):
                        corner_out[group, side, above, lane * frames:(lane + 1) * frames] = (
                            wide_out[lane, pl.ds(start + at, frames, stride=block), :]
                            .astype(jnp.bfloat16).astype(jnp.float32)
                        )
            for condition, copy in next_copies(group):
                when(condition, copy.start)

        for near in range(2):
            own_home = (group == tm) & (near == half)

            @pl.when(own_home)
            def _(near=near):
                own_copy(group, near).start()

            @pl.when(jnp.logical_not(own_home))
            def _(near=near):
                home_copy(group, near).start()

        @pl.when(group < groups - 1)
        def _():
            partial[...] = taps(first + frames, 0)

        return carry

    @pl.when(worker)
    def _():
        load_gain.wait()
        lax.fori_loop(0, groups, process, 0)

    for at in range(TILES):
        arrived(out.at[0, :, :, at * wide:(at + 1) * wide], home_sem.at[at])

    @pl.when(sender)
    def _():
        for condition, copy in clip_copies():
            when(condition, copy.wait_send)

    def drain(group, carry):
        @pl.when(section < sections - 1)
        def _():
            for condition, copy in next_copies(group):
                when(condition, copy.wait_send)

        for near in range(2):
            @pl.when(jnp.logical_not((group == tm) & (near == half)))
            def _(near=near):
                home_copy(group, near).wait_send()

        return carry

    @pl.when(worker)
    def _():
        lax.fori_loop(0, groups, drain, 0)


def on_device(clip_features, conv_kernels, norm_gains):
    frames, pair, columns, channels = clip_features.shape
    groups = lax.axis_size("tm")
    wide = columns // TILES
    edge_cells = frames * TALL
    edge = (edge_cells * channels // LANES, LANES)
    corner = (frames * channels // LANES, LANES)
    edges = 2 * (TILES - 1)
    in_hbm = pl.BlockSpec(memory_space=pltpu.HBM)
    return pl.pallas_call(
        chain_kernel,
        out_shape=jax.ShapeDtypeStruct((1, frames, pair, columns, channels), jnp.bfloat16),
        in_specs=[in_hbm] * 3,
        out_specs=in_hbm,
        scratch_shapes=[
            pltpu.VMEM((groups, frames, TALL, wide, channels), jnp.bfloat16),
            pltpu.VMEM((groups, 2, frames, wide, channels), jnp.bfloat16),
            pltpu.VMEM((groups, 2, 2, *edge), jnp.bfloat16),
            pltpu.VMEM((groups, 2, 2, *corner), jnp.float32),
            pltpu.VMEM((TAPS - 1 + groups * frames, TALL + 2, wide, TAPS * channels), jnp.bfloat16),
            pltpu.VMEM((frames * TALL * wide, channels), jnp.float32),
            pltpu.VMEM((2 * (edge_cells + 2 * frames), channels), jnp.float32),
            pltpu.VMEM((2 * (edge_cells + 2 * frames), channels), jnp.float32),
            pltpu.VMEM(conv_kernels.shape[1:], jnp.bfloat16),
            pltpu.VMEM(norm_gains.shape, jnp.float32),
            pltpu.VMEM((channels // LANES, frames * TALL * wide, LANES), jnp.float32),
            pltpu.VMEM((groups, frames, TALL, wide, channels), jnp.bfloat16),
            pltpu.VMEM((groups, 2, *edge), jnp.bfloat16),
            pltpu.VMEM((groups, 2, 2, *corner), jnp.float32),
            pltpu.VMEM((frames, pair, columns, channels), jnp.bfloat16),
            pltpu.VMEM((channels // LANES, frames * pair * columns, LANES), jnp.float32),
            pltpu.VMEM((edges, *edge), jnp.bfloat16),
            pltpu.VMEM((edges, *corner), jnp.float32),
            pltpu.SemaphoreType.DMA((groups, 2)),
            pltpu.SemaphoreType.DMA((groups, 2)),
            pltpu.SemaphoreType.DMA((groups, 2, 2)),
            pltpu.SemaphoreType.DMA((groups, 2, 2)),
            pltpu.SemaphoreType.DMA((TILES,)),
            pltpu.SemaphoreType.DMA((2 * edges + 2 * TILES,)),
            pltpu.SemaphoreType.DMA((groups, 9)),
            pltpu.SemaphoreType.DMA((groups, 2)),
            pltpu.SemaphoreType.DMA((3,)),
        ],
        compiler_params=pltpu.CompilerParams(
            collective_id=0, has_side_effects=True, vmem_limit_bytes=56 * 2**20
        ),
        name="chain",
    )(clip_features, conv_kernels, norm_gains)


def solution(mesh):
    return jax.shard_map(
        on_device,
        mesh=mesh,
        in_specs=(P("tm", "space", None, None), P("section", None, None, None), P("section", None)),
        out_specs=P("section", "tm", "space", None, None),
        check_vma=False,
    )
```

```python
import jax
import jax.numpy as jnp
from jax import lax
from jax.experimental import pallas as pl
from jax.experimental.pallas import tpu as pltpu
from jax.sharding import PartitionSpec as P

MESH = pl.DeviceIdType.MESH
WORKER = 1
TAPS = 3
TALL = 4
TILES = 4
LANES = 128


def chain_kernel(
    clip, weights, gains, out,
    own_in, row_in, edge_in, corner_in, hidden, partial, raw, halo, filters, gain, wide_out, tile_out, edge_out,
    corner_out, clip_in, clip_wide, clip_edge, clip_corner,
    own_sem, row_sem, edge_sem, corner_sem, home_sem, clip_send, next_send, home_send, load_sem,
):
    section = lax.axis_index("section")
    tm = lax.axis_index("tm")
    space = lax.axis_index("space")
    sections = lax.axis_size("section")
    groups = lax.axis_size("tm")
    bands = lax.axis_size("space") // 2
    band = space // 2
    half = space % 2
    run = tm // 2
    tile = 2 * half + run
    worker = tm % 2 == WORKER
    sender = section == tm % sections
    frames, pair, columns, channels = clip.shape
    wide = columns // TILES
    cells = frames * TALL * wide
    edge_cells = frames * TALL
    ahead = TAPS - 1
    beside = band + 2 * half - 1
    has_beside = (beside >= 0) & (beside < bands)

    near_tm = {0: 2 * run + WORKER, 1: 2 * (1 - run) + WORKER, -1: 2 * (1 - run) + WORKER}
    near_half = {0: half, 1: jnp.minimum(half + run, 1), -1: jnp.maximum(half + run - 1, 0)}
    near_band = {0: 2 * band, 1: 2 * jnp.minimum(band + 1, bands - 1), -1: 2 * jnp.maximum(band - 1, 0)}
    near_space = {(t, b): near_band[b] + near_half[t] for t in (-1, 0, 1) for b in (-1, 0, 1)}
    next_section = jnp.minimum(section + 1, sections - 1)
    previous_section = jnp.maximum(section - 1, 0)
    beside_space = 2 * jnp.clip(beside, 0, bands - 1)

    def neighbour(at_section, t, b):
        return (at_section, near_tm[t], near_space[t, b])

    def in_band(at_section, at_tile, at_space):
        return (at_section, 2 * (at_tile % 2) + WORKER, at_space + at_tile // 2)

    def inside(step_tile, step_band):
        there = None
        for at, step, end in ((tile, step_tile, TILES), (band, step_band, bands)):
            if step:
                here = (at > 0) if step < 0 else (at < end - 1)
                there = here if there is None else there & here
        return there

    def when(condition, action):
        if condition is None:
            action()
        else:
            pl.when(condition)(action)

    barrier = pltpu.get_barrier_semaphore()

    def greet(device):
        pl.semaphore_signal(barrier, inc=1, device_id=device, device_id_type=MESH)

    @pl.when(worker & (section == 0))
    def _():
        for group in range(groups):
            for near in range(2):
                greet((group % sections, group, 2 * band + near))

        @pl.when(band > 0)
        def _():
            for group in range(groups):
                greet((group % sections, group, jnp.maximum(2 * band - 1, 0)))

        @pl.when(band < bands - 1)
        def _():
            for group in range(groups):
                greet((group % sections, group, jnp.minimum(2 * band + 2, 2 * bands - 1)))

    load_filters = pltpu.make_async_copy(weights.at[0], filters, load_sem.at[0])
    load_gain = pltpu.make_async_copy(gains, gain, load_sem.at[1])
    load_clip = pltpu.make_async_copy(clip, clip_in, load_sem.at[2])

    @pl.when(sender)
    def _():
        load_clip.start()

    @pl.when(worker)
    def _():
        load_gain.start()
        load_filters.start()

    steps = [(t, b) for t in (-1, 1, 0) for b in (-1, 1, 0)]

    @pl.when(worker & (section > 0))
    def _():
        for t, b in steps:
            when(inside(t, b), lambda t=t, b=b: greet(neighbour(previous_section, t, b)))

    for near in range(TILES):
        @pl.when(jnp.logical_not(worker & (tile == near)))
        def _(near=near):
            greet(in_band(section, near, near_band[0]))

    @pl.when(worker)
    def _():
        hidden[0:ahead] = jnp.zeros((ahead, *hidden.shape[1:]), hidden.dtype)
        partial[...] = jnp.zeros_like(partial)

        @pl.when(band == 0)
        def _():
            row_in[:, 0] = jnp.zeros((groups, *row_in.shape[2:]), row_in.dtype)
            corner_in[:, :, 0] = jnp.zeros((groups, 2, *corner_in.shape[3:]), corner_in.dtype)

        @pl.when(band == bands - 1)
        def _():
            row_in[:, 1] = jnp.zeros((groups, *row_in.shape[2:]), row_in.dtype)
            corner_in[:, :, 1] = jnp.zeros((groups, 2, *corner_in.shape[3:]), corner_in.dtype)

        @pl.when(section > 0)
        def _():
            edge_in[:, :, 1] = jnp.zeros((groups, 2, *edge_in.shape[3:]), edge_in.dtype)

        @pl.when(tile == 0)
        def _():
            edge_in[:, 0] = jnp.zeros((groups, *edge_in.shape[2:]), edge_in.dtype)
            corner_in[:, 0] = jnp.zeros((groups, *corner_in.shape[2:]), corner_in.dtype)

        @pl.when(tile == TILES - 1)
        def _():
            edge_in[:, 1] = jnp.zeros((groups, *edge_in.shape[2:]), edge_in.dtype)
            corner_in[:, 1] = jnp.zeros((groups, *corner_in.shape[2:]), corner_in.dtype)

    left_edges = [(0, at, at * wide - 1) for at in range(1, TILES)]
    right_edges = [(1, at, at * wide + wide) for at in range(TILES - 1)]
    clip_edges = left_edges + right_edges

    @pl.when(sender)
    def _():
        load_clip.wait()
        for n in range(channels // LANES):
            clip_wide[n] = clip_in[:, :, :, n * LANES:(n + 1) * LANES].reshape(-1, LANES).astype(jnp.float32)
        for n, (_, _, column) in enumerate(clip_edges):
            parts = []
            for lane in range(channels // LANES):
                part = clip_wide[lane, pl.ds(column, frames * pair, stride=columns), :]
                parts += [part, part]
            clip_edge[n] = jnp.concatenate(parts, axis=0).astype(jnp.bfloat16)
            for lane in range(channels // LANES):
                for row in range(pair):
                    @pl.when(half == row)
                    def _(n=n, column=column, lane=lane, row=row):
                        clip_corner[n, lane * frames:(lane + 1) * frames] = (
                            clip_wide[lane, pl.ds(row * columns + column, frames, stride=pair * columns), :]
                        )

    def one_if(condition):
        return jnp.where(condition, 1, 0)

    near_tiles = 1 + one_if(tile > 0) + one_if(tile < TILES - 1)
    near_bands = 1 + one_if(band > 0) + one_if(band < bands - 1)
    receivers = (
        one_if(sender) * TILES * (1 + one_if(has_beside))
        + one_if(worker) * (2 * groups - 1 + one_if(section < sections - 1) * near_tiles * near_bands)
    )

    @pl.when(receivers > 0)
    def _():
        pl.semaphore_wait(barrier, receivers)

    def clip_copies():
        copies = []

        def add(condition, source, target, arrived, at_tile, at_space):
            copies.append((condition, pltpu.make_async_remote_copy(
                src_ref=source,
                dst_ref=target,
                send_sem=clip_send.at[len(copies)],
                recv_sem=arrived,
                device_id=in_band(0, at_tile, at_space),
                device_id_type=MESH,
            )))

        for n, (side, at, _) in enumerate(clip_edges):
            add(has_beside, clip_corner.at[n], corner_in.at[tm, side, 1 - half], corner_sem.at[tm, side, 1 - half],
                at, beside_space)
        for at in range(TILES):
            add(has_beside, clip.at[:, half, at * wide:(at + 1) * wide], row_in.at[tm, 1 - half],
                row_sem.at[tm, 1 - half], at, beside_space)
        for n, (side, at, _) in enumerate(clip_edges):
            add(None, clip_edge.at[n], edge_in.at[tm, side, half], edge_sem.at[tm, side, half], at, near_band[0])
        for at in range(TILES):
            add(None, clip.at[:, :, at * wide:(at + 1) * wide], own_in.at[tm, :, pl.ds(pair * half, pair)],
                own_sem.at[tm, half], at, near_band[0])
        return copies

    @pl.when(sender)
    def _():
        for condition, copy in clip_copies():
            when(condition, copy.start)

    def next_copies(group):
        copies = []
        for n, (t, b) in enumerate(steps):
            if t and b:
                side, above = (1 if t < 0 else 0), (1 if b < 0 else 0)
                source = corner_out.at[group, 1 - side, 1 - above]
                target, arrived = corner_in.at[group, side, above], corner_sem.at[group, side, above]
            elif t:
                side = 1 if t < 0 else 0
                source = edge_out.at[group, 1 - side]
                target, arrived = edge_in.at[group, side, 0], edge_sem.at[group, side, 0]
            elif b:
                source = tile_out.at[group, :, 0 if b < 0 else TALL - 1]
                above = 1 if b < 0 else 0
                target, arrived = row_in.at[group, above], row_sem.at[group, above]
            else:
                source, target, arrived = tile_out.at[group], own_in.at[group], own_sem.at[group, 0]
            copies.append((inside(t, b), pltpu.make_async_remote_copy(
                src_ref=source,
                dst_ref=target,
                send_sem=next_send.at[group, n],
                recv_sem=arrived,
                device_id=neighbour(next_section, t, b),
                device_id_type=MESH,
            )))
        return copies

    def home_target():
        return out.at[0, :, :, pl.ds(pl.multiple_of(tile * wide, wide), wide)]

    def home_copy(group, near):
        return pltpu.make_async_remote_copy(
            src_ref=tile_out.at[group, :, near * pair:(near + 1) * pair],
            dst_ref=home_target(),
            send_sem=home_send.at[group, near],
            recv_sem=home_sem.at[tile],
            device_id=(section, group, 2 * band + near),
            device_id_type=MESH,
        )

    def own_copy(group, near):
        source = tile_out.at[group, :, near * pair:(near + 1) * pair]
        return pltpu.make_async_copy(source, home_target(), home_sem.at[tile])

    def arrived(ref, sem):
        pltpu.make_async_copy(ref, ref, sem).wait()

    def activated(value):
        factor = lax.rsqrt(jnp.mean(value * value, axis=-1, keepdims=True) + 1e-06)
        value = value * factor * gain[...]
        value = 0.5 * value
        return value + value * jnp.tanh(value)

    def taps(frame, time_tap):
        summed = jnp.zeros((cells, channels), jnp.float32)
        for row_tap in range(TAPS):
            window = hidden[pl.ds(frame, frames), row_tap:row_tap + TALL]
            summed = summed + jnp.dot(
                window.reshape(cells, TAPS * channels),
                filters[TAPS * time_tap + row_tap],
                preferred_element_type=jnp.float32,
            )
        return summed

    def process(group, carry):
        first = group * frames

        for side, t in ((0, -1), (1, 1)):
            for above, b in ((0, -1), (1, 1)):
                when(inside(t, b), lambda side=side, above=above: arrived(
                    corner_in.at[group, side, above], corner_sem.at[group, side, above]))
            when(inside(t, 0), lambda side=side: arrived(edge_in.at[group, side, 0], edge_sem.at[group, side, 0]))

            @pl.when((section == 0) & inside(t, 0))
            def _(side=side):
                arrived(edge_in.at[group, side, 1], edge_sem.at[group, side, 1])

        for above, b in ((0, -1), (1, 1)):
            when(inside(0, b), lambda above=above: arrived(row_in.at[group, above], row_sem.at[group, above]))

        @pl.when(section == 0)
        def _():
            for near in range(2):
                arrived(own_in.at[group, :, near * pair:(near + 1) * pair], own_sem.at[group, near])

        @pl.when(section > 0)
        def _():
            arrived(own_in.at[group], own_sem.at[group, 0])

        lower = lax.broadcasted_iota(jnp.int32, (edge_cells, channels), 0) >= edge_cells // 2
        stored = edge_cells + 2 * frames
        for side in range(2):
            upper, under = (
                jnp.concatenate(
                    [edge_in[group, side, p][n * edge_cells:(n + 1) * edge_cells].astype(jnp.float32)
                     for n in range(channels // LANES)],
                    axis=1,
                )
                for p in range(2)
            )
            raw[pl.ds(side * stored, edge_cells), :] = jnp.where(lower & (section == 0), under, upper)
            for above in range(2):
                at = side * stored + edge_cells + above * frames
                for n in range(channels // LANES):
                    raw[pl.ds(at, frames), n * LANES:(n + 1) * LANES] = (
                        corner_in[group, side, above, n * frames:(n + 1) * frames]
                    )
        halo[...] = activated(raw[...])

        own = own_in[group].reshape(cells, channels).astype(jnp.float32)
        middle = activated(own).reshape(frames, TALL, wide, channels)
        outer = activated(row_in[group].reshape(2 * frames * wide, channels).astype(jnp.float32))
        outer = outer.reshape(2, frames, wide, channels)
        column = lax.broadcasted_iota(jnp.int32, (wide, channels), 0)
        for frame in range(frames):
            for row in range(TALL + 2):
                if row == 0:
                    here, at = outer[0, frame], edge_cells + frame
                elif row == TALL + 1:
                    here, at = outer[1, frame], edge_cells + frames + frame
                else:
                    part, within = divmod(row - 1, pair)
                    here = middle[frame, row - 1]
                    at = part * (edge_cells // 2) + pair * frame + within
                left = jnp.where(column == 0, halo[pl.ds(at, 1), :], pltpu.roll(here, 1, 0))
                at += stored
                right = jnp.where(column == wide - 1, halo[pl.ds(at, 1), :], pltpu.roll(here, wide - 1, 0))
                for part, shifted in enumerate((left, here, right)):
                    hidden[first + ahead + frame, row, :, part * channels:(part + 1) * channels] = (
                        shifted.astype(jnp.bfloat16)
                    )

        @pl.when(group == 0)
        def _():
            load_filters.wait()

        summed = partial[...]
        for time_tap in range(1, TAPS):
            summed = summed + taps(first + time_tap, time_tap)
        result = own + summed
        tile_out[group] = result.astype(jnp.bfloat16).reshape(frames, TALL, wide, channels)

        @pl.when(section < sections - 1)
        def _():
            block = pair * wide
            for frame in range(frames):
                for part in range(TALL // pair):
                    source = (frame * (TALL // pair) + part) * block
                    for n in range(channels // LANES):
                        wide_out[n, pl.ds((part * frames + frame) * block, block), :] = (
                            result[source:source + block, n * LANES:(n + 1) * LANES]
                        )
            for side, at in enumerate((0, wide - 1)):
                parts = [
                    wide_out[n, pl.ds(at, edge_cells, stride=wide), :]
                    for n in range(channels // LANES)
                ]
                edge_out[group, side] = jnp.concatenate(parts, axis=0).astype(jnp.bfloat16)
                for above, start in enumerate((0, frames * block + (pair - 1) * wide)):
                    for lane in range(channels // LANES):
                        corner_out[group, side, above, lane * frames:(lane + 1) * frames] = (
                            wide_out[lane, pl.ds(start + at, frames, stride=block), :]
                            .astype(jnp.bfloat16).astype(jnp.float32)
                        )
            for condition, copy in next_copies(group):
                when(condition, copy.start)

        for near in range(2):
            own_home = (group == tm) & (near == half)

            @pl.when(own_home)
            def _(near=near):
                own_copy(group, near).start()

            @pl.when(jnp.logical_not(own_home))
            def _(near=near):
                home_copy(group, near).start()

        @pl.when(group < groups - 1)
        def _():
            partial[...] = taps(first + frames, 0)

        return carry

    @pl.when(worker)
    def _():
        load_gain.wait()
        lax.fori_loop(0, groups, process, 0)

    for at in range(TILES):
        arrived(out.at[0, :, :, at * wide:(at + 1) * wide], home_sem.at[at])

    @pl.when(sender)
    def _():
        for condition, copy in clip_copies():
            when(condition, copy.wait_send)

    def drain(group, carry):
        @pl.when(section < sections - 1)
        def _():
            for condition, copy in next_copies(group):
                when(condition, copy.wait_send)

        for near in range(2):
            @pl.when(jnp.logical_not((group == tm) & (near == half)))
            def _(near=near):
                home_copy(group, near).wait_send()

        return carry

    @pl.when(worker)
    def _():
        lax.fori_loop(0, groups, drain, 0)


def on_device(clip_features, conv_kernels, norm_gains):
    frames, pair, columns, channels = clip_features.shape
    groups = lax.axis_size("tm")
    wide = columns // TILES
    edge_cells = frames * TALL
    edge = (edge_cells * channels // LANES, LANES)
    corner = (frames * channels // LANES, LANES)
    edges = 2 * (TILES - 1)
    in_hbm = pl.BlockSpec(memory_space=pltpu.HBM)
    return pl.pallas_call(
        chain_kernel,
        out_shape=jax.ShapeDtypeStruct((1, frames, pair, columns, channels), jnp.bfloat16),
        in_specs=[in_hbm] * 3,
        out_specs=in_hbm,
        scratch_shapes=[
            pltpu.VMEM((groups, frames, TALL, wide, channels), jnp.bfloat16),
            pltpu.VMEM((groups, 2, frames, wide, channels), jnp.bfloat16),
            pltpu.VMEM((groups, 2, 2, *edge), jnp.bfloat16),
            pltpu.VMEM((groups, 2, 2, *corner), jnp.float32),
            pltpu.VMEM((TAPS - 1 + groups * frames, TALL + 2, wide, TAPS * channels), jnp.bfloat16),
            pltpu.VMEM((frames * TALL * wide, channels), jnp.float32),
            pltpu.VMEM((2 * (edge_cells + 2 * frames), channels), jnp.float32),
            pltpu.VMEM((2 * (edge_cells + 2 * frames), channels), jnp.float32),
            pltpu.VMEM(conv_kernels.shape[1:], jnp.bfloat16),
            pltpu.VMEM(norm_gains.shape, jnp.float32),
            pltpu.VMEM((channels // LANES, frames * TALL * wide, LANES), jnp.float32),
            pltpu.VMEM((groups, frames, TALL, wide, channels), jnp.bfloat16),
            pltpu.VMEM((groups, 2, *edge), jnp.bfloat16),
            pltpu.VMEM((groups, 2, 2, *corner), jnp.float32),
            pltpu.VMEM((frames, pair, columns, channels), jnp.bfloat16),
            pltpu.VMEM((channels // LANES, frames * pair * columns, LANES), jnp.float32),
            pltpu.VMEM((edges, *edge), jnp.bfloat16),
            pltpu.VMEM((edges, *corner), jnp.float32),
            pltpu.SemaphoreType.DMA((groups, 2)),
            pltpu.SemaphoreType.DMA((groups, 2)),
            pltpu.SemaphoreType.DMA((groups, 2, 2)),
            pltpu.SemaphoreType.DMA((groups, 2, 2)),
            pltpu.SemaphoreType.DMA((TILES,)),
            pltpu.SemaphoreType.DMA((2 * edges + 2 * TILES,)),
            pltpu.SemaphoreType.DMA((groups, 9)),
            pltpu.SemaphoreType.DMA((groups, 2)),
            pltpu.SemaphoreType.DMA((3,)),
        ],
        compiler_params=pltpu.CompilerParams(
            collective_id=0, has_side_effects=True, vmem_limit_bytes=56 * 2**20
        ),
        name="chain",
    )(clip_features, conv_kernels, norm_gains)


def solution(mesh):
    return jax.shard_map(
        on_device,
        mesh=mesh,
        in_specs=(P("tm", "space", None, None), P("section", None, None, None), P("section", None)),
        out_specs=P("section", "tm", "space", None, None),
        check_vma=False,
    )
```

```python
import jax
import jax.numpy as jnp
from jax import lax
from jax.experimental import pallas as pl
from jax.experimental.pallas import tpu as pltpu
from jax.sharding import PartitionSpec as P

MESH = pl.DeviceIdType.MESH
WORKER = 1
TAPS = 3
TALL = 4
HEAD = 3
TILES = 4
LANES = 128


def chain_kernel(
    clip, weights, gains, out,
    rows_in, edge_in, hidden, partial, halo, filters, gain, wide_out, tile_out, edge_out,
    clip_in, clip_wide, clip_edge,
    rows_sem, edge_sem, home_sem, clip_send, next_send, home_send, load_sem,
):
    section = lax.axis_index("section")
    tm = lax.axis_index("tm")
    space = lax.axis_index("space")
    sections = lax.axis_size("section")
    groups = lax.axis_size("tm")
    bands = lax.axis_size("space") // 2
    band = space // 2
    half = space % 2
    run = tm // 2
    tile = 2 * half + run
    worker = tm % 2 == WORKER
    sender = section == tm % sections
    frames, pair, columns, channels = clip.shape
    wide = columns // TILES
    cells = frames * TALL * wide
    edge_cells = frames * TALL
    ahead = TAPS - 1
    low = sections - 1 - section
    first_band = band == 0
    has_below = band < bands - 1

    near_tm = {0: 2 * run + WORKER, 1: 2 * (1 - run) + WORKER, -1: 2 * (1 - run) + WORKER}
    near_half = {0: half, 1: jnp.minimum(half + run, 1), -1: jnp.maximum(half + run - 1, 0)}
    near_band = {0: 2 * band, 1: 2 * jnp.minimum(band + 1, bands - 1), -1: 2 * jnp.maximum(band - 1, 0)}
    near_space = {(t, b): near_band[b] + near_half[t] for t in (-1, 0, 1) for b in (-1, 0, 1)}
    next_section = jnp.minimum(section + 1, sections - 1)
    previous_section = jnp.maximum(section - 1, 0)

    def neighbour(at_section, t, b):
        return (at_section, near_tm[t], near_space[t, b])

    def in_band(at_section, at_tile, at_space):
        return (at_section, 2 * (at_tile % 2) + WORKER, at_space + at_tile // 2)

    def owner(row):
        return jnp.maximum(row - low, 0) // TALL

    def inside(t):
        return (tile > 0) if t < 0 else (tile < TILES - 1)

    def tile_when(t, action):
        if t:
            pl.when(inside(t))(action)
        else:
            action()

    barrier = pltpu.get_barrier_semaphore()

    def greet(device):
        pl.semaphore_signal(barrier, inc=1, device_id=device, device_id_type=MESH)

    @pl.when(worker)
    def _():
        rows_in[...] = jnp.zeros_like(rows_in)
        edge_in[...] = jnp.zeros_like(edge_in)
        hidden[0:ahead] = jnp.zeros((ahead, *hidden.shape[1:]), hidden.dtype)
        partial[...] = jnp.zeros_like(partial)

    @pl.when(worker & (section == 0))
    def _():
        for group in range(groups):
            greet((group % sections, group, near_band[0] + 1))

        @pl.when(has_below)
        def _():
            for group in range(groups):
                for near in range(2):
                    greet((group % sections, group, near_band[1] + near))

        @pl.when(first_band)
        def _():
            for group in range(groups):
                greet((group % sections, group, 0))

    load_filters = pltpu.make_async_copy(weights.at[0], filters, load_sem.at[0])
    load_gain = pltpu.make_async_copy(gains, gain, load_sem.at[1])
    load_clip = pltpu.make_async_copy(clip, clip_in, load_sem.at[2])

    @pl.when(sender)
    def _():
        load_clip.start()

    @pl.when(worker)
    def _():
        load_gain.start()
        load_filters.start()

    @pl.when(worker & (section > 0))
    def _():
        for t in (-1, 1, 0):
            def _(t=t):
                greet(neighbour(previous_section, t, 0))

                @pl.when(band > 0)
                def _():
                    greet(neighbour(previous_section, t, -1))

            tile_when(t, _)

    owners = [owner(2 * space + near) for near in range(pair)]
    for near in range(pair):
        for at in range(TILES):
            @pl.when(jnp.logical_not(worker & (tile == at) & (owners[near] == band)))
            def _(near=near, at=at):
                greet(in_band(section, at, 2 * owners[near]))

    left_edges = [(0, at, at * wide - 1) for at in range(1, TILES)]
    right_edges = [(1, at, at * wide + wide) for at in range(TILES - 1)]
    clip_edges = left_edges + right_edges

    @pl.when(sender)
    def _():
        load_clip.wait()
        for n in range(channels // LANES):
            clip_wide[n] = clip_in[:, :, :, n * LANES:(n + 1) * LANES].reshape(-1, LANES).astype(jnp.float32)
        for n, (_, _, column) in enumerate(clip_edges):
            parts = []
            for lane in range(channels // LANES):
                cells_of = [
                    clip_wide[lane, pl.ds(row * columns + column, frames, stride=pair * columns), :]
                    for row in range(pair)
                ]
                parts += cells_of + cells_of
            clip_edge[n] = jnp.concatenate(parts, axis=0).astype(jnp.bfloat16)


    def one_if(condition):
        return jnp.where(condition, 1, 0)

    near_tiles = 1 + one_if(tile > 0) + one_if(tile < TILES - 1)
    own_rows = TALL - one_if(band == bands - 1) * low + one_if(first_band) * low
    own_homes = one_if(owners[0] == band) + one_if(owners[1] == band)
    receivers = (
        one_if(sender) * TILES * (1 + one_if((half == 1) & (band > 0)))
        + one_if(worker) * (
            own_rows * groups - own_homes + one_if(section < sections - 1) * near_tiles * (1 + one_if(has_below))
        )
    )

    @pl.when(receivers > 0)
    def _():
        pl.semaphore_wait(barrier, receivers)

    def clip_copies(part, at_space, start):
        copies = []

        def add(source, target, arrived, at):
            copies.append(pltpu.make_async_remote_copy(
                src_ref=source,
                dst_ref=target,
                send_sem=clip_send.at[start + len(copies)],
                recv_sem=arrived,
                device_id=in_band(0, at, at_space),
                device_id_type=MESH,
            ))

        for n, (side, at, _) in enumerate(clip_edges):
            add(clip_edge.at[n], edge_in.at[tm, side, part], edge_sem.at[tm, side, part], at)
        for at in range(TILES):
            add(clip_in.at[:, :, at * wide:(at + 1) * wide], rows_in.at[tm, :, pl.ds(1 + 2 * part, pair)],
                rows_sem.at[tm, part], at)
        return copies

    clip_part = jnp.where(half == 1, 1, jnp.where(first_band, 0, 2))
    clip_space = jnp.where(half == 1, near_band[0], near_band[-1])

    def both_clip_copies(act):
        @pl.when(sender)
        def _():
            for copy in clip_copies(clip_part, clip_space, 0):
                act(copy)

        @pl.when(sender & (half == 1) & (band > 0))
        def _():
            for copy in clip_copies(3, near_band[-1], len(clip_edges) + TILES):
                act(copy)

    both_clip_copies(lambda copy: copy.start())

    def next_copy(group, t, part):
        step = 1 if part == 1 else 0
        if t:
            side = 1 if t < 0 else 0
            source = edge_out.at[group, 1 - side, 0 if part else 1]
            target, arrived = edge_in.at[group, side, part], edge_sem.at[group, side, part]
        else:
            begin, end = ((0, HEAD), (HEAD + TALL - 2, HEAD + TALL), (HEAD, HEAD + TALL))[part]
            source = tile_out.at[group, :, begin:end]
            offset = 2 - step * TALL
            target, arrived = rows_in.at[group, :, begin + offset:end + offset], rows_sem.at[group, part]
        return pltpu.make_async_remote_copy(
            src_ref=source,
            dst_ref=target,
            send_sem=next_send.at[group, t + 1, part],
            recv_sem=arrived,
            device_id=neighbour(next_section, t, step),
            device_id_type=MESH,
        )

    def all_next_copies(group, act):
        for part, condition in ((1, has_below), (0, first_band), (2, None)):
            def _(part=part):
                for t in (-1, 1, 0):
                    tile_when(t, lambda t=t: act(next_copy(group, t, part)))

            if condition is None:
                _()
            else:
                pl.when(condition)(_)

    def home_copy(group, row, remote):
        source = tile_out.at[group, :, HEAD + row]
        at = jnp.maximum(low + row, 0)
        within = at % TALL
        target = out.at[0, :, within % pair, pl.ds(pl.multiple_of(tile * wide, wide), wide)]
        at_space = jnp.minimum(near_band[0] + 2 * (at // TALL) + within // pair, 2 * bands - 1)
        if not remote:
            return pltpu.make_async_copy(source, target, home_sem.at[tile, within % pair]), at_space
        return pltpu.make_async_remote_copy(
            src_ref=source,
            dst_ref=target,
            send_sem=home_send.at[group, HEAD + row],
            recv_sem=home_sem.at[tile, within % pair],
            device_id=(section, group, at_space),
            device_id_type=MESH,
        ), at_space

    def all_home_copies(group, act):
        for row in range(-HEAD, TALL):
            there = (first_band & (low + row >= 0)) if row < 0 else (TALL * band + low + row < TALL * bands)

            @pl.when(there)
            def _(row=row):
                remote, at_space = home_copy(group, row, True)
                stays = (group == tm) & (at_space == space)

                @pl.when(jnp.logical_not(stays))
                def _():
                    act(remote)

                if act is start:
                    @pl.when(stays)
                    def _():
                        home_copy(group, row, False)[0].start()

    def start(copy):
        copy.start()

    def wait_send(copy):
        copy.wait_send()

    def arrived(ref, sem):
        pltpu.make_async_copy(ref, ref, sem).wait()

    def activated(value):
        factor = lax.rsqrt(jnp.mean(value * value, axis=-1, keepdims=True) + 1e-06)
        value = value * factor * gain[...]
        value = 0.5 * value
        return value + value * jnp.tanh(value)

    def taps(frame, time_tap, top):
        count = HEAD + TALL - top
        summed = jnp.zeros((frames * count * wide, channels), jnp.float32)
        for row_tap in range(TAPS):
            window = hidden[pl.ds(frame, frames), top + row_tap:top + row_tap + count]
            summed = summed + jnp.dot(
                window.reshape(frames * count * wide, TAPS * channels),
                filters[TAPS * time_tap + row_tap],
                preferred_element_type=jnp.float32,
            )
        return summed

    def receive(group, part, rows):
        for side, t in ((0, -1), (1, 1)):
            tile_when(t, lambda side=side: arrived(edge_in.at[group, side, part], edge_sem.at[group, side, part]))
        arrived(rows_in.at[group, :, rows[0]:rows[1]], rows_sem.at[group, part])

    def process(group, top):
        first = group * frames
        count = HEAD + TALL - top

        @pl.when(section == 0)
        def _():
            if top == 0:
                receive(group, 0, (1, 3))
            receive(group, 1, (3, 5))

            @pl.when(has_below)
            def _():
                receive(group, 2, (5, 7))
                receive(group, 3, (7, 9))

        @pl.when(section > 0)
        def _():
            if top == 0:
                receive(group, 0, (2, 5))
            else:
                receive(group, 1, (3, 5))
            receive(group, 2, (5, 9))

        lower = lax.broadcasted_iota(jnp.int32, (edge_cells, channels), 0) >= edge_cells // 2
        pieces = []
        for side in range(2):
            upper, above, middle, under = (
                jnp.concatenate(
                    [edge_in[group, side, p][n * edge_cells:(n + 1) * edge_cells].astype(jnp.float32)
                     for n in range(channels // LANES)],
                    axis=1,
                )
                for p in range(4)
            )
            pieces += [jnp.where(lower & (section == 0), under, middle), above] + ([upper] if top == 0 else [])
        halo[0:len(pieces) * edge_cells] = activated(jnp.concatenate(pieces, axis=0))
        per_side = len(pieces) // 2 * edge_cells

        def edge_cell(side, row, frame):
            def cell(piece, at):
                return halo[pl.ds(side * per_side + piece * edge_cells + at * frames + frame, 1), :]

            if row >= 5:
                return cell(0, row - 5)
            if top:
                return cell(1, row - 1)
            if row >= 3:
                return jnp.where(section == 0, cell(1, row - 1), cell(2, row - 2))
            if row == 2:
                return jnp.where(section == 0, cell(2, 1), cell(2, 0))
            return cell(2, 0)

        taken = count + TAPS - 1
        given = rows_in[group, :, top:top + taken].reshape(frames * taken * wide, channels).astype(jnp.float32)
        values = activated(given).reshape(frames, taken, wide, channels)
        column = lax.broadcasted_iota(jnp.int32, (wide, channels), 0)
        for frame in range(frames):
            for row in range(top, top + taken):
                here = values[frame, row - top]
                image_row = TALL * band + low - TALL + row
                inside_image = (image_row >= 0) & (image_row < TALL * bands)
                left = jnp.where(column == 0, edge_cell(0, row, frame), pltpu.roll(here, 1, 0))
                right = jnp.where(column == wide - 1, edge_cell(1, row, frame), pltpu.roll(here, wide - 1, 0))
                for part, shifted in enumerate((left, here, right)):
                    hidden[first + ahead + frame, row, :, part * channels:(part + 1) * channels] = (
                        jnp.where(inside_image, shifted, 0.0).astype(jnp.bfloat16)
                    )

        @pl.when(group == 0)
        def _():
            load_filters.wait()

        own = given.reshape(frames, taken, wide, channels)[:, 1:1 + count].reshape(frames * count * wide, channels)
        summed = partial[0:frames * count * wide]
        for time_tap in range(1, TAPS):
            summed = summed + taps(first + time_tap, time_tap, top)
        result = own + summed
        tile_out[group, :, top:] = result.astype(jnp.bfloat16).reshape(frames, count, wide, channels)

        @pl.when(section < sections - 1)
        def _():
            for frame in range(frames):
                for row in range(count):
                    source = (frame * count + row) * wide
                    at = (row + top - HEAD) if row + top >= HEAD else TALL + row
                    for lane in range(channels // LANES):
                        wide_out[lane, pl.ds((at * frames + frame) * wide, wide), :] = (
                            result[source:source + wide, lane * LANES:(lane + 1) * LANES]
                        )
            for side, at in enumerate((0, wide - 1)):
                for piece in range(1 if top else 2):
                    parts = [
                        wide_out[lane, pl.ds(piece * edge_cells * wide + at, edge_cells, stride=wide), :]
                        for lane in range(channels // LANES)
                    ]
                    edge_out[group, side, piece] = jnp.concatenate(parts, axis=0).astype(jnp.bfloat16)
            all_next_copies(group, start)

        all_home_copies(group, start)

        @pl.when(group < groups - 1)
        def _():
            partial[0:frames * count * wide] = taps(first + frames, 0, top)

    def process_group(group, carry):
        @pl.when(first_band)
        def _():
            process(group, 0)

        @pl.when(jnp.logical_not(first_band))
        def _():
            process(group, HEAD)

        return carry

    @pl.when(worker)
    def _():
        wide_out[...] = jnp.zeros_like(wide_out)
        load_gain.wait()
        lax.fori_loop(0, groups, process_group, 0)

    for near in range(pair):
        for at in range(TILES):
            arrived(out.at[0, :, near, at * wide:(at + 1) * wide], home_sem.at[at, near])

    both_clip_copies(wait_send)

    def drain(group, carry):
        @pl.when(section < sections - 1)
        def _():
            all_next_copies(group, wait_send)

        all_home_copies(group, wait_send)
        return carry

    @pl.when(worker)
    def _():
        lax.fori_loop(0, groups, drain, 0)


def on_device(clip_features, conv_kernels, norm_gains):
    frames, pair, columns, channels = clip_features.shape
    groups = lax.axis_size("tm")
    wide = columns // TILES
    edge_cells = frames * TALL
    edge = (edge_cells * channels // LANES, LANES)
    tallest = HEAD + TALL
    edges = 2 * (TILES - 1)
    in_hbm = pl.BlockSpec(memory_space=pltpu.HBM)
    return pl.pallas_call(
        chain_kernel,
        out_shape=jax.ShapeDtypeStruct((1, frames, pair, columns, channels), jnp.bfloat16),
        in_specs=[in_hbm] * 3,
        out_specs=in_hbm,
        scratch_shapes=[
            pltpu.VMEM((groups, frames, tallest + 2, wide, channels), jnp.bfloat16),
            pltpu.VMEM((groups, 2, 4, *edge), jnp.bfloat16),
            pltpu.VMEM((TAPS - 1 + groups * frames, tallest + 2, wide, TAPS * channels), jnp.bfloat16),
            pltpu.VMEM((frames * tallest * wide, channels), jnp.float32),
            pltpu.VMEM((2 * 3 * edge_cells, channels), jnp.float32),
            pltpu.VMEM(conv_kernels.shape[1:], jnp.bfloat16),
            pltpu.VMEM(norm_gains.shape, jnp.float32),
            pltpu.VMEM((channels // LANES, frames * 2 * TALL * wide, LANES), jnp.float32),
            pltpu.VMEM((groups, frames, tallest, wide, channels), jnp.bfloat16),
            pltpu.VMEM((groups, 2, 2, *edge), jnp.bfloat16),
            pltpu.VMEM((frames, pair, columns, channels), jnp.bfloat16),
            pltpu.VMEM((channels // LANES, frames * pair * columns, LANES), jnp.float32),
            pltpu.VMEM((edges, *edge), jnp.bfloat16),
            pltpu.SemaphoreType.DMA((groups, 4)),
            pltpu.SemaphoreType.DMA((groups, 2, 4)),
            pltpu.SemaphoreType.DMA((TILES, pair)),
            pltpu.SemaphoreType.DMA((2 * (edges + TILES),)),
            pltpu.SemaphoreType.DMA((groups, 3, 3)),
            pltpu.SemaphoreType.DMA((groups, tallest)),
            pltpu.SemaphoreType.DMA((3,)),
        ],
        compiler_params=pltpu.CompilerParams(
            collective_id=0, has_side_effects=True, vmem_limit_bytes=56 * 2**20
        ),
        name="chain",
    )(clip_features, conv_kernels, norm_gains)


def solution(mesh):
    return jax.shard_map(
        on_device,
        mesh=mesh,
        in_specs=(P("tm", "space", None, None), P("section", None, None, None), P("section", None)),
        out_specs=P("section", "tm", "space", None, None),
        check_vma=False,
    )
```

```python
import jax
import jax.numpy as jnp
from jax import lax
from jax.experimental import pallas as pl
from jax.experimental.pallas import tpu as pltpu
from jax.sharding import PartitionSpec as P

MESH = pl.DeviceIdType.MESH
WORKER = 1
EXTRA_Z = 1
TAPS = 3
TALL = 4
TILES = 4
LANES = 128


def chain_kernel(
    clip, weights, gains, out,
    rows_in, edge_in, hidden, partial, halo, filters, gain, wide_out, tile_out, edge_out,
    clip_in, clip_wide, clip_edge,
    rows_sem, edge_sem, home_sem, clip_send, next_send, home_send, load_sem,
):
    section = lax.axis_index("section")
    tm = lax.axis_index("tm")
    space = lax.axis_index("space")
    sections = lax.axis_size("section")
    groups = lax.axis_size("tm")
    bands = lax.axis_size("space") // 2
    home_band = space // 2
    half = space % 2
    run = tm // 2
    tile = 2 * half + run
    extra = (tm % 2 != WORKER) & (home_band == EXTRA_Z)
    worker = (tm % 2 == WORKER) | extra
    band = jnp.where(extra, -1, home_band)
    sender = section == jnp.where((tm == 0) & (space == 0), 1, tm % sections)
    frames, pair, columns, channels = clip.shape
    wide = columns // TILES
    cells = frames * TALL * wide
    edge_cells = frames * TALL
    ahead = TAPS - 1
    low = sections - 1 - section
    has_above = band >= 0
    has_below = band < bands - 1

    def worker_device(at_section, at_tile, at_band):
        return (
            at_section,
            2 * (at_tile % 2) + jnp.where(at_band < 0, 1 - WORKER, WORKER),
            2 * jnp.where(at_band < 0, EXTRA_Z, at_band) + at_tile // 2,
        )

    near_run = {0: run, 1: 1 - run, -1: 1 - run}
    near_half = {0: half, 1: jnp.minimum(half + run, 1), -1: jnp.maximum(half + run - 1, 0)}
    near_band = {0: band, 1: jnp.minimum(band + 1, bands - 1), -1: jnp.maximum(band - 1, -1)}
    near_core = {b: jnp.where(near_band[b] < 0, 1 - WORKER, WORKER) for b in near_band}
    near_z = {b: jnp.where(near_band[b] < 0, EXTRA_Z, near_band[b]) for b in near_band}
    near_tm = {(t, b): 2 * near_run[t] + near_core[b] for t in near_run for b in near_band}
    near_space = {(t, b): 2 * near_z[b] + near_half[t] for t in near_run for b in near_band}
    next_section = jnp.minimum(section + 1, sections - 1)
    previous_section = jnp.maximum(section - 1, 0)

    def neighbour(at_section, t, b):
        return (at_section, near_tm[t, b], near_space[t, b])

    def owner(row):
        return (row - low + TALL) // TALL - 1

    homes = []
    for row in range(TALL):
        at = TALL * band + low + row
        kept = jnp.clip(at, 0, TALL * bands - 1)
        homes.append(((at >= 0) & (at < TALL * bands), kept // pair, kept % pair))

    def inside(t):
        return (tile > 0) if t < 0 else (tile < TILES - 1)

    def tile_when(t, action):
        if t:
            pl.when(inside(t))(action)
        else:
            action()

    barrier = pltpu.get_barrier_semaphore()

    def greet(device):
        pl.semaphore_signal(barrier, inc=1, device_id=device, device_id_type=MESH)

    @pl.when(worker)
    def _():
        rows_in[...] = jnp.zeros_like(rows_in)
        edge_in[...] = jnp.zeros_like(edge_in)
        hidden[0:ahead] = jnp.zeros((ahead, *hidden.shape[1:]), hidden.dtype)
        partial[...] = jnp.zeros_like(partial)

    @pl.when(worker & (section == 0))
    def _():
        @pl.when(has_below)
        def _():
            for group in range(groups):
                source = jnp.where(band < 0, 1, 0) if group == 0 else group % sections
                greet((source, group, 2 * near_band[1]))
                greet((group % sections, group, 2 * near_band[1] + 1))

        @pl.when(has_above)
        def _():
            for group in range(groups):
                greet((group % sections, group, 2 * jnp.maximum(band, 0) + 1))

    load_filters = pltpu.make_async_copy(weights.at[0], filters, load_sem.at[0])
    load_gain = pltpu.make_async_copy(gains, gain, load_sem.at[1])
    load_clip = pltpu.make_async_copy(clip, clip_in, load_sem.at[2])

    @pl.when(sender)
    def _():
        load_clip.start()

    @pl.when(worker)
    def _():
        load_gain.start()
        load_filters.start()

    @pl.when(worker & (section > 0))
    def _():
        for t in (-1, 1, 0):
            def _(t=t):
                greet(neighbour(previous_section, t, 0))

                @pl.when(has_above)
                def _():
                    greet(neighbour(previous_section, t, -1))

            tile_when(t, _)

    owners = [owner(2 * space + near) for near in range(pair)]
    for near in range(pair):
        for at in range(TILES):
            @pl.when(jnp.logical_not(worker & (tile == at) & (owners[near] == band)))
            def _(near=near, at=at):
                greet(worker_device(section, at, owners[near]))

    left_edges = [(0, at, at * wide - 1) for at in range(1, TILES)]
    right_edges = [(1, at, at * wide + wide) for at in range(TILES - 1)]
    clip_edges = left_edges + right_edges

    @pl.when(sender)
    def _():
        load_clip.wait()
        for n in range(channels // LANES):
            clip_wide[n] = clip_in[:, :, :, n * LANES:(n + 1) * LANES].reshape(-1, LANES).astype(jnp.float32)
        for n, (_, _, column) in enumerate(clip_edges):
            parts = []
            for lane in range(channels // LANES):
                cells_of = [
                    clip_wide[lane, pl.ds(row * columns + column, frames, stride=pair * columns), :]
                    for row in range(pair)
                ]
                parts += cells_of + cells_of
            clip_edge[n] = jnp.concatenate(parts, axis=0).astype(jnp.bfloat16)


    def one_if(condition):
        return jnp.where(condition, 1, 0)

    near_tiles = 1 + one_if(tile > 0) + one_if(tile < TILES - 1)
    own_rows = sum(one_if(there) for there, _, _ in homes)
    own_homes = one_if(owners[0] == band) + one_if(owners[1] == band)
    receivers = (
        one_if(sender) * TILES * (1 + half)
        + one_if(worker) * (
            own_rows * groups - own_homes + one_if(section < sections - 1) * near_tiles * (1 + one_if(has_below))
        )
    )

    @pl.when(receivers > 0)
    def _():
        pl.semaphore_wait(barrier, receivers)

    def clip_copies(part, at_band, start):
        copies = []

        def add(source, target, arrived, at):
            copies.append(pltpu.make_async_remote_copy(
                src_ref=source,
                dst_ref=target,
                send_sem=clip_send.at[start + len(copies)],
                recv_sem=arrived,
                device_id=worker_device(0, at, at_band),
                device_id_type=MESH,
            ))

        for n, (side, at, _) in enumerate(clip_edges):
            add(clip_edge.at[n], edge_in.at[tm, side, part], edge_sem.at[tm, side, part], at)
        for at in range(TILES):
            add(clip_in.at[:, :, at * wide:(at + 1) * wide], rows_in.at[tm, :, pl.ds(2 * part, pair)],
                rows_sem.at[tm, part], at)
        return copies

    def both_clip_copies(act):
        @pl.when(sender)
        def _():
            for copy in clip_copies(1 - half, home_band - 1 + half, 0):
                act(copy)

        @pl.when(sender & (half == 1))
        def _():
            for copy in clip_copies(2, home_band - 1, len(clip_edges) + TILES):
                act(copy)

    both_clip_copies(lambda copy: copy.start())

    def next_copy(group, t, part):
        step = 1 - part
        if t:
            side = 1 if t < 0 else 0
            source = edge_out.at[group, 1 - side]
            target, arrived = edge_in.at[group, side, part], edge_sem.at[group, side, part]
        elif part:
            source, target, arrived = tile_out.at[group], rows_in.at[group, :, 2:2 + TALL], rows_sem.at[group, 1]
        else:
            source, target, arrived = tile_out.at[group, :, TALL - 2:], rows_in.at[group, :, 0:2], rows_sem.at[group, 0]
        return pltpu.make_async_remote_copy(
            src_ref=source,
            dst_ref=target,
            send_sem=next_send.at[group, t + 1, part],
            recv_sem=arrived,
            device_id=neighbour(next_section, t, step),
            device_id_type=MESH,
        )

    def all_next_copies(group, act):
        @pl.when(has_below)
        def _():
            for t in (-1, 1, 0):
                tile_when(t, lambda t=t: act(next_copy(group, t, 0)))

        for t in (-1, 1, 0):
            tile_when(t, lambda t=t: act(next_copy(group, t, 1)))

    def home_copy(group, row, remote):
        _, at_space, at_row = homes[row]
        source = tile_out.at[group, :, row]
        target = out.at[0, :, at_row, pl.ds(pl.multiple_of(tile * wide, wide), wide)]
        if not remote:
            return pltpu.make_async_copy(source, target, home_sem.at[tile, at_row])
        return pltpu.make_async_remote_copy(
            src_ref=source,
            dst_ref=target,
            send_sem=home_send.at[group, row],
            recv_sem=home_sem.at[tile, at_row],
            device_id=(section, group, at_space),
            device_id_type=MESH,
        )

    def all_home_copies(group, act):
        for row in range(TALL):
            there, at_space, _ = homes[row]
            stays = (group == tm) & (at_space == space)

            @pl.when(there & jnp.logical_not(stays))
            def _(row=row):
                act(home_copy(group, row, True))

            if act is start:
                @pl.when(there & stays)
                def _(row=row):
                    home_copy(group, row, False).start()

    def start(copy):
        copy.start()

    def wait_send(copy):
        copy.wait_send()

    def arrived(ref, sem):
        pltpu.make_async_copy(ref, ref, sem).wait()

    def activated(value):
        factor = lax.rsqrt(jnp.mean(value * value, axis=-1, keepdims=True) + 1e-06)
        value = value * factor * gain[...]
        value = 0.5 * value
        return value + value * jnp.tanh(value)

    def taps(frame, time_tap):
        summed = jnp.zeros((cells, channels), jnp.float32)
        for row_tap in range(TAPS):
            window = hidden[pl.ds(frame, frames), row_tap:row_tap + TALL]
            summed = summed + jnp.dot(
                window.reshape(cells, TAPS * channels),
                filters[TAPS * time_tap + row_tap],
                preferred_element_type=jnp.float32,
            )
        return summed

    def receive(group, part, rows):
        for side, t in ((0, -1), (1, 1)):
            tile_when(t, lambda side=side: arrived(edge_in.at[group, side, part], edge_sem.at[group, side, part]))
        arrived(rows_in.at[group, :, rows[0]:rows[1]], rows_sem.at[group, part])

    def process(group, carry):
        first = group * frames

        @pl.when(has_above)
        def _():
            receive(group, 0, (0, 2))

        @pl.when((section == 0) & has_below)
        def _():
            receive(group, 1, (2, 4))
            receive(group, 2, (4, 6))

        @pl.when(section > 0)
        def _():
            receive(group, 1, (2, 6))

        lower = lax.broadcasted_iota(jnp.int32, (edge_cells, channels), 0) >= edge_cells // 2
        pieces = []
        for side in range(2):
            above, middle, under = (
                jnp.concatenate(
                    [edge_in[group, side, p][n * edge_cells:(n + 1) * edge_cells].astype(jnp.float32)
                     for n in range(channels // LANES)],
                    axis=1,
                )
                for p in range(3)
            )
            pieces += [above, jnp.where(lower & (section == 0), under, middle)]
        halo[...] = activated(jnp.concatenate(pieces, axis=0))

        def edge_cell(side, row, frame):
            at = (2 * side * TALL + row + TALL - 2) * frames + frame
            return halo[pl.ds(at, 1), :]

        taken = TALL + 2
        given = rows_in[group].reshape(frames * taken * wide, channels).astype(jnp.float32)
        values = activated(given).reshape(frames, taken, wide, channels)
        column = lax.broadcasted_iota(jnp.int32, (wide, channels), 0)
        for frame in range(frames):
            for row in range(taken):
                here = values[frame, row]
                image_row = TALL * band + low - 1 + row
                inside_image = (image_row >= 0) & (image_row < TALL * bands)
                left = jnp.where(column == 0, edge_cell(0, row, frame), pltpu.roll(here, 1, 0))
                right = jnp.where(column == wide - 1, edge_cell(1, row, frame), pltpu.roll(here, wide - 1, 0))
                for part, shifted in enumerate((left, here, right)):
                    hidden[first + ahead + frame, row, :, part * channels:(part + 1) * channels] = (
                        jnp.where(inside_image, shifted, 0.0).astype(jnp.bfloat16)
                    )

        @pl.when(group == 0)
        def _():
            load_filters.wait()

        own = given.reshape(frames, taken, wide, channels)[:, 1:1 + TALL].reshape(cells, channels)
        summed = partial[...]
        for time_tap in range(1, TAPS):
            summed = summed + taps(first + time_tap, time_tap)
        result = own + summed
        tile_out[group] = result.astype(jnp.bfloat16).reshape(frames, TALL, wide, channels)

        @pl.when(section < sections - 1)
        def _():
            for frame in range(frames):
                for row in range(TALL):
                    source = (frame * TALL + row) * wide
                    for lane in range(channels // LANES):
                        wide_out[lane, pl.ds((row * frames + frame) * wide, wide), :] = (
                            result[source:source + wide, lane * LANES:(lane + 1) * LANES]
                        )
            for side, at in enumerate((0, wide - 1)):
                parts = [
                    wide_out[lane, pl.ds(at, edge_cells, stride=wide), :]
                    for lane in range(channels // LANES)
                ]
                edge_out[group, side] = jnp.concatenate(parts, axis=0).astype(jnp.bfloat16)
            all_next_copies(group, start)

        all_home_copies(group, start)

        @pl.when(group < groups - 1)
        def _():
            partial[...] = taps(first + frames, 0)

        return carry

    @pl.when(worker)
    def _():
        load_gain.wait()
        lax.fori_loop(0, groups, process, 0)

    for near in range(pair):
        for at in range(TILES):
            arrived(out.at[0, :, near, at * wide:(at + 1) * wide], home_sem.at[at, near])

    both_clip_copies(wait_send)

    def drain(group, carry):
        @pl.when(section < sections - 1)
        def _():
            all_next_copies(group, wait_send)

        all_home_copies(group, wait_send)
        return carry

    @pl.when(worker)
    def _():
        lax.fori_loop(0, groups, drain, 0)


def on_device(clip_features, conv_kernels, norm_gains):
    frames, pair, columns, channels = clip_features.shape
    groups = lax.axis_size("tm")
    wide = columns // TILES
    edge_cells = frames * TALL
    edge = (edge_cells * channels // LANES, LANES)
    edges = 2 * (TILES - 1)
    in_hbm = pl.BlockSpec(memory_space=pltpu.HBM)
    return pl.pallas_call(
        chain_kernel,
        out_shape=jax.ShapeDtypeStruct((1, frames, pair, columns, channels), jnp.bfloat16),
        in_specs=[in_hbm] * 3,
        out_specs=in_hbm,
        scratch_shapes=[
            pltpu.VMEM((groups, frames, TALL + 2, wide, channels), jnp.bfloat16),
            pltpu.VMEM((groups, 2, 3, *edge), jnp.bfloat16),
            pltpu.VMEM((TAPS - 1 + groups * frames, TALL + 2, wide, TAPS * channels), jnp.bfloat16),
            pltpu.VMEM((frames * TALL * wide, channels), jnp.float32),
            pltpu.VMEM((2 * 2 * edge_cells, channels), jnp.float32),
            pltpu.VMEM(conv_kernels.shape[1:], jnp.bfloat16),
            pltpu.VMEM(norm_gains.shape, jnp.float32),
            pltpu.VMEM((channels // LANES, frames * TALL * wide, LANES), jnp.float32),
            pltpu.VMEM((groups, frames, TALL, wide, channels), jnp.bfloat16),
            pltpu.VMEM((groups, 2, *edge), jnp.bfloat16),
            pltpu.VMEM((frames, pair, columns, channels), jnp.bfloat16),
            pltpu.VMEM((channels // LANES, frames * pair * columns, LANES), jnp.float32),
            pltpu.VMEM((edges, *edge), jnp.bfloat16),
            pltpu.SemaphoreType.DMA((groups, 3)),
            pltpu.SemaphoreType.DMA((groups, 2, 3)),
            pltpu.SemaphoreType.DMA((TILES, pair)),
            pltpu.SemaphoreType.DMA((2 * (edges + TILES),)),
            pltpu.SemaphoreType.DMA((groups, 3, 2)),
            pltpu.SemaphoreType.DMA((groups, TALL)),
            pltpu.SemaphoreType.DMA((3,)),
        ],
        compiler_params=pltpu.CompilerParams(
            collective_id=0, has_side_effects=True, vmem_limit_bytes=56 * 2**20
        ),
        name="chain",
    )(clip_features, conv_kernels, norm_gains)


def solution(mesh):
    return jax.shard_map(
        on_device,
        mesh=mesh,
        in_specs=(P("tm", "space", None, None), P("section", None, None, None), P("section", None)),
        out_specs=P("section", "tm", "space", None, None),
        check_vma=False,
    )
```

```python
import jax
import jax.numpy as jnp
from jax import lax
from jax.experimental import pallas as pl
from jax.experimental.pallas import tpu as pltpu
from jax.sharding import PartitionSpec as P

MESH = pl.DeviceIdType.MESH
WORKER = 1
TAPS = 3
TALL = 4
TILES = 4
LANES = 128


def chain_kernel(
    clip, weights, gains, out,
    own_in, row_in, edge_in, corner_in, hidden, partial, raw, halo, filters, gain, wide_out, tile_out, edge_out,
    corner_out, clip_in, clip_wide, clip_edge, clip_corner,
    own_sem, row_sem, edge_sem, corner_sem, home_sem, clip_send, next_send, home_send, load_sem,
):
    section = lax.axis_index("section")
    tm = lax.axis_index("tm")
    space = lax.axis_index("space")
    sections = lax.axis_size("section")
    groups = lax.axis_size("tm")
    bands = lax.axis_size("space") // 2
    band = space // 2
    half = space % 2
    run = tm // 2
    tile = 2 * half + run
    worker = tm % 2 == WORKER
    sender = section == tm % sections
    frames, pair, columns, channels = clip.shape
    wide = columns // TILES
    cells = frames * TALL * wide
    edge_cells = frames * TALL
    ahead = TAPS - 1
    beside = band + 2 * half - 1
    has_beside = (beside >= 0) & (beside < bands)

    near_tm = {0: 2 * run + WORKER, 1: 2 * (1 - run) + WORKER, -1: 2 * (1 - run) + WORKER}
    near_half = {0: half, 1: jnp.minimum(half + run, 1), -1: jnp.maximum(half + run - 1, 0)}
    near_band = {0: 2 * band, 1: 2 * jnp.minimum(band + 1, bands - 1), -1: 2 * jnp.maximum(band - 1, 0)}
    near_space = {(t, b): near_band[b] + near_half[t] for t in (-1, 0, 1) for b in (-1, 0, 1)}
    next_section = jnp.minimum(section + 1, sections - 1)
    previous_section = jnp.maximum(section - 1, 0)
    beside_space = 2 * jnp.clip(beside, 0, bands - 1)

    def neighbour(at_section, t, b):
        return (at_section, near_tm[t], near_space[t, b])

    def in_band(at_section, at_tile, at_space):
        return (at_section, 2 * (at_tile % 2) + WORKER, at_space + at_tile // 2)

    def inside(step_tile, step_band):
        there = None
        for at, step, end in ((tile, step_tile, TILES), (band, step_band, bands)):
            if step:
                here = (at > 0) if step < 0 else (at < end - 1)
                there = here if there is None else there & here
        return there

    def when(condition, action):
        if condition is None:
            action()
        else:
            pl.when(condition)(action)

    barrier = pltpu.get_barrier_semaphore()

    def greet(device):
        pl.semaphore_signal(barrier, inc=1, device_id=device, device_id_type=MESH)

    @pl.when(worker & (section == 0))
    def _():
        for group in range(groups):
            for near in range(2):
                greet((group % sections, group, 2 * band + near))

        @pl.when(band > 0)
        def _():
            for group in range(groups):
                greet((group % sections, group, jnp.maximum(2 * band - 1, 0)))

        @pl.when(band < bands - 1)
        def _():
            for group in range(groups):
                greet((group % sections, group, jnp.minimum(2 * band + 2, 2 * bands - 1)))

    load_filters = pltpu.make_async_copy(weights.at[0], filters, load_sem.at[0])
    load_gain = pltpu.make_async_copy(gains, gain, load_sem.at[1])
    load_clip = pltpu.make_async_copy(clip, clip_in, load_sem.at[2])

    @pl.when(sender)
    def _():
        load_clip.start()

    @pl.when(worker)
    def _():
        load_gain.start()
        load_filters.start()

    steps = [(t, b) for t in (-1, 1, 0) for b in (-1, 1, 0)]

    @pl.when(worker & (section > 0))
    def _():
        for t, b in steps:
            when(inside(t, b), lambda t=t, b=b: greet(neighbour(previous_section, t, b)))

    for near in range(TILES):
        @pl.when(jnp.logical_not(worker & (tile == near)))
        def _(near=near):
            greet(in_band(section, near, near_band[0]))

    @pl.when(worker)
    def _():
        hidden[0:ahead] = jnp.zeros((ahead, *hidden.shape[1:]), hidden.dtype)
        partial[...] = jnp.zeros_like(partial)

        @pl.when(band == 0)
        def _():
            row_in[:, 0] = jnp.zeros((groups, *row_in.shape[2:]), row_in.dtype)
            corner_in[:, :, 0] = jnp.zeros((groups, 2, *corner_in.shape[3:]), corner_in.dtype)

        @pl.when(band == bands - 1)
        def _():
            row_in[:, 1] = jnp.zeros((groups, *row_in.shape[2:]), row_in.dtype)
            corner_in[:, :, 1] = jnp.zeros((groups, 2, *corner_in.shape[3:]), corner_in.dtype)

        @pl.when(section > 0)
        def _():
            edge_in[:, :, 1] = jnp.zeros((groups, 2, *edge_in.shape[3:]), edge_in.dtype)

        @pl.when(tile == 0)
        def _():
            edge_in[:, 0] = jnp.zeros((groups, *edge_in.shape[2:]), edge_in.dtype)
            corner_in[:, 0] = jnp.zeros((groups, *corner_in.shape[2:]), corner_in.dtype)

        @pl.when(tile == TILES - 1)
        def _():
            edge_in[:, 1] = jnp.zeros((groups, *edge_in.shape[2:]), edge_in.dtype)
            corner_in[:, 1] = jnp.zeros((groups, *corner_in.shape[2:]), corner_in.dtype)

    left_edges = [(0, at, at * wide - 1) for at in range(1, TILES)]
    right_edges = [(1, at, at * wide + wide) for at in range(TILES - 1)]
    clip_edges = left_edges + right_edges

    @pl.when(sender)
    def _():
        load_clip.wait()
        for n in range(channels // LANES):
            clip_wide[n] = clip_in[:, :, :, n * LANES:(n + 1) * LANES].reshape(-1, LANES).astype(jnp.float32)
        for n, (_, _, column) in enumerate(clip_edges):
            parts = []
            for lane in range(channels // LANES):
                part = clip_wide[lane, pl.ds(column, frames * pair, stride=columns), :]
                parts += [part, part]
            clip_edge[n] = jnp.concatenate(parts, axis=0).astype(jnp.bfloat16)
            for lane in range(channels // LANES):
                for row in range(pair):
                    @pl.when(half == row)
                    def _(n=n, column=column, lane=lane, row=row):
                        clip_corner[n, lane * frames:(lane + 1) * frames] = (
                            clip_wide[lane, pl.ds(row * columns + column, frames, stride=pair * columns), :]
                        )

    def one_if(condition):
        return jnp.where(condition, 1, 0)

    near_tiles = 1 + one_if(tile > 0) + one_if(tile < TILES - 1)
    near_bands = 1 + one_if(band > 0) + one_if(band < bands - 1)
    receivers = (
        one_if(sender) * TILES * (1 + one_if(has_beside))
        + one_if(worker) * (2 * groups - 1 + one_if(section < sections - 1) * near_tiles * near_bands)
    )

    @pl.when(receivers > 0)
    def _():
        pl.semaphore_wait(barrier, receivers)

    def clip_copies():
        copies = []

        def add(condition, source, target, arrived, at_tile, at_space):
            copies.append((condition, pltpu.make_async_remote_copy(
                src_ref=source,
                dst_ref=target,
                send_sem=clip_send.at[len(copies)],
                recv_sem=arrived,
                device_id=in_band(0, at_tile, at_space),
                device_id_type=MESH,
            )))

        for n, (side, at, _) in enumerate(clip_edges):
            add(has_beside, clip_corner.at[n], corner_in.at[tm, side, 1 - half], corner_sem.at[tm, side, 1 - half],
                at, beside_space)
        for at in range(TILES):
            add(has_beside, clip.at[:, half, at * wide:(at + 1) * wide], row_in.at[tm, 1 - half],
                row_sem.at[tm, 1 - half], at, beside_space)
        for n, (side, at, _) in enumerate(clip_edges):
            add(None, clip_edge.at[n], edge_in.at[tm, side, half], edge_sem.at[tm, side, half], at, near_band[0])
        for at in range(TILES):
            add(None, clip.at[:, :, at * wide:(at + 1) * wide], own_in.at[tm, :, pl.ds(pair * half, pair)],
                own_sem.at[tm, half], at, near_band[0])
        return copies

    @pl.when(sender)
    def _():
        for condition, copy in clip_copies():
            when(condition, copy.start)

    def next_copies(group):
        copies = []
        for n, (t, b) in enumerate(steps):
            if t and b:
                side, above = (1 if t < 0 else 0), (1 if b < 0 else 0)
                source = corner_out.at[group, 1 - side, 1 - above]
                target, arrived = corner_in.at[group, side, above], corner_sem.at[group, side, above]
            elif t:
                side = 1 if t < 0 else 0
                source = edge_out.at[group, 1 - side]
                target, arrived = edge_in.at[group, side, 0], edge_sem.at[group, side, 0]
            elif b:
                source = tile_out.at[group, :, 0 if b < 0 else TALL - 1]
                above = 1 if b < 0 else 0
                target, arrived = row_in.at[group, above], row_sem.at[group, above]
            else:
                source, target, arrived = tile_out.at[group], own_in.at[group], own_sem.at[group, 0]
            copies.append((inside(t, b), pltpu.make_async_remote_copy(
                src_ref=source,
                dst_ref=target,
                send_sem=next_send.at[group, n],
                recv_sem=arrived,
                device_id=neighbour(next_section, t, b),
                device_id_type=MESH,
            )))
        return copies

    def home_target():
        return out.at[0, :, :, pl.ds(pl.multiple_of(tile * wide, wide), wide)]

    def home_copy(group, near):
        return pltpu.make_async_remote_copy(
            src_ref=tile_out.at[group, :, near * pair:(near + 1) * pair],
            dst_ref=home_target(),
            send_sem=home_send.at[group, near],
            recv_sem=home_sem.at[tile],
            device_id=(section, group, 2 * band + near),
            device_id_type=MESH,
        )

    def own_copy(group, near):
        source = tile_out.at[group, :, near * pair:(near + 1) * pair]
        return pltpu.make_async_copy(source, home_target(), home_sem.at[tile])

    def arrived(ref, sem):
        pltpu.make_async_copy(ref, ref, sem).wait()

    def activated(value):
        factor = lax.rsqrt(jnp.mean(value * value, axis=-1, keepdims=True) + 1e-06)
        value = value * factor * gain[...]
        value = 0.5 * value
        return value + value * jnp.tanh(value)

    def taps(frame, time_tap):
        summed = jnp.zeros((cells, channels), jnp.float32)
        for row_tap in range(TAPS):
            window = hidden[pl.ds(frame, frames), row_tap:row_tap + TALL]
            summed = summed + jnp.dot(
                window.reshape(cells, TAPS * channels),
                filters[TAPS * time_tap + row_tap],
                preferred_element_type=jnp.float32,
            )
        return summed

    def process(group, carry):
        first = group * frames

        for side, t in ((0, -1), (1, 1)):
            for above, b in ((0, -1), (1, 1)):
                when(inside(t, b), lambda side=side, above=above: arrived(
                    corner_in.at[group, side, above], corner_sem.at[group, side, above]))
            when(inside(t, 0), lambda side=side: arrived(edge_in.at[group, side, 0], edge_sem.at[group, side, 0]))

            @pl.when((section == 0) & inside(t, 0))
            def _(side=side):
                arrived(edge_in.at[group, side, 1], edge_sem.at[group, side, 1])

        for above, b in ((0, -1), (1, 1)):
            when(inside(0, b), lambda above=above: arrived(row_in.at[group, above], row_sem.at[group, above]))

        @pl.when(section == 0)
        def _():
            for near in range(2):
                arrived(own_in.at[group, :, near * pair:(near + 1) * pair], own_sem.at[group, near])

        @pl.when(section > 0)
        def _():
            arrived(own_in.at[group], own_sem.at[group, 0])

        lower = lax.broadcasted_iota(jnp.int32, (edge_cells, channels), 0) >= edge_cells // 2
        stored = edge_cells + 2 * frames
        for side in range(2):
            upper, under = (
                jnp.concatenate(
                    [edge_in[group, side, p][n * edge_cells:(n + 1) * edge_cells].astype(jnp.float32)
                     for n in range(channels // LANES)],
                    axis=1,
                )
                for p in range(2)
            )
            raw[pl.ds(side * stored, edge_cells), :] = jnp.where(lower & (section == 0), under, upper)
            for above in range(2):
                at = side * stored + edge_cells + above * frames
                for n in range(channels // LANES):
                    raw[pl.ds(at, frames), n * LANES:(n + 1) * LANES] = (
                        corner_in[group, side, above, n * frames:(n + 1) * frames]
                    )
        halo[...] = activated(raw[...])

        own = own_in[group].reshape(cells, channels).astype(jnp.float32)
        middle = activated(own).reshape(frames, TALL, wide, channels)
        outer = activated(row_in[group].reshape(2 * frames * wide, channels).astype(jnp.float32))
        outer = outer.reshape(2, frames, wide, channels)
        column = lax.broadcasted_iota(jnp.int32, (wide, channels), 0)
        for frame in range(frames):
            for row in range(TALL + 2):
                if row == 0:
                    here, at = outer[0, frame], edge_cells + frame
                elif row == TALL + 1:
                    here, at = outer[1, frame], edge_cells + frames + frame
                else:
                    part, within = divmod(row - 1, pair)
                    here = middle[frame, row - 1]
                    at = part * (edge_cells // 2) + pair * frame + within
                left = jnp.where(column == 0, halo[pl.ds(at, 1), :], pltpu.roll(here, 1, 0))
                at += stored
                right = jnp.where(column == wide - 1, halo[pl.ds(at, 1), :], pltpu.roll(here, wide - 1, 0))
                for part, shifted in enumerate((left, here, right)):
                    hidden[first + ahead + frame, row, :, part * channels:(part + 1) * channels] = (
                        shifted.astype(jnp.bfloat16)
                    )

        @pl.when(group == 0)
        def _():
            load_filters.wait()

        summed = partial[...]
        for time_tap in range(1, TAPS):
            summed = summed + taps(first + time_tap, time_tap)
        result = own + summed
        tile_out[group] = result.astype(jnp.bfloat16).reshape(frames, TALL, wide, channels)

        @pl.when(section < sections - 1)
        def _():
            block = pair * wide
            for frame in range(frames):
                for part in range(TALL // pair):
                    source = (frame * (TALL // pair) + part) * block
                    for n in range(channels // LANES):
                        wide_out[n, pl.ds((part * frames + frame) * block, block), :] = (
                            result[source:source + block, n * LANES:(n + 1) * LANES]
                        )
            for side, at in enumerate((0, wide - 1)):
                parts = [
                    wide_out[n, pl.ds(at, edge_cells, stride=wide), :]
                    for n in range(channels // LANES)
                ]
                edge_out[group, side] = jnp.concatenate(parts, axis=0).astype(jnp.bfloat16)
                for above, start in enumerate((0, frames * block + (pair - 1) * wide)):
                    for lane in range(channels // LANES):
                        corner_out[group, side, above, lane * frames:(lane + 1) * frames] = (
                            wide_out[lane, pl.ds(start + at, frames, stride=block), :]
                            .astype(jnp.bfloat16).astype(jnp.float32)
                        )
            for condition, copy in next_copies(group):
                when(condition, copy.start)

        for near in range(2):
            own_home = (group == tm) & (near == half)

            @pl.when(own_home)
            def _(near=near):
                own_copy(group, near).start()

            @pl.when(jnp.logical_not(own_home))
            def _(near=near):
                home_copy(group, near).start()

        @pl.when(group < groups - 1)
        def _():
            partial[...] = taps(first + frames, 0)

        return carry

    @pl.when(worker)
    def _():
        load_gain.wait()
        lax.fori_loop(0, groups, process, 0)

    for at in range(TILES):
        arrived(out.at[0, :, :, at * wide:(at + 1) * wide], home_sem.at[at])

    @pl.when(sender)
    def _():
        for condition, copy in clip_copies():
            when(condition, copy.wait_send)

    def drain(group, carry):
        @pl.when(section < sections - 1)
        def _():
            for condition, copy in next_copies(group):
                when(condition, copy.wait_send)

        for near in range(2):
            @pl.when(jnp.logical_not((group == tm) & (near == half)))
            def _(near=near):
                home_copy(group, near).wait_send()

        return carry

    @pl.when(worker)
    def _():
        lax.fori_loop(0, groups, drain, 0)


def on_device(clip_features, conv_kernels, norm_gains):
    frames, pair, columns, channels = clip_features.shape
    groups = lax.axis_size("tm")
    wide = columns // TILES
    edge_cells = frames * TALL
    edge = (edge_cells * channels // LANES, LANES)
    corner = (frames * channels // LANES, LANES)
    edges = 2 * (TILES - 1)
    in_hbm = pl.BlockSpec(memory_space=pltpu.HBM)
    return pl.pallas_call(
        chain_kernel,
        out_shape=jax.ShapeDtypeStruct((1, frames, pair, columns, channels), jnp.bfloat16),
        in_specs=[in_hbm] * 3,
        out_specs=in_hbm,
        scratch_shapes=[
            pltpu.VMEM((groups, frames, TALL, wide, channels), jnp.bfloat16),
            pltpu.VMEM((groups, 2, frames, wide, channels), jnp.bfloat16),
            pltpu.VMEM((groups, 2, 2, *edge), jnp.bfloat16),
            pltpu.VMEM((groups, 2, 2, *corner), jnp.float32),
            pltpu.VMEM((TAPS - 1 + groups * frames, TALL + 2, wide, TAPS * channels), jnp.bfloat16),
            pltpu.VMEM((frames * TALL * wide, channels), jnp.float32),
            pltpu.VMEM((2 * (edge_cells + 2 * frames), channels), jnp.float32),
            pltpu.VMEM((2 * (edge_cells + 2 * frames), channels), jnp.float32),
            pltpu.VMEM(conv_kernels.shape[1:], jnp.bfloat16),
            pltpu.VMEM(norm_gains.shape, jnp.float32),
            pltpu.VMEM((channels // LANES, frames * TALL * wide, LANES), jnp.float32),
            pltpu.VMEM((groups, frames, TALL, wide, channels), jnp.bfloat16),
            pltpu.VMEM((groups, 2, *edge), jnp.bfloat16),
            pltpu.VMEM((groups, 2, 2, *corner), jnp.float32),
            pltpu.VMEM((frames, pair, columns, channels), jnp.bfloat16),
            pltpu.VMEM((channels // LANES, frames * pair * columns, LANES), jnp.float32),
            pltpu.VMEM((edges, *edge), jnp.bfloat16),
            pltpu.VMEM((edges, *corner), jnp.float32),
            pltpu.SemaphoreType.DMA((groups, 2)),
            pltpu.SemaphoreType.DMA((groups, 2)),
            pltpu.SemaphoreType.DMA((groups, 2, 2)),
            pltpu.SemaphoreType.DMA((groups, 2, 2)),
            pltpu.SemaphoreType.DMA((TILES,)),
            pltpu.SemaphoreType.DMA((2 * edges + 2 * TILES,)),
            pltpu.SemaphoreType.DMA((groups, 9)),
            pltpu.SemaphoreType.DMA((groups, 2)),
            pltpu.SemaphoreType.DMA((3,)),
        ],
        compiler_params=pltpu.CompilerParams(
            collective_id=0, has_side_effects=True, vmem_limit_bytes=55040 * 2**10
        ),
        name="chain",
    )(clip_features, conv_kernels, norm_gains)


def solution(mesh):
    return jax.shard_map(
        on_device,
        mesh=mesh,
        in_specs=(P("tm", "space", None, None), P("section", None, None, None), P("section", None)),
        out_specs=P("section", "tm", "space", None, None),
        check_vma=False,
    )
```

```python
import jax
import jax.numpy as jnp
from jax import lax
from jax.experimental import pallas as pl
from jax.experimental.pallas import tpu as pltpu
from jax.sharding import PartitionSpec as P

MESH = pl.DeviceIdType.MESH
WORKER = 1
TAPS = 3
TALL = 4
TILES = 4
LANES = 128
SOURCES = (0, 3, 1, 2)


def chain_kernel(
    clip, weights, gains, out,
    own_in, row_in, edge_in, corner_in, hidden, partial, raw, halo, filters, gain, wide_out, tile_out, edge_out,
    corner_out, clip_in, clip_wide, clip_edge, clip_corner,
    own_sem, row_sem, edge_sem, corner_sem, home_sem, clip_send, next_send, home_send, load_sem,
):
    section = lax.axis_index("section")
    tm = lax.axis_index("tm")
    space = lax.axis_index("space")
    sections = lax.axis_size("section")
    groups = lax.axis_size("tm")
    bands = lax.axis_size("space") // 2
    band = space // 2
    half = space % 2
    run = tm // 2
    tile = 2 * half + run
    worker = tm % 2 == WORKER
    sender = section == sum(jnp.where(tm == group, source, 0) for group, source in enumerate(SOURCES))
    frames, pair, columns, channels = clip.shape
    wide = columns // TILES
    cells = frames * TALL * wide
    edge_cells = frames * TALL
    ahead = TAPS - 1
    beside = band + 2 * half - 1
    has_beside = (beside >= 0) & (beside < bands)

    near_tm = {0: 2 * run + WORKER, 1: 2 * (1 - run) + WORKER, -1: 2 * (1 - run) + WORKER}
    near_half = {0: half, 1: jnp.minimum(half + run, 1), -1: jnp.maximum(half + run - 1, 0)}
    near_band = {0: 2 * band, 1: 2 * jnp.minimum(band + 1, bands - 1), -1: 2 * jnp.maximum(band - 1, 0)}
    near_space = {(t, b): near_band[b] + near_half[t] for t in (-1, 0, 1) for b in (-1, 0, 1)}
    next_section = jnp.minimum(section + 1, sections - 1)
    previous_section = jnp.maximum(section - 1, 0)
    beside_space = 2 * jnp.clip(beside, 0, bands - 1)

    def neighbour(at_section, t, b):
        return (at_section, near_tm[t], near_space[t, b])

    def in_band(at_section, at_tile, at_space):
        return (at_section, 2 * (at_tile % 2) + WORKER, at_space + at_tile // 2)

    def inside(step_tile, step_band):
        there = None
        for at, step, end in ((tile, step_tile, TILES), (band, step_band, bands)):
            if step:
                here = (at > 0) if step < 0 else (at < end - 1)
                there = here if there is None else there & here
        return there

    def when(condition, action):
        if condition is None:
            action()
        else:
            pl.when(condition)(action)

    barrier = pltpu.get_barrier_semaphore()

    def greet(device):
        pl.semaphore_signal(barrier, inc=1, device_id=device, device_id_type=MESH)

    @pl.when(worker & (section == 0))
    def _():
        for group, source in enumerate(SOURCES):
            for near in range(2):
                greet((source, group, 2 * band + near))

        @pl.when(band > 0)
        def _():
            for group, source in enumerate(SOURCES):
                greet((source, group, jnp.maximum(2 * band - 1, 0)))

        @pl.when(band < bands - 1)
        def _():
            for group, source in enumerate(SOURCES):
                greet((source, group, jnp.minimum(2 * band + 2, 2 * bands - 1)))

    load_filters = pltpu.make_async_copy(weights.at[0], filters, load_sem.at[0])
    load_gain = pltpu.make_async_copy(gains, gain, load_sem.at[1])
    load_clip = pltpu.make_async_copy(clip, clip_in, load_sem.at[2])

    @pl.when(sender)
    def _():
        load_clip.start()

    @pl.when(worker)
    def _():
        load_gain.start()
        load_filters.start()

    steps = [(t, b) for t in (-1, 1, 0) for b in (-1, 1, 0)]

    @pl.when(worker & (section > 0))
    def _():
        for t, b in steps:
            when(inside(t, b), lambda t=t, b=b: greet(neighbour(previous_section, t, b)))

    for near in range(TILES):
        @pl.when(jnp.logical_not(worker & (tile == near)))
        def _(near=near):
            greet(in_band(section, near, near_band[0]))

    @pl.when(worker)
    def _():
        hidden[0:ahead] = jnp.zeros((ahead, *hidden.shape[1:]), hidden.dtype)
        partial[...] = jnp.zeros_like(partial)

        @pl.when(band == 0)
        def _():
            row_in[:, 0] = jnp.zeros((groups, *row_in.shape[2:]), row_in.dtype)
            corner_in[:, :, 0] = jnp.zeros((groups, 2, *corner_in.shape[3:]), corner_in.dtype)

        @pl.when(band == bands - 1)
        def _():
            row_in[:, 1] = jnp.zeros((groups, *row_in.shape[2:]), row_in.dtype)
            corner_in[:, :, 1] = jnp.zeros((groups, 2, *corner_in.shape[3:]), corner_in.dtype)

        @pl.when(section > 0)
        def _():
            edge_in[:, :, 1] = jnp.zeros((groups, 2, *edge_in.shape[3:]), edge_in.dtype)

        @pl.when(tile == 0)
        def _():
            edge_in[:, 0] = jnp.zeros((groups, *edge_in.shape[2:]), edge_in.dtype)
            corner_in[:, 0] = jnp.zeros((groups, *corner_in.shape[2:]), corner_in.dtype)

        @pl.when(tile == TILES - 1)
        def _():
            edge_in[:, 1] = jnp.zeros((groups, *edge_in.shape[2:]), edge_in.dtype)
            corner_in[:, 1] = jnp.zeros((groups, *corner_in.shape[2:]), corner_in.dtype)

    left_edges = [(0, at, at * wide - 1) for at in range(1, TILES)]
    right_edges = [(1, at, at * wide + wide) for at in range(TILES - 1)]
    clip_edges = left_edges + right_edges

    @pl.when(sender)
    def _():
        load_clip.wait()
        for n in range(channels // LANES):
            clip_wide[n] = clip_in[:, :, :, n * LANES:(n + 1) * LANES].reshape(-1, LANES).astype(jnp.float32)
        for n, (_, _, column) in enumerate(clip_edges):
            parts = []
            for lane in range(channels // LANES):
                part = clip_wide[lane, pl.ds(column, frames * pair, stride=columns), :]
                parts += [part, part]
            clip_edge[n] = jnp.concatenate(parts, axis=0).astype(jnp.bfloat16)
            for lane in range(channels // LANES):
                for row in range(pair):
                    @pl.when(half == row)
                    def _(n=n, column=column, lane=lane, row=row):
                        clip_corner[n, lane * frames:(lane + 1) * frames] = (
                            clip_wide[lane, pl.ds(row * columns + column, frames, stride=pair * columns), :]
                        )

    def one_if(condition):
        return jnp.where(condition, 1, 0)

    near_tiles = 1 + one_if(tile > 0) + one_if(tile < TILES - 1)
    near_bands = 1 + one_if(band > 0) + one_if(band < bands - 1)
    receivers = (
        one_if(sender) * TILES * (1 + one_if(has_beside))
        + one_if(worker) * (2 * groups - 1 + one_if(section < sections - 1) * near_tiles * near_bands)
    )

    @pl.when(receivers > 0)
    def _():
        pl.semaphore_wait(barrier, receivers)

    def clip_copies():
        copies = []

        def add(condition, source, target, arrived, at_tile, at_space):
            copies.append((condition, pltpu.make_async_remote_copy(
                src_ref=source,
                dst_ref=target,
                send_sem=clip_send.at[len(copies)],
                recv_sem=arrived,
                device_id=in_band(0, at_tile, at_space),
                device_id_type=MESH,
            )))

        for n, (side, at, _) in enumerate(clip_edges):
            add(has_beside, clip_corner.at[n], corner_in.at[tm, side, 1 - half], corner_sem.at[tm, side, 1 - half],
                at, beside_space)
        for at in range(TILES):
            add(has_beside, clip.at[:, half, at * wide:(at + 1) * wide], row_in.at[tm, 1 - half],
                row_sem.at[tm, 1 - half], at, beside_space)
        for n, (side, at, _) in enumerate(clip_edges):
            add(None, clip_edge.at[n], edge_in.at[tm, side, half], edge_sem.at[tm, side, half], at, near_band[0])
        for at in range(TILES):
            add(None, clip.at[:, :, at * wide:(at + 1) * wide], own_in.at[tm, :, pl.ds(pair * half, pair)],
                own_sem.at[tm, half], at, near_band[0])
        return copies

    @pl.when(sender)
    def _():
        for condition, copy in clip_copies():
            when(condition, copy.start)

    def next_copies(group):
        copies = []
        for n, (t, b) in enumerate(steps):
            if t and b:
                side, above = (1 if t < 0 else 0), (1 if b < 0 else 0)
                source = corner_out.at[group, 1 - side, 1 - above]
                target, arrived = corner_in.at[group, side, above], corner_sem.at[group, side, above]
            elif t:
                side = 1 if t < 0 else 0
                source = edge_out.at[group, 1 - side]
                target, arrived = edge_in.at[group, side, 0], edge_sem.at[group, side, 0]
            elif b:
                source = tile_out.at[group, :, 0 if b < 0 else TALL - 1]
                above = 1 if b < 0 else 0
                target, arrived = row_in.at[group, above], row_sem.at[group, above]
            else:
                source, target, arrived = tile_out.at[group], own_in.at[group], own_sem.at[group, 0]
            copies.append((inside(t, b), pltpu.make_async_remote_copy(
                src_ref=source,
                dst_ref=target,
                send_sem=next_send.at[group, n],
                recv_sem=arrived,
                device_id=neighbour(next_section, t, b),
                device_id_type=MESH,
            )))
        return copies

    def home_target():
        return out.at[0, :, :, pl.ds(pl.multiple_of(tile * wide, wide), wide)]

    def home_copy(group, near):
        return pltpu.make_async_remote_copy(
            src_ref=tile_out.at[group, :, near * pair:(near + 1) * pair],
            dst_ref=home_target(),
            send_sem=home_send.at[group, near],
            recv_sem=home_sem.at[tile],
            device_id=(section, group, 2 * band + near),
            device_id_type=MESH,
        )

    def own_copy(group, near):
        source = tile_out.at[group, :, near * pair:(near + 1) * pair]
        return pltpu.make_async_copy(source, home_target(), home_sem.at[tile])

    def arrived(ref, sem):
        pltpu.make_async_copy(ref, ref, sem).wait()

    def activated(value):
        factor = lax.rsqrt(jnp.mean(value * value, axis=-1, keepdims=True) + 1e-06)
        value = value * factor * gain[...]
        value = 0.5 * value
        return value + value * jnp.tanh(value)

    def taps(frame, time_tap):
        summed = jnp.zeros((cells, channels), jnp.float32)
        for row_tap in range(TAPS):
            window = hidden[pl.ds(frame, frames), row_tap:row_tap + TALL]
            summed = summed + jnp.dot(
                window.reshape(cells, TAPS * channels),
                filters[TAPS * time_tap + row_tap],
                preferred_element_type=jnp.float32,
            )
        return summed

    def process(group, carry):
        first = group * frames

        for side, t in ((0, -1), (1, 1)):
            for above, b in ((0, -1), (1, 1)):
                when(inside(t, b), lambda side=side, above=above: arrived(
                    corner_in.at[group, side, above], corner_sem.at[group, side, above]))
            when(inside(t, 0), lambda side=side: arrived(edge_in.at[group, side, 0], edge_sem.at[group, side, 0]))

            @pl.when((section == 0) & inside(t, 0))
            def _(side=side):
                arrived(edge_in.at[group, side, 1], edge_sem.at[group, side, 1])

        for above, b in ((0, -1), (1, 1)):
            when(inside(0, b), lambda above=above: arrived(row_in.at[group, above], row_sem.at[group, above]))

        @pl.when(section == 0)
        def _():
            for near in range(2):
                arrived(own_in.at[group, :, near * pair:(near + 1) * pair], own_sem.at[group, near])

        @pl.when(section > 0)
        def _():
            arrived(own_in.at[group], own_sem.at[group, 0])

        lower = lax.broadcasted_iota(jnp.int32, (edge_cells, channels), 0) >= edge_cells // 2
        stored = edge_cells + 2 * frames
        for side in range(2):
            upper, under = (
                jnp.concatenate(
                    [edge_in[group, side, p][n * edge_cells:(n + 1) * edge_cells].astype(jnp.float32)
                     for n in range(channels // LANES)],
                    axis=1,
                )
                for p in range(2)
            )
            raw[pl.ds(side * stored, edge_cells), :] = jnp.where(lower & (section == 0), under, upper)
            for above in range(2):
                at = side * stored + edge_cells + above * frames
                for n in range(channels // LANES):
                    raw[pl.ds(at, frames), n * LANES:(n + 1) * LANES] = (
                        corner_in[group, side, above, n * frames:(n + 1) * frames]
                    )
        halo[...] = activated(raw[...])

        own = own_in[group].reshape(cells, channels).astype(jnp.float32)
        middle = activated(own).reshape(frames, TALL, wide, channels)
        outer = activated(row_in[group].reshape(2 * frames * wide, channels).astype(jnp.float32))
        outer = outer.reshape(2, frames, wide, channels)
        column = lax.broadcasted_iota(jnp.int32, (wide, channels), 0)
        for frame in range(frames):
            for row in range(TALL + 2):
                if row == 0:
                    here, at = outer[0, frame], edge_cells + frame
                elif row == TALL + 1:
                    here, at = outer[1, frame], edge_cells + frames + frame
                else:
                    part, within = divmod(row - 1, pair)
                    here = middle[frame, row - 1]
                    at = part * (edge_cells // 2) + pair * frame + within
                left = jnp.where(column == 0, halo[pl.ds(at, 1), :], pltpu.roll(here, 1, 0))
                at += stored
                right = jnp.where(column == wide - 1, halo[pl.ds(at, 1), :], pltpu.roll(here, wide - 1, 0))
                for part, shifted in enumerate((left, here, right)):
                    hidden[first + ahead + frame, row, :, part * channels:(part + 1) * channels] = (
                        shifted.astype(jnp.bfloat16)
                    )

        @pl.when(group == 0)
        def _():
            load_filters.wait()

        summed = partial[...]
        for time_tap in range(1, TAPS):
            summed = summed + taps(first + time_tap, time_tap)
        result = own + summed
        tile_out[group] = result.astype(jnp.bfloat16).reshape(frames, TALL, wide, channels)

        @pl.when(section < sections - 1)
        def _():
            block = pair * wide
            for frame in range(frames):
                for part in range(TALL // pair):
                    source = (frame * (TALL // pair) + part) * block
                    for n in range(channels // LANES):
                        wide_out[n, pl.ds((part * frames + frame) * block, block), :] = (
                            result[source:source + block, n * LANES:(n + 1) * LANES]
                        )
            for side, at in enumerate((0, wide - 1)):
                parts = [
                    wide_out[n, pl.ds(at, edge_cells, stride=wide), :]
                    for n in range(channels // LANES)
                ]
                edge_out[group, side] = jnp.concatenate(parts, axis=0).astype(jnp.bfloat16)
                for above, start in enumerate((0, frames * block + (pair - 1) * wide)):
                    for lane in range(channels // LANES):
                        corner_out[group, side, above, lane * frames:(lane + 1) * frames] = (
                            wide_out[lane, pl.ds(start + at, frames, stride=block), :]
                            .astype(jnp.bfloat16).astype(jnp.float32)
                        )
            for condition, copy in next_copies(group):
                when(condition, copy.start)

        for near in range(2):
            own_home = (group == tm) & (near == half)

            @pl.when(own_home)
            def _(near=near):
                own_copy(group, near).start()

            @pl.when(jnp.logical_not(own_home))
            def _(near=near):
                home_copy(group, near).start()

        @pl.when(group < groups - 1)
        def _():
            partial[...] = taps(first + frames, 0)

        return carry

    @pl.when(worker)
    def _():
        load_gain.wait()
        lax.fori_loop(0, groups, process, 0)

    for at in range(TILES):
        arrived(out.at[0, :, :, at * wide:(at + 1) * wide], home_sem.at[at])

    @pl.when(sender)
    def _():
        for condition, copy in clip_copies():
            when(condition, copy.wait_send)

    def drain(group, carry):
        @pl.when(section < sections - 1)
        def _():
            for condition, copy in next_copies(group):
                when(condition, copy.wait_send)

        for near in range(2):
            @pl.when(jnp.logical_not((group == tm) & (near == half)))
            def _(near=near):
                home_copy(group, near).wait_send()

        return carry

    @pl.when(worker)
    def _():
        lax.fori_loop(0, groups, drain, 0)


def on_device(clip_features, conv_kernels, norm_gains):
    frames, pair, columns, channels = clip_features.shape
    groups = lax.axis_size("tm")
    wide = columns // TILES
    edge_cells = frames * TALL
    edge = (edge_cells * channels // LANES, LANES)
    corner = (frames * channels // LANES, LANES)
    edges = 2 * (TILES - 1)
    in_hbm = pl.BlockSpec(memory_space=pltpu.HBM)
    return pl.pallas_call(
        chain_kernel,
        out_shape=jax.ShapeDtypeStruct((1, frames, pair, columns, channels), jnp.bfloat16),
        in_specs=[in_hbm] * 3,
        out_specs=in_hbm,
        scratch_shapes=[
            pltpu.VMEM((groups, frames, TALL, wide, channels), jnp.bfloat16),
            pltpu.VMEM((groups, 2, frames, wide, channels), jnp.bfloat16),
            pltpu.VMEM((groups, 2, 2, *edge), jnp.bfloat16),
            pltpu.VMEM((groups, 2, 2, *corner), jnp.float32),
            pltpu.VMEM((TAPS - 1 + groups * frames, TALL + 2, wide, TAPS * channels), jnp.bfloat16),
            pltpu.VMEM((frames * TALL * wide, channels), jnp.float32),
            pltpu.VMEM((2 * (edge_cells + 2 * frames), channels), jnp.float32),
            pltpu.VMEM((2 * (edge_cells + 2 * frames), channels), jnp.float32),
            pltpu.VMEM(conv_kernels.shape[1:], jnp.bfloat16),
            pltpu.VMEM(norm_gains.shape, jnp.float32),
            pltpu.VMEM((channels // LANES, frames * TALL * wide, LANES), jnp.float32),
            pltpu.VMEM((groups, frames, TALL, wide, channels), jnp.bfloat16),
            pltpu.VMEM((groups, 2, *edge), jnp.bfloat16),
            pltpu.VMEM((groups, 2, 2, *corner), jnp.float32),
            pltpu.VMEM((frames, pair, columns, channels), jnp.bfloat16),
            pltpu.VMEM((channels // LANES, frames * pair * columns, LANES), jnp.float32),
            pltpu.VMEM((edges, *edge), jnp.bfloat16),
            pltpu.VMEM((edges, *corner), jnp.float32),
            pltpu.SemaphoreType.DMA((groups, 2)),
            pltpu.SemaphoreType.DMA((groups, 2)),
            pltpu.SemaphoreType.DMA((groups, 2, 2)),
            pltpu.SemaphoreType.DMA((groups, 2, 2)),
            pltpu.SemaphoreType.DMA((TILES,)),
            pltpu.SemaphoreType.DMA((2 * edges + 2 * TILES,)),
            pltpu.SemaphoreType.DMA((groups, 9)),
            pltpu.SemaphoreType.DMA((groups, 2)),
            pltpu.SemaphoreType.DMA((3,)),
        ],
        compiler_params=pltpu.CompilerParams(
            collective_id=0, has_side_effects=True, vmem_limit_bytes=55040 * 2**10
        ),
        name="chain",
    )(clip_features, conv_kernels, norm_gains)


def solution(mesh):
    return jax.shard_map(
        on_device,
        mesh=mesh,
        in_specs=(P("tm", "space", None, None), P("section", None, None, None), P("section", None)),
        out_specs=P("section", "tm", "space", None, None),
        check_vma=False,
    )
```

```python
import jax
import jax.numpy as jnp
from jax import lax
from jax.experimental import pallas as pl
from jax.experimental.pallas import tpu as pltpu
from jax.sharding import PartitionSpec as P

MESH = pl.DeviceIdType.MESH
WORKER = 1
TAPS = 3
TALL = 4
TILES = 4
LANES = 128


def chain_kernel(
    clip, weights, gains, out,
    own_in, row_in, edge_in, corner_in, hidden, partial, raw, halo, filters, gain, wide_out, tile_out, edge_out,
    corner_out, clip_in, clip_wide, clip_edge, clip_corner,
    own_sem, row_sem, edge_sem, corner_sem, home_sem, clip_send, next_send, home_send, load_sem,
):
    section = lax.axis_index("section")
    tm = lax.axis_index("tm")
    space = lax.axis_index("space")
    sections = lax.axis_size("section")
    groups = lax.axis_size("tm")
    bands = lax.axis_size("space") // 2
    band = space // 2
    half = space % 2
    run = tm // 2
    tile = 2 * half + run
    worker = tm % 2 == WORKER
    sender = section == jnp.where((tm == 0) & (space == 0), 1, tm % sections)
    frames, pair, columns, channels = clip.shape
    wide = columns // TILES
    cells = frames * TALL * wide
    edge_cells = frames * TALL
    ahead = TAPS - 1
    beside = band + 2 * half - 1
    has_beside = (beside >= 0) & (beside < bands)

    near_tm = {0: 2 * run + WORKER, 1: 2 * (1 - run) + WORKER, -1: 2 * (1 - run) + WORKER}
    near_half = {0: half, 1: jnp.minimum(half + run, 1), -1: jnp.maximum(half + run - 1, 0)}
    near_band = {0: 2 * band, 1: 2 * jnp.minimum(band + 1, bands - 1), -1: 2 * jnp.maximum(band - 1, 0)}
    near_space = {(t, b): near_band[b] + near_half[t] for t in (-1, 0, 1) for b in (-1, 0, 1)}
    next_section = jnp.minimum(section + 1, sections - 1)
    previous_section = jnp.maximum(section - 1, 0)
    beside_space = 2 * jnp.clip(beside, 0, bands - 1)

    def neighbour(at_section, t, b):
        return (at_section, near_tm[t], near_space[t, b])

    def in_band(at_section, at_tile, at_space):
        return (at_section, 2 * (at_tile % 2) + WORKER, at_space + at_tile // 2)

    def inside(step_tile, step_band):
        there = None
        for at, step, end in ((tile, step_tile, TILES), (band, step_band, bands)):
            if step:
                here = (at > 0) if step < 0 else (at < end - 1)
                there = here if there is None else there & here
        return there

    def when(condition, action):
        if condition is None:
            action()
        else:
            pl.when(condition)(action)

    barrier = pltpu.get_barrier_semaphore()

    def greet(device):
        pl.semaphore_signal(barrier, inc=1, device_id=device, device_id_type=MESH)

    @pl.when(worker & (section == 0))
    def _():
        for group in range(groups):
            for near in range(2):
                source = jnp.where(band == 0, 1, 0) if group + near == 0 else group % sections
                greet((source, group, 2 * band + near))

        @pl.when(band > 0)
        def _():
            for group in range(groups):
                greet((group % sections, group, jnp.maximum(2 * band - 1, 0)))

        @pl.when(band < bands - 1)
        def _():
            for group in range(groups):
                greet((group % sections, group, jnp.minimum(2 * band + 2, 2 * bands - 1)))

    load_filters = pltpu.make_async_copy(weights.at[0], filters, load_sem.at[0])
    load_gain = pltpu.make_async_copy(gains, gain, load_sem.at[1])
    load_clip = pltpu.make_async_copy(clip, clip_in, load_sem.at[2])

    @pl.when(sender)
    def _():
        load_clip.start()

    @pl.when(worker)
    def _():
        load_gain.start()
        load_filters.start()

    steps = [(t, b) for t in (-1, 1, 0) for b in (-1, 1, 0)]

    @pl.when(worker & (section > 0))
    def _():
        for t, b in steps:
            when(inside(t, b), lambda t=t, b=b: greet(neighbour(previous_section, t, b)))

    for near in range(TILES):
        @pl.when(jnp.logical_not(worker & (tile == near)))
        def _(near=near):
            greet(in_band(section, near, near_band[0]))

    @pl.when(worker)
    def _():
        hidden[0:ahead] = jnp.zeros((ahead, *hidden.shape[1:]), hidden.dtype)
        partial[...] = jnp.zeros_like(partial)

        @pl.when(band == 0)
        def _():
            row_in[:, 0] = jnp.zeros((groups, *row_in.shape[2:]), row_in.dtype)
            corner_in[:, :, 0] = jnp.zeros((groups, 2, *corner_in.shape[3:]), corner_in.dtype)

        @pl.when(band == bands - 1)
        def _():
            row_in[:, 1] = jnp.zeros((groups, *row_in.shape[2:]), row_in.dtype)
            corner_in[:, :, 1] = jnp.zeros((groups, 2, *corner_in.shape[3:]), corner_in.dtype)

        @pl.when(section > 0)
        def _():
            edge_in[:, :, 1] = jnp.zeros((groups, 2, *edge_in.shape[3:]), edge_in.dtype)

        @pl.when(tile == 0)
        def _():
            edge_in[:, 0] = jnp.zeros((groups, *edge_in.shape[2:]), edge_in.dtype)
            corner_in[:, 0] = jnp.zeros((groups, *corner_in.shape[2:]), corner_in.dtype)

        @pl.when(tile == TILES - 1)
        def _():
            edge_in[:, 1] = jnp.zeros((groups, *edge_in.shape[2:]), edge_in.dtype)
            corner_in[:, 1] = jnp.zeros((groups, *corner_in.shape[2:]), corner_in.dtype)

    left_edges = [(0, at, at * wide - 1) for at in range(1, TILES)]
    right_edges = [(1, at, at * wide + wide) for at in range(TILES - 1)]
    clip_edges = left_edges + right_edges

    @pl.when(sender)
    def _():
        load_clip.wait()
        for n in range(channels // LANES):
            clip_wide[n] = clip_in[:, :, :, n * LANES:(n + 1) * LANES].reshape(-1, LANES).astype(jnp.float32)
        for n, (_, _, column) in enumerate(clip_edges):
            parts = []
            for lane in range(channels // LANES):
                part = clip_wide[lane, pl.ds(column, frames * pair, stride=columns), :]
                parts += [part, part]
            clip_edge[n] = jnp.concatenate(parts, axis=0).astype(jnp.bfloat16)
            for lane in range(channels // LANES):
                for row in range(pair):
                    @pl.when(half == row)
                    def _(n=n, column=column, lane=lane, row=row):
                        clip_corner[n, lane * frames:(lane + 1) * frames] = (
                            clip_wide[lane, pl.ds(row * columns + column, frames, stride=pair * columns), :]
                        )

    def one_if(condition):
        return jnp.where(condition, 1, 0)

    near_tiles = 1 + one_if(tile > 0) + one_if(tile < TILES - 1)
    near_bands = 1 + one_if(band > 0) + one_if(band < bands - 1)
    receivers = (
        one_if(sender) * TILES * (1 + one_if(has_beside))
        + one_if(worker) * (2 * groups - 1 + one_if(section < sections - 1) * near_tiles * near_bands)
    )

    @pl.when(receivers > 0)
    def _():
        pl.semaphore_wait(barrier, receivers)

    def clip_copies():
        copies = []

        def add(condition, source, target, arrived, at_tile, at_space):
            copies.append((condition, pltpu.make_async_remote_copy(
                src_ref=source,
                dst_ref=target,
                send_sem=clip_send.at[len(copies)],
                recv_sem=arrived,
                device_id=in_band(0, at_tile, at_space),
                device_id_type=MESH,
            )))

        for n, (side, at, _) in enumerate(clip_edges):
            add(has_beside, clip_corner.at[n], corner_in.at[tm, side, 1 - half], corner_sem.at[tm, side, 1 - half],
                at, beside_space)
        for at in range(TILES):
            add(has_beside, clip.at[:, half, at * wide:(at + 1) * wide], row_in.at[tm, 1 - half],
                row_sem.at[tm, 1 - half], at, beside_space)
        for n, (side, at, _) in enumerate(clip_edges):
            add(None, clip_edge.at[n], edge_in.at[tm, side, half], edge_sem.at[tm, side, half], at, near_band[0])
        for at in range(TILES):
            add(None, clip.at[:, :, at * wide:(at + 1) * wide], own_in.at[tm, :, pl.ds(pair * half, pair)],
                own_sem.at[tm, half], at, near_band[0])
        return copies

    @pl.when(sender)
    def _():
        for condition, copy in clip_copies():
            when(condition, copy.start)

    def next_copies(group):
        copies = []
        for n, (t, b) in enumerate(steps):
            if t and b:
                side, above = (1 if t < 0 else 0), (1 if b < 0 else 0)
                source = corner_out.at[group, 1 - side, 1 - above]
                target, arrived = corner_in.at[group, side, above], corner_sem.at[group, side, above]
            elif t:
                side = 1 if t < 0 else 0
                source = edge_out.at[group, 1 - side]
                target, arrived = edge_in.at[group, side, 0], edge_sem.at[group, side, 0]
            elif b:
                source = tile_out.at[group, :, 0 if b < 0 else TALL - 1]
                above = 1 if b < 0 else 0
                target, arrived = row_in.at[group, above], row_sem.at[group, above]
            else:
                source, target, arrived = tile_out.at[group], own_in.at[group], own_sem.at[group, 0]
            copies.append((inside(t, b), pltpu.make_async_remote_copy(
                src_ref=source,
                dst_ref=target,
                send_sem=next_send.at[group, n],
                recv_sem=arrived,
                device_id=neighbour(next_section, t, b),
                device_id_type=MESH,
            )))
        return copies

    def home_target():
        return out.at[0, :, :, pl.ds(pl.multiple_of(tile * wide, wide), wide)]

    def home_copy(group, near):
        return pltpu.make_async_remote_copy(
            src_ref=tile_out.at[group, :, near * pair:(near + 1) * pair],
            dst_ref=home_target(),
            send_sem=home_send.at[group, near],
            recv_sem=home_sem.at[tile],
            device_id=(section, group, 2 * band + near),
            device_id_type=MESH,
        )

    def own_copy(group, near):
        source = tile_out.at[group, :, near * pair:(near + 1) * pair]
        return pltpu.make_async_copy(source, home_target(), home_sem.at[tile])

    def arrived(ref, sem):
        pltpu.make_async_copy(ref, ref, sem).wait()

    def activated(value):
        factor = lax.rsqrt(jnp.mean(value * value, axis=-1, keepdims=True) + 1e-06)
        value = value * factor * gain[...]
        value = 0.5 * value
        return value + value * jnp.tanh(value)

    def taps(frame, time_tap):
        summed = jnp.zeros((cells, channels), jnp.float32)
        for row_tap in range(TAPS):
            window = hidden[pl.ds(frame, frames), row_tap:row_tap + TALL]
            summed = summed + jnp.dot(
                window.reshape(cells, TAPS * channels),
                filters[TAPS * time_tap + row_tap],
                preferred_element_type=jnp.float32,
            )
        return summed

    def process(group, carry):
        first = group * frames

        for side, t in ((0, -1), (1, 1)):
            for above, b in ((0, -1), (1, 1)):
                when(inside(t, b), lambda side=side, above=above: arrived(
                    corner_in.at[group, side, above], corner_sem.at[group, side, above]))
            when(inside(t, 0), lambda side=side: arrived(edge_in.at[group, side, 0], edge_sem.at[group, side, 0]))

            @pl.when((section == 0) & inside(t, 0))
            def _(side=side):
                arrived(edge_in.at[group, side, 1], edge_sem.at[group, side, 1])

        for above, b in ((0, -1), (1, 1)):
            when(inside(0, b), lambda above=above: arrived(row_in.at[group, above], row_sem.at[group, above]))

        @pl.when(section == 0)
        def _():
            for near in range(2):
                arrived(own_in.at[group, :, near * pair:(near + 1) * pair], own_sem.at[group, near])

        @pl.when(section > 0)
        def _():
            arrived(own_in.at[group], own_sem.at[group, 0])

        lower = lax.broadcasted_iota(jnp.int32, (edge_cells, channels), 0) >= edge_cells // 2
        stored = edge_cells + 2 * frames
        for side in range(2):
            upper, under = (
                jnp.concatenate(
                    [edge_in[group, side, p][n * edge_cells:(n + 1) * edge_cells].astype(jnp.float32)
                     for n in range(channels // LANES)],
                    axis=1,
                )
                for p in range(2)
            )
            raw[pl.ds(side * stored, edge_cells), :] = jnp.where(lower & (section == 0), under, upper)
            for above in range(2):
                at = side * stored + edge_cells + above * frames
                for n in range(channels // LANES):
                    raw[pl.ds(at, frames), n * LANES:(n + 1) * LANES] = (
                        corner_in[group, side, above, n * frames:(n + 1) * frames]
                    )
        halo[...] = activated(raw[...])

        own = own_in[group].reshape(cells, channels).astype(jnp.float32)
        middle = activated(own).reshape(frames, TALL, wide, channels)
        outer = activated(row_in[group].reshape(2 * frames * wide, channels).astype(jnp.float32))
        outer = outer.reshape(2, frames, wide, channels)
        column = lax.broadcasted_iota(jnp.int32, (wide, channels), 0)
        for frame in range(frames):
            for row in range(TALL + 2):
                if row == 0:
                    here, at = outer[0, frame], edge_cells + frame
                elif row == TALL + 1:
                    here, at = outer[1, frame], edge_cells + frames + frame
                else:
                    part, within = divmod(row - 1, pair)
                    here = middle[frame, row - 1]
                    at = part * (edge_cells // 2) + pair * frame + within
                left = jnp.where(column == 0, halo[pl.ds(at, 1), :], pltpu.roll(here, 1, 0))
                at += stored
                right = jnp.where(column == wide - 1, halo[pl.ds(at, 1), :], pltpu.roll(here, wide - 1, 0))
                for part, shifted in enumerate((left, here, right)):
                    hidden[first + ahead + frame, row, :, part * channels:(part + 1) * channels] = (
                        shifted.astype(jnp.bfloat16)
                    )

        @pl.when(group == 0)
        def _():
            load_filters.wait()

        summed = partial[...]
        for time_tap in range(1, TAPS):
            summed = summed + taps(first + time_tap, time_tap)
        result = own + summed
        tile_out[group] = result.astype(jnp.bfloat16).reshape(frames, TALL, wide, channels)

        @pl.when(section < sections - 1)
        def _():
            block = pair * wide
            for frame in range(frames):
                for part in range(TALL // pair):
                    source = (frame * (TALL // pair) + part) * block
                    for n in range(channels // LANES):
                        wide_out[n, pl.ds((part * frames + frame) * block, block), :] = (
                            result[source:source + block, n * LANES:(n + 1) * LANES]
                        )
            for side, at in enumerate((0, wide - 1)):
                parts = [
                    wide_out[n, pl.ds(at, edge_cells, stride=wide), :]
                    for n in range(channels // LANES)
                ]
                edge_out[group, side] = jnp.concatenate(parts, axis=0).astype(jnp.bfloat16)
                for above, start in enumerate((0, frames * block + (pair - 1) * wide)):
                    for lane in range(channels // LANES):
                        corner_out[group, side, above, lane * frames:(lane + 1) * frames] = (
                            wide_out[lane, pl.ds(start + at, frames, stride=block), :]
                            .astype(jnp.bfloat16).astype(jnp.float32)
                        )
            for condition, copy in next_copies(group):
                when(condition, copy.start)

        for near in range(2):
            own_home = (group == tm) & (near == half)

            @pl.when(own_home)
            def _(near=near):
                own_copy(group, near).start()

            @pl.when(jnp.logical_not(own_home))
            def _(near=near):
                home_copy(group, near).start()

        @pl.when(group < groups - 1)
        def _():
            partial[...] = taps(first + frames, 0)

        return carry

    @pl.when(worker)
    def _():
        load_gain.wait()
        lax.fori_loop(0, groups, process, 0)

    for at in range(TILES):
        arrived(out.at[0, :, :, at * wide:(at + 1) * wide], home_sem.at[at])

    @pl.when(sender)
    def _():
        for condition, copy in clip_copies():
            when(condition, copy.wait_send)

    def drain(group, carry):
        @pl.when(section < sections - 1)
        def _():
            for condition, copy in next_copies(group):
                when(condition, copy.wait_send)

        for near in range(2):
            @pl.when(jnp.logical_not((group == tm) & (near == half)))
            def _(near=near):
                home_copy(group, near).wait_send()

        return carry

    @pl.when(worker)
    def _():
        lax.fori_loop(0, groups, drain, 0)


def on_device(clip_features, conv_kernels, norm_gains):
    frames, pair, columns, channels = clip_features.shape
    groups = lax.axis_size("tm")
    wide = columns // TILES
    edge_cells = frames * TALL
    edge = (edge_cells * channels // LANES, LANES)
    corner = (frames * channels // LANES, LANES)
    edges = 2 * (TILES - 1)
    in_hbm = pl.BlockSpec(memory_space=pltpu.HBM)
    return pl.pallas_call(
        chain_kernel,
        out_shape=jax.ShapeDtypeStruct((1, frames, pair, columns, channels), jnp.bfloat16),
        in_specs=[in_hbm] * 3,
        out_specs=in_hbm,
        scratch_shapes=[
            pltpu.VMEM((groups, frames, TALL, wide, channels), jnp.bfloat16),
            pltpu.VMEM((groups, 2, frames, wide, channels), jnp.bfloat16),
            pltpu.VMEM((groups, 2, 2, *edge), jnp.bfloat16),
            pltpu.VMEM((groups, 2, 2, *corner), jnp.float32),
            pltpu.VMEM((TAPS - 1 + groups * frames, TALL + 2, wide, TAPS * channels), jnp.bfloat16),
            pltpu.VMEM((frames * TALL * wide, channels), jnp.float32),
            pltpu.VMEM((2 * (edge_cells + 2 * frames), channels), jnp.float32),
            pltpu.VMEM((2 * (edge_cells + 2 * frames), channels), jnp.float32),
            pltpu.VMEM(conv_kernels.shape[1:], jnp.bfloat16),
            pltpu.VMEM(norm_gains.shape, jnp.float32),
            pltpu.VMEM((channels // LANES, frames * TALL * wide, LANES), jnp.float32),
            pltpu.VMEM((groups, frames, TALL, wide, channels), jnp.bfloat16),
            pltpu.VMEM((groups, 2, *edge), jnp.bfloat16),
            pltpu.VMEM((groups, 2, 2, *corner), jnp.float32),
            pltpu.VMEM((frames, pair, columns, channels), jnp.bfloat16),
            pltpu.VMEM((channels // LANES, frames * pair * columns, LANES), jnp.float32),
            pltpu.VMEM((edges, *edge), jnp.bfloat16),
            pltpu.VMEM((edges, *corner), jnp.float32),
            pltpu.SemaphoreType.DMA((groups, 2)),
            pltpu.SemaphoreType.DMA((groups, 2)),
            pltpu.SemaphoreType.DMA((groups, 2, 2)),
            pltpu.SemaphoreType.DMA((groups, 2, 2)),
            pltpu.SemaphoreType.DMA((TILES,)),
            pltpu.SemaphoreType.DMA((2 * edges + 2 * TILES,)),
            pltpu.SemaphoreType.DMA((groups, 9)),
            pltpu.SemaphoreType.DMA((groups, 2)),
            pltpu.SemaphoreType.DMA((3,)),
        ],
        compiler_params=pltpu.CompilerParams(
            collective_id=0, has_side_effects=True, vmem_limit_bytes=55040 * 2**10
        ),
        name="chain",
    )(clip_features, conv_kernels, norm_gains)


def solution(mesh):
    return jax.shard_map(
        on_device,
        mesh=mesh,
        in_specs=(P("tm", "space", None, None), P("section", None, None, None), P("section", None)),
        out_specs=P("section", "tm", "space", None, None),
        check_vma=False,
    )
```

```python
import jax
import jax.numpy as jnp
from jax import lax
from jax.experimental import pallas as pl
from jax.experimental.pallas import tpu as pltpu
from jax.sharding import PartitionSpec as P

MESH = pl.DeviceIdType.MESH
WORKER = 1
TAPS = 3
TALL = 4
TILES = 4
LANES = 128


def chain_kernel(
    clip, weights, gains, out,
    own_in, row_in, edge_in, corner_in, hidden, partial, raw, halo, filters, gain, wide_out, tile_out, edge_out,
    corner_out, clip_in, clip_wide, clip_edge, clip_corner,
    own_sem, row_sem, edge_sem, corner_sem, home_sem, clip_send, next_send, home_send, load_sem,
):
    section = lax.axis_index("section")
    tm = lax.axis_index("tm")
    space = lax.axis_index("space")
    sections = lax.axis_size("section")
    groups = lax.axis_size("tm")
    bands = lax.axis_size("space") // 2
    band = space // 2
    half = space % 2
    run = tm // 2
    tile = 2 * half + run
    worker = tm % 2 == WORKER
    sender = section == tm % sections
    frames, pair, columns, channels = clip.shape
    wide = columns // TILES
    cells = frames * TALL * wide
    edge_cells = frames * TALL
    ahead = TAPS - 1
    beside = band + 2 * half - 1
    has_beside = (beside >= 0) & (beside < bands)

    near_tm = {0: 2 * run + WORKER, 1: 2 * (1 - run) + WORKER, -1: 2 * (1 - run) + WORKER}
    near_half = {0: half, 1: jnp.minimum(half + run, 1), -1: jnp.maximum(half + run - 1, 0)}
    near_band = {0: 2 * band, 1: 2 * jnp.minimum(band + 1, bands - 1), -1: 2 * jnp.maximum(band - 1, 0)}
    near_space = {(t, b): near_band[b] + near_half[t] for t in (-1, 0, 1) for b in (-1, 0, 1)}
    next_section = jnp.minimum(section + 1, sections - 1)
    previous_section = jnp.maximum(section - 1, 0)
    beside_space = 2 * jnp.clip(beside, 0, bands - 1)

    def neighbour(at_section, t, b):
        return (at_section, near_tm[t], near_space[t, b])

    def in_band(at_section, at_tile, at_space):
        return (at_section, 2 * (at_tile % 2) + WORKER, at_space + at_tile // 2)

    def inside(step_tile, step_band):
        there = None
        for at, step, end in ((tile, step_tile, TILES), (band, step_band, bands)):
            if step:
                here = (at > 0) if step < 0 else (at < end - 1)
                there = here if there is None else there & here
        return there

    def when(condition, action):
        if condition is None:
            action()
        else:
            pl.when(condition)(action)

    barrier = pltpu.get_barrier_semaphore()

    def greet(device):
        pl.semaphore_signal(barrier, inc=1, device_id=device, device_id_type=MESH)

    @pl.when(worker & (section == 0))
    def _():
        for group in range(groups):
            for near in range(2):
                greet((group % sections, group, 2 * band + near))

        @pl.when(band > 0)
        def _():
            for group in range(groups):
                greet((group % sections, group, jnp.maximum(2 * band - 1, 0)))

        @pl.when(band < bands - 1)
        def _():
            for group in range(groups):
                greet((group % sections, group, jnp.minimum(2 * band + 2, 2 * bands - 1)))

    load_filters = pltpu.make_async_copy(weights.at[0], filters, load_sem.at[0])
    load_gain = pltpu.make_async_copy(gains, gain, load_sem.at[1])
    load_clip = pltpu.make_async_copy(clip, clip_in, load_sem.at[2])

    @pl.when(sender)
    def _():
        load_clip.start()

    @pl.when(worker)
    def _():
        load_gain.start()
        load_filters.start()

    steps = [(t, b) for t in (-1, 1, 0) for b in (-1, 1, 0)]

    @pl.when(worker & (section > 0))
    def _():
        for t, b in steps:
            when(inside(t, b), lambda t=t, b=b: greet(neighbour(previous_section, t, b)))

    for near in range(TILES):
        @pl.when(jnp.logical_not(worker & (tile == near)))
        def _(near=near):
            greet(in_band(section, near, near_band[0]))

    @pl.when(worker)
    def _():
        hidden[0:ahead] = jnp.zeros((ahead, *hidden.shape[1:]), hidden.dtype)
        partial[...] = jnp.zeros_like(partial)

        @pl.when(band == 0)
        def _():
            row_in[:, 0] = jnp.zeros((groups, *row_in.shape[2:]), row_in.dtype)
            corner_in[:, :, 0] = jnp.zeros((groups, 2, *corner_in.shape[3:]), corner_in.dtype)

        @pl.when(band == bands - 1)
        def _():
            row_in[:, 1] = jnp.zeros((groups, *row_in.shape[2:]), row_in.dtype)
            corner_in[:, :, 1] = jnp.zeros((groups, 2, *corner_in.shape[3:]), corner_in.dtype)

        @pl.when(section > 0)
        def _():
            edge_in[:, :, 1] = jnp.zeros((groups, 2, *edge_in.shape[3:]), edge_in.dtype)

        @pl.when(tile == 0)
        def _():
            edge_in[:, 0] = jnp.zeros((groups, *edge_in.shape[2:]), edge_in.dtype)
            corner_in[:, 0] = jnp.zeros((groups, *corner_in.shape[2:]), corner_in.dtype)

        @pl.when(tile == TILES - 1)
        def _():
            edge_in[:, 1] = jnp.zeros((groups, *edge_in.shape[2:]), edge_in.dtype)
            corner_in[:, 1] = jnp.zeros((groups, *corner_in.shape[2:]), corner_in.dtype)

    left_edges = [(0, at, at * wide - 1) for at in range(1, TILES)]
    right_edges = [(1, at, at * wide + wide) for at in range(TILES - 1)]
    clip_edges = left_edges + right_edges

    @pl.when(sender)
    def _():
        load_clip.wait()
        for n in range(channels // LANES):
            clip_wide[n] = clip_in[:, :, :, n * LANES:(n + 1) * LANES].reshape(-1, LANES).astype(jnp.float32)
        for n, (_, _, column) in enumerate(clip_edges):
            parts = []
            for lane in range(channels // LANES):
                part = clip_wide[lane, pl.ds(column, frames * pair, stride=columns), :]
                parts += [part, part]
            clip_edge[n] = jnp.concatenate(parts, axis=0).astype(jnp.bfloat16)
            for lane in range(channels // LANES):
                for row in range(pair):
                    @pl.when(half == row)
                    def _(n=n, column=column, lane=lane, row=row):
                        clip_corner[n, lane * frames:(lane + 1) * frames] = (
                            clip_wide[lane, pl.ds(row * columns + column, frames, stride=pair * columns), :]
                        )

    def one_if(condition):
        return jnp.where(condition, 1, 0)

    near_tiles = 1 + one_if(tile > 0) + one_if(tile < TILES - 1)
    near_bands = 1 + one_if(band > 0) + one_if(band < bands - 1)
    receivers = (
        one_if(sender) * TILES * (1 + one_if(has_beside))
        + one_if(worker) * (2 * groups - 1 + one_if(section < sections - 1) * near_tiles * near_bands)
    )

    @pl.when(receivers > 0)
    def _():
        pl.semaphore_wait(barrier, receivers)

    def clip_copies():
        copies = []

        def add(condition, source, target, arrived, at_tile, at_space):
            copies.append((condition, pltpu.make_async_remote_copy(
                src_ref=source,
                dst_ref=target,
                send_sem=clip_send.at[len(copies)],
                recv_sem=arrived,
                device_id=in_band(0, at_tile, at_space),
                device_id_type=MESH,
            )))

        for n, (side, at, _) in enumerate(clip_edges):
            add(has_beside, clip_corner.at[n], corner_in.at[tm, side, 1 - half], corner_sem.at[tm, side, 1 - half],
                at, beside_space)
        for at in range(TILES):
            add(has_beside, clip.at[:, half, at * wide:(at + 1) * wide], row_in.at[tm, 1 - half],
                row_sem.at[tm, 1 - half], at, beside_space)
        for n, (side, at, _) in enumerate(clip_edges):
            add(None, clip_edge.at[n], edge_in.at[tm, side, half], edge_sem.at[tm, side, half], at, near_band[0])
        for at in range(TILES):
            add(None, clip.at[:, :, at * wide:(at + 1) * wide], own_in.at[tm, :, pl.ds(pair * half, pair)],
                own_sem.at[tm, half], at, near_band[0])
        return copies

    @pl.when(sender)
    def _():
        for condition, copy in clip_copies():
            when(condition, copy.start)

    def next_copies(group):
        copies = []
        for n, (t, b) in enumerate(steps):
            if t and b:
                side, above = (1 if t < 0 else 0), (1 if b < 0 else 0)
                source = corner_out.at[group, 1 - side, 1 - above]
                target, arrived = corner_in.at[group, side, above], corner_sem.at[group, side, above]
            elif t:
                side = 1 if t < 0 else 0
                source = edge_out.at[group, 1 - side]
                target, arrived = edge_in.at[group, side, 0], edge_sem.at[group, side, 0]
            elif b:
                source = tile_out.at[group, :, 0 if b < 0 else TALL - 1]
                above = 1 if b < 0 else 0
                target, arrived = row_in.at[group, above], row_sem.at[group, above]
            else:
                source, target, arrived = tile_out.at[group], own_in.at[group], own_sem.at[group, 0]
            copies.append((inside(t, b), pltpu.make_async_remote_copy(
                src_ref=source,
                dst_ref=target,
                send_sem=next_send.at[group, n],
                recv_sem=arrived,
                device_id=neighbour(next_section, t, b),
                device_id_type=MESH,
            )))
        return copies

    def home_target():
        return out.at[0, :, :, pl.ds(pl.multiple_of(tile * wide, wide), wide)]

    def home_copy(group, near):
        return pltpu.make_async_remote_copy(
            src_ref=tile_out.at[group, :, near * pair:(near + 1) * pair],
            dst_ref=home_target(),
            send_sem=home_send.at[group, near],
            recv_sem=home_sem.at[tile],
            device_id=(section, group, 2 * band + near),
            device_id_type=MESH,
        )

    def own_copy(group, near):
        source = tile_out.at[group, :, near * pair:(near + 1) * pair]
        return pltpu.make_async_copy(source, home_target(), home_sem.at[tile])

    def arrived(ref, sem):
        pltpu.make_async_copy(ref, ref, sem).wait()

    def activated(value):
        factor = lax.rsqrt(jnp.mean(value * value, axis=-1, keepdims=True) + 1e-06)
        value = value * factor * gain[...]
        value = 0.5 * value
        return value + value * jnp.tanh(value)

    def taps(frame, time_tap):
        summed = jnp.zeros((cells, channels), jnp.float32)
        for row_tap in range(TAPS):
            window = hidden[pl.ds(frame, frames), row_tap:row_tap + TALL]
            summed = summed + jnp.dot(
                window.reshape(cells, TAPS * channels),
                filters[TAPS * time_tap + row_tap],
                preferred_element_type=jnp.float32,
            )
        return summed

    def send_home(group):
        for near in range(2):
            own_home = (group == tm) & (near == half)

            @pl.when(own_home)
            def _(near=near):
                own_copy(group, near).start()

            @pl.when(jnp.logical_not(own_home))
            def _(near=near):
                home_copy(group, near).start()

    def process(group, carry):
        first = group * frames

        for side, t in ((0, -1), (1, 1)):
            for above, b in ((0, -1), (1, 1)):
                when(inside(t, b), lambda side=side, above=above: arrived(
                    corner_in.at[group, side, above], corner_sem.at[group, side, above]))
            when(inside(t, 0), lambda side=side: arrived(edge_in.at[group, side, 0], edge_sem.at[group, side, 0]))

            @pl.when((section == 0) & inside(t, 0))
            def _(side=side):
                arrived(edge_in.at[group, side, 1], edge_sem.at[group, side, 1])

        for above, b in ((0, -1), (1, 1)):
            when(inside(0, b), lambda above=above: arrived(row_in.at[group, above], row_sem.at[group, above]))

        @pl.when(section == 0)
        def _():
            for near in range(2):
                arrived(own_in.at[group, :, near * pair:(near + 1) * pair], own_sem.at[group, near])

        @pl.when(section > 0)
        def _():
            arrived(own_in.at[group], own_sem.at[group, 0])

        lower = lax.broadcasted_iota(jnp.int32, (edge_cells, channels), 0) >= edge_cells // 2
        stored = edge_cells + 2 * frames
        for side in range(2):
            upper, under = (
                jnp.concatenate(
                    [edge_in[group, side, p][n * edge_cells:(n + 1) * edge_cells].astype(jnp.float32)
                     for n in range(channels // LANES)],
                    axis=1,
                )
                for p in range(2)
            )
            raw[pl.ds(side * stored, edge_cells), :] = jnp.where(lower & (section == 0), under, upper)
            for above in range(2):
                at = side * stored + edge_cells + above * frames
                for n in range(channels // LANES):
                    raw[pl.ds(at, frames), n * LANES:(n + 1) * LANES] = (
                        corner_in[group, side, above, n * frames:(n + 1) * frames]
                    )
        halo[...] = activated(raw[...])

        own = own_in[group].reshape(cells, channels).astype(jnp.float32)
        middle = activated(own).reshape(frames, TALL, wide, channels)
        outer = activated(row_in[group].reshape(2 * frames * wide, channels).astype(jnp.float32))
        outer = outer.reshape(2, frames, wide, channels)
        column = lax.broadcasted_iota(jnp.int32, (wide, channels), 0)
        for frame in range(frames):
            for row in range(TALL + 2):
                if row == 0:
                    here, at = outer[0, frame], edge_cells + frame
                elif row == TALL + 1:
                    here, at = outer[1, frame], edge_cells + frames + frame
                else:
                    part, within = divmod(row - 1, pair)
                    here = middle[frame, row - 1]
                    at = part * (edge_cells // 2) + pair * frame + within
                left = jnp.where(column == 0, halo[pl.ds(at, 1), :], pltpu.roll(here, 1, 0))
                at += stored
                right = jnp.where(column == wide - 1, halo[pl.ds(at, 1), :], pltpu.roll(here, wide - 1, 0))
                for part, shifted in enumerate((left, here, right)):
                    hidden[first + ahead + frame, row, :, part * channels:(part + 1) * channels] = (
                        shifted.astype(jnp.bfloat16)
                    )

        @pl.when(group == 0)
        def _():
            load_filters.wait()

        summed = partial[...]
        for time_tap in range(1, TAPS):
            summed = summed + taps(first + time_tap, time_tap)
        result = own + summed
        tile_out[group] = result.astype(jnp.bfloat16).reshape(frames, TALL, wide, channels)

        @pl.when(section < sections - 1)
        def _():
            block = pair * wide
            for frame in range(frames):
                for part in range(TALL // pair):
                    source = (frame * (TALL // pair) + part) * block
                    for n in range(channels // LANES):
                        wide_out[n, pl.ds((part * frames + frame) * block, block), :] = (
                            result[source:source + block, n * LANES:(n + 1) * LANES]
                        )
            for side, at in enumerate((0, wide - 1)):
                parts = [
                    wide_out[n, pl.ds(at, edge_cells, stride=wide), :]
                    for n in range(channels // LANES)
                ]
                edge_out[group, side] = jnp.concatenate(parts, axis=0).astype(jnp.bfloat16)
                for above, start in enumerate((0, frames * block + (pair - 1) * wide)):
                    for lane in range(channels // LANES):
                        corner_out[group, side, above, lane * frames:(lane + 1) * frames] = (
                            wide_out[lane, pl.ds(start + at, frames, stride=block), :]
                            .astype(jnp.bfloat16).astype(jnp.float32)
                        )
            for condition, copy in next_copies(group):
                when(condition, copy.start)

        @pl.when(section == sections - 1)
        def _():
            send_home(group)

        @pl.when(group < groups - 1)
        def _():
            partial[...] = taps(first + frames, 0)

        return carry

    @pl.when(worker)
    def _():
        load_gain.wait()
        lax.fori_loop(0, groups, process, 0)

        @pl.when(section < sections - 1)
        def _():
            lax.fori_loop(0, groups, lambda group, carry: (send_home(group), carry)[1], 0)

    for at in range(TILES):
        arrived(out.at[0, :, :, at * wide:(at + 1) * wide], home_sem.at[at])

    @pl.when(sender)
    def _():
        for condition, copy in clip_copies():
            when(condition, copy.wait_send)

    def drain(group, carry):
        @pl.when(section < sections - 1)
        def _():
            for condition, copy in next_copies(group):
                when(condition, copy.wait_send)

        for near in range(2):
            @pl.when(jnp.logical_not((group == tm) & (near == half)))
            def _(near=near):
                home_copy(group, near).wait_send()

        return carry

    @pl.when(worker)
    def _():
        lax.fori_loop(0, groups, drain, 0)


def on_device(clip_features, conv_kernels, norm_gains):
    frames, pair, columns, channels = clip_features.shape
    groups = lax.axis_size("tm")
    wide = columns // TILES
    edge_cells = frames * TALL
    edge = (edge_cells * channels // LANES, LANES)
    corner = (frames * channels // LANES, LANES)
    edges = 2 * (TILES - 1)
    in_hbm = pl.BlockSpec(memory_space=pltpu.HBM)
    return pl.pallas_call(
        chain_kernel,
        out_shape=jax.ShapeDtypeStruct((1, frames, pair, columns, channels), jnp.bfloat16),
        in_specs=[in_hbm] * 3,
        out_specs=in_hbm,
        scratch_shapes=[
            pltpu.VMEM((groups, frames, TALL, wide, channels), jnp.bfloat16),
            pltpu.VMEM((groups, 2, frames, wide, channels), jnp.bfloat16),
            pltpu.VMEM((groups, 2, 2, *edge), jnp.bfloat16),
            pltpu.VMEM((groups, 2, 2, *corner), jnp.float32),
            pltpu.VMEM((TAPS - 1 + groups * frames, TALL + 2, wide, TAPS * channels), jnp.bfloat16),
            pltpu.VMEM((frames * TALL * wide, channels), jnp.float32),
            pltpu.VMEM((2 * (edge_cells + 2 * frames), channels), jnp.float32),
            pltpu.VMEM((2 * (edge_cells + 2 * frames), channels), jnp.float32),
            pltpu.VMEM(conv_kernels.shape[1:], jnp.bfloat16),
            pltpu.VMEM(norm_gains.shape, jnp.float32),
            pltpu.VMEM((channels // LANES, frames * TALL * wide, LANES), jnp.float32),
            pltpu.VMEM((groups, frames, TALL, wide, channels), jnp.bfloat16),
            pltpu.VMEM((groups, 2, *edge), jnp.bfloat16),
            pltpu.VMEM((groups, 2, 2, *corner), jnp.float32),
            pltpu.VMEM((frames, pair, columns, channels), jnp.bfloat16),
            pltpu.VMEM((channels // LANES, frames * pair * columns, LANES), jnp.float32),
            pltpu.VMEM((edges, *edge), jnp.bfloat16),
            pltpu.VMEM((edges, *corner), jnp.float32),
            pltpu.SemaphoreType.DMA((groups, 2)),
            pltpu.SemaphoreType.DMA((groups, 2)),
            pltpu.SemaphoreType.DMA((groups, 2, 2)),
            pltpu.SemaphoreType.DMA((groups, 2, 2)),
            pltpu.SemaphoreType.DMA((TILES,)),
            pltpu.SemaphoreType.DMA((2 * edges + 2 * TILES,)),
            pltpu.SemaphoreType.DMA((groups, 9)),
            pltpu.SemaphoreType.DMA((groups, 2)),
            pltpu.SemaphoreType.DMA((3,)),
        ],
        compiler_params=pltpu.CompilerParams(
            collective_id=0, has_side_effects=True, vmem_limit_bytes=55040 * 2**10
        ),
        name="chain",
    )(clip_features, conv_kernels, norm_gains)


def solution(mesh):
    return jax.shard_map(
        on_device,
        mesh=mesh,
        in_specs=(P("tm", "space", None, None), P("section", None, None, None), P("section", None)),
        out_specs=P("section", "tm", "space", None, None),
        check_vma=False,
    )
```

```python
import jax
import jax.numpy as jnp
from jax import lax
from jax.experimental import pallas as pl
from jax.experimental.pallas import tpu as pltpu
from jax.sharding import PartitionSpec as P

MESH = pl.DeviceIdType.MESH
WORKER = 1
TAPS = 3
TALL = 4
TILES = 4
LANES = 128


def chain_kernel(
    clip, weights, gains, out,
    own_in, row_in, edge_in, corner_in, hidden, partial, raw, halo, filters, gain, wide_out, tile_out, edge_out,
    corner_out, clip_in, clip_wide, clip_edge, clip_corner,
    own_sem, row_sem, edge_sem, corner_sem, home_sem, clip_send, next_send, home_send, load_sem,
):
    section = lax.axis_index("section")
    tm = lax.axis_index("tm")
    space = lax.axis_index("space")
    sections = lax.axis_size("section")
    groups = lax.axis_size("tm")
    bands = lax.axis_size("space") // 2
    band = space // 2
    half = space % 2
    run = tm // 2
    tile = 2 * half + run
    worker = tm % 2 == WORKER
    sender = section == tm % sections
    frames, pair, columns, channels = clip.shape
    wide = columns // TILES
    cells = frames * TALL * wide
    edge_cells = frames * TALL
    ahead = TAPS - 1
    beside = band + 2 * half - 1
    has_beside = (beside >= 0) & (beside < bands)

    near_tm = {0: 2 * run + WORKER, 1: 2 * (1 - run) + WORKER, -1: 2 * (1 - run) + WORKER}
    near_half = {0: half, 1: jnp.minimum(half + run, 1), -1: jnp.maximum(half + run - 1, 0)}
    near_band = {0: 2 * band, 1: 2 * jnp.minimum(band + 1, bands - 1), -1: 2 * jnp.maximum(band - 1, 0)}
    near_space = {(t, b): near_band[b] + near_half[t] for t in (-1, 0, 1) for b in (-1, 0, 1)}
    next_section = jnp.minimum(section + 1, sections - 1)
    previous_section = jnp.maximum(section - 1, 0)
    beside_space = 2 * jnp.clip(beside, 0, bands - 1)

    def neighbour(at_section, t, b):
        return (at_section, near_tm[t], near_space[t, b])

    def in_band(at_section, at_tile, at_space):
        return (at_section, 2 * (at_tile % 2) + WORKER, at_space + at_tile // 2)

    def inside(step_tile, step_band):
        there = None
        for at, step, end in ((tile, step_tile, TILES), (band, step_band, bands)):
            if step:
                here = (at > 0) if step < 0 else (at < end - 1)
                there = here if there is None else there & here
        return there

    def when(condition, action):
        if condition is None:
            action()
        else:
            pl.when(condition)(action)

    barrier = pltpu.get_barrier_semaphore()

    def greet(device):
        pl.semaphore_signal(barrier, inc=1, device_id=device, device_id_type=MESH)

    @pl.when(worker & (section == 0))
    def _():
        for group in range(groups):
            for near in range(2):
                greet((group % sections, group, 2 * band + near))

        @pl.when(band > 0)
        def _():
            for group in range(groups):
                greet((group % sections, group, jnp.maximum(2 * band - 1, 0)))

        @pl.when(band < bands - 1)
        def _():
            for group in range(groups):
                greet((group % sections, group, jnp.minimum(2 * band + 2, 2 * bands - 1)))

    load_filters = pltpu.make_async_copy(weights.at[0], filters, load_sem.at[0])
    load_gain = pltpu.make_async_copy(gains, gain, load_sem.at[1])
    load_clip = pltpu.make_async_copy(clip, clip_in, load_sem.at[2])

    @pl.when(sender)
    def _():
        load_clip.start()

    @pl.when(worker)
    def _():
        load_gain.start()
        load_filters.start()

    steps = [(t, b) for b in (-1, 0, 1) for t in (-1, 1, 0)]

    @pl.when(worker & (section > 0))
    def _():
        for t, b in steps:
            when(inside(t, b), lambda t=t, b=b: greet(neighbour(previous_section, t, b)))

    for near in range(TILES):
        @pl.when(jnp.logical_not(worker & (tile == near)))
        def _(near=near):
            greet(in_band(section, near, near_band[0]))

    @pl.when(worker)
    def _():
        hidden[0:ahead] = jnp.zeros((ahead, *hidden.shape[1:]), hidden.dtype)
        partial[...] = jnp.zeros_like(partial)

        @pl.when(band == 0)
        def _():
            row_in[:, 0] = jnp.zeros((groups, *row_in.shape[2:]), row_in.dtype)
            corner_in[:, :, 0] = jnp.zeros((groups, 2, *corner_in.shape[3:]), corner_in.dtype)

        @pl.when(band == bands - 1)
        def _():
            row_in[:, 1] = jnp.zeros((groups, *row_in.shape[2:]), row_in.dtype)
            corner_in[:, :, 1] = jnp.zeros((groups, 2, *corner_in.shape[3:]), corner_in.dtype)

        @pl.when(section > 0)
        def _():
            edge_in[:, :, 1] = jnp.zeros((groups, 2, *edge_in.shape[3:]), edge_in.dtype)

        @pl.when(tile == 0)
        def _():
            edge_in[:, 0] = jnp.zeros((groups, *edge_in.shape[2:]), edge_in.dtype)
            corner_in[:, 0] = jnp.zeros((groups, *corner_in.shape[2:]), corner_in.dtype)

        @pl.when(tile == TILES - 1)
        def _():
            edge_in[:, 1] = jnp.zeros((groups, *edge_in.shape[2:]), edge_in.dtype)
            corner_in[:, 1] = jnp.zeros((groups, *corner_in.shape[2:]), corner_in.dtype)

    left_edges = [(0, at, at * wide - 1) for at in range(1, TILES)]
    right_edges = [(1, at, at * wide + wide) for at in range(TILES - 1)]
    clip_edges = left_edges + right_edges

    @pl.when(sender)
    def _():
        load_clip.wait()
        for n in range(channels // LANES):
            clip_wide[n] = clip_in[:, :, :, n * LANES:(n + 1) * LANES].reshape(-1, LANES).astype(jnp.float32)
        for n, (_, _, column) in enumerate(clip_edges):
            parts = []
            for lane in range(channels // LANES):
                part = clip_wide[lane, pl.ds(column, frames * pair, stride=columns), :]
                parts += [part, part]
            clip_edge[n] = jnp.concatenate(parts, axis=0).astype(jnp.bfloat16)
            for lane in range(channels // LANES):
                for row in range(pair):
                    @pl.when(half == row)
                    def _(n=n, column=column, lane=lane, row=row):
                        clip_corner[n, lane * frames:(lane + 1) * frames] = (
                            clip_wide[lane, pl.ds(row * columns + column, frames, stride=pair * columns), :]
                        )

    def one_if(condition):
        return jnp.where(condition, 1, 0)

    near_tiles = 1 + one_if(tile > 0) + one_if(tile < TILES - 1)
    near_bands = 1 + one_if(band > 0) + one_if(band < bands - 1)
    receivers = (
        one_if(sender) * TILES * (1 + one_if(has_beside))
        + one_if(worker) * (2 * groups - 1 + one_if(section < sections - 1) * near_tiles * near_bands)
    )

    @pl.when(receivers > 0)
    def _():
        pl.semaphore_wait(barrier, receivers)

    def clip_copies():
        copies = []

        def add(condition, source, target, arrived, at_tile, at_space):
            copies.append((condition, pltpu.make_async_remote_copy(
                src_ref=source,
                dst_ref=target,
                send_sem=clip_send.at[len(copies)],
                recv_sem=arrived,
                device_id=in_band(0, at_tile, at_space),
                device_id_type=MESH,
            )))

        for n, (side, at, _) in enumerate(clip_edges):
            add(has_beside, clip_corner.at[n], corner_in.at[tm, side, 1 - half], corner_sem.at[tm, side, 1 - half],
                at, beside_space)
        for at in range(TILES):
            add(has_beside, clip.at[:, half, at * wide:(at + 1) * wide], row_in.at[tm, 1 - half],
                row_sem.at[tm, 1 - half], at, beside_space)
        for n, (side, at, _) in enumerate(clip_edges):
            add(None, clip_edge.at[n], edge_in.at[tm, side, half], edge_sem.at[tm, side, half], at, near_band[0])
        for at in range(TILES):
            add(None, clip.at[:, :, at * wide:(at + 1) * wide], own_in.at[tm, :, pl.ds(pair * half, pair)],
                own_sem.at[tm, half], at, near_band[0])
        return copies

    @pl.when(sender)
    def _():
        for condition, copy in clip_copies():
            when(condition, copy.start)

    def next_copies(group):
        copies = []
        for n, (t, b) in enumerate(steps):
            if t and b:
                side, above = (1 if t < 0 else 0), (1 if b < 0 else 0)
                source = corner_out.at[group, 1 - side, 1 - above]
                target, arrived = corner_in.at[group, side, above], corner_sem.at[group, side, above]
            elif t:
                side = 1 if t < 0 else 0
                source = edge_out.at[group, 1 - side]
                target, arrived = edge_in.at[group, side, 0], edge_sem.at[group, side, 0]
            elif b:
                source = tile_out.at[group, :, 0 if b < 0 else TALL - 1]
                above = 1 if b < 0 else 0
                target, arrived = row_in.at[group, above], row_sem.at[group, above]
            else:
                source, target, arrived = tile_out.at[group], own_in.at[group], own_sem.at[group, 0]
            copies.append((inside(t, b), pltpu.make_async_remote_copy(
                src_ref=source,
                dst_ref=target,
                send_sem=next_send.at[group, n],
                recv_sem=arrived,
                device_id=neighbour(next_section, t, b),
                device_id_type=MESH,
            )))
        return copies

    def home_target():
        return out.at[0, :, :, pl.ds(pl.multiple_of(tile * wide, wide), wide)]

    def home_copy(group, near):
        return pltpu.make_async_remote_copy(
            src_ref=tile_out.at[group, :, near * pair:(near + 1) * pair],
            dst_ref=home_target(),
            send_sem=home_send.at[group, near],
            recv_sem=home_sem.at[tile],
            device_id=(section, group, 2 * band + near),
            device_id_type=MESH,
        )

    def own_copy(group, near):
        source = tile_out.at[group, :, near * pair:(near + 1) * pair]
        return pltpu.make_async_copy(source, home_target(), home_sem.at[tile])

    def arrived(ref, sem):
        pltpu.make_async_copy(ref, ref, sem).wait()

    def activated(value):
        factor = lax.rsqrt(jnp.mean(value * value, axis=-1, keepdims=True) + 1e-06)
        value = value * factor * gain[...]
        value = 0.5 * value
        return value + value * jnp.tanh(value)

    def taps(frame, time_tap):
        summed = jnp.zeros((cells, channels), jnp.float32)
        for row_tap in range(TAPS):
            window = hidden[pl.ds(frame, frames), row_tap:row_tap + TALL]
            summed = summed + jnp.dot(
                window.reshape(cells, TAPS * channels),
                filters[TAPS * time_tap + row_tap],
                preferred_element_type=jnp.float32,
            )
        return summed

    def process(group, carry):
        first = group * frames

        for side, t in ((0, -1), (1, 1)):
            for above, b in ((0, -1), (1, 1)):
                when(inside(t, b), lambda side=side, above=above: arrived(
                    corner_in.at[group, side, above], corner_sem.at[group, side, above]))
            when(inside(t, 0), lambda side=side: arrived(edge_in.at[group, side, 0], edge_sem.at[group, side, 0]))

            @pl.when((section == 0) & inside(t, 0))
            def _(side=side):
                arrived(edge_in.at[group, side, 1], edge_sem.at[group, side, 1])

        for above, b in ((0, -1), (1, 1)):
            when(inside(0, b), lambda above=above: arrived(row_in.at[group, above], row_sem.at[group, above]))

        @pl.when(section == 0)
        def _():
            for near in range(2):
                arrived(own_in.at[group, :, near * pair:(near + 1) * pair], own_sem.at[group, near])

        @pl.when(section > 0)
        def _():
            arrived(own_in.at[group], own_sem.at[group, 0])

        lower = lax.broadcasted_iota(jnp.int32, (edge_cells, channels), 0) >= edge_cells // 2
        stored = edge_cells + 2 * frames
        for side in range(2):
            upper, under = (
                jnp.concatenate(
                    [edge_in[group, side, p][n * edge_cells:(n + 1) * edge_cells].astype(jnp.float32)
                     for n in range(channels // LANES)],
                    axis=1,
                )
                for p in range(2)
            )
            raw[pl.ds(side * stored, edge_cells), :] = jnp.where(lower & (section == 0), under, upper)
            for above in range(2):
                at = side * stored + edge_cells + above * frames
                for n in range(channels // LANES):
                    raw[pl.ds(at, frames), n * LANES:(n + 1) * LANES] = (
                        corner_in[group, side, above, n * frames:(n + 1) * frames]
                    )
        halo[...] = activated(raw[...])

        own = own_in[group].reshape(cells, channels).astype(jnp.float32)
        middle = activated(own).reshape(frames, TALL, wide, channels)
        outer = activated(row_in[group].reshape(2 * frames * wide, channels).astype(jnp.float32))
        outer = outer.reshape(2, frames, wide, channels)
        column = lax.broadcasted_iota(jnp.int32, (wide, channels), 0)
        for frame in range(frames):
            for row in range(TALL + 2):
                if row == 0:
                    here, at = outer[0, frame], edge_cells + frame
                elif row == TALL + 1:
                    here, at = outer[1, frame], edge_cells + frames + frame
                else:
                    part, within = divmod(row - 1, pair)
                    here = middle[frame, row - 1]
                    at = part * (edge_cells // 2) + pair * frame + within
                left = jnp.where(column == 0, halo[pl.ds(at, 1), :], pltpu.roll(here, 1, 0))
                at += stored
                right = jnp.where(column == wide - 1, halo[pl.ds(at, 1), :], pltpu.roll(here, wide - 1, 0))
                for part, shifted in enumerate((left, here, right)):
                    hidden[first + ahead + frame, row, :, part * channels:(part + 1) * channels] = (
                        shifted.astype(jnp.bfloat16)
                    )

        @pl.when(group == 0)
        def _():
            load_filters.wait()

        summed = partial[...]
        for time_tap in range(1, TAPS):
            summed = summed + taps(first + time_tap, time_tap)
        result = own + summed
        tile_out[group] = result.astype(jnp.bfloat16).reshape(frames, TALL, wide, channels)

        @pl.when(section < sections - 1)
        def _():
            block = pair * wide
            for frame in range(frames):
                for part in range(TALL // pair):
                    source = (frame * (TALL // pair) + part) * block
                    for n in range(channels // LANES):
                        wide_out[n, pl.ds((part * frames + frame) * block, block), :] = (
                            result[source:source + block, n * LANES:(n + 1) * LANES]
                        )
            for side, at in enumerate((0, wide - 1)):
                parts = [
                    wide_out[n, pl.ds(at, edge_cells, stride=wide), :]
                    for n in range(channels // LANES)
                ]
                edge_out[group, side] = jnp.concatenate(parts, axis=0).astype(jnp.bfloat16)
                for above, start in enumerate((0, frames * block + (pair - 1) * wide)):
                    for lane in range(channels // LANES):
                        corner_out[group, side, above, lane * frames:(lane + 1) * frames] = (
                            wide_out[lane, pl.ds(start + at, frames, stride=block), :]
                            .astype(jnp.bfloat16).astype(jnp.float32)
                        )
            for condition, copy in next_copies(group):
                when(condition, copy.start)

        for near in range(2):
            own_home = (group == tm) & (near == half)

            @pl.when(own_home)
            def _(near=near):
                own_copy(group, near).start()

            @pl.when(jnp.logical_not(own_home))
            def _(near=near):
                home_copy(group, near).start()

        @pl.when(group < groups - 1)
        def _():
            partial[...] = taps(first + frames, 0)

        return carry

    @pl.when(worker)
    def _():
        load_gain.wait()
        lax.fori_loop(0, groups, process, 0)

    for at in range(TILES):
        arrived(out.at[0, :, :, at * wide:(at + 1) * wide], home_sem.at[at])

    @pl.when(sender)
    def _():
        for condition, copy in clip_copies():
            when(condition, copy.wait_send)

    def drain(group, carry):
        @pl.when(section < sections - 1)
        def _():
            for condition, copy in next_copies(group):
                when(condition, copy.wait_send)

        for near in range(2):
            @pl.when(jnp.logical_not((group == tm) & (near == half)))
            def _(near=near):
                home_copy(group, near).wait_send()

        return carry

    @pl.when(worker)
    def _():
        lax.fori_loop(0, groups, drain, 0)


def on_device(clip_features, conv_kernels, norm_gains):
    frames, pair, columns, channels = clip_features.shape
    groups = lax.axis_size("tm")
    wide = columns // TILES
    edge_cells = frames * TALL
    edge = (edge_cells * channels // LANES, LANES)
    corner = (frames * channels // LANES, LANES)
    edges = 2 * (TILES - 1)
    in_hbm = pl.BlockSpec(memory_space=pltpu.HBM)
    return pl.pallas_call(
        chain_kernel,
        out_shape=jax.ShapeDtypeStruct((1, frames, pair, columns, channels), jnp.bfloat16),
        in_specs=[in_hbm] * 3,
        out_specs=in_hbm,
        scratch_shapes=[
            pltpu.VMEM((groups, frames, TALL, wide, channels), jnp.bfloat16),
            pltpu.VMEM((groups, 2, frames, wide, channels), jnp.bfloat16),
            pltpu.VMEM((groups, 2, 2, *edge), jnp.bfloat16),
            pltpu.VMEM((groups, 2, 2, *corner), jnp.float32),
            pltpu.VMEM((TAPS - 1 + groups * frames, TALL + 2, wide, TAPS * channels), jnp.bfloat16),
            pltpu.VMEM((frames * TALL * wide, channels), jnp.float32),
            pltpu.VMEM((2 * (edge_cells + 2 * frames), channels), jnp.float32),
            pltpu.VMEM((2 * (edge_cells + 2 * frames), channels), jnp.float32),
            pltpu.VMEM(conv_kernels.shape[1:], jnp.bfloat16),
            pltpu.VMEM(norm_gains.shape, jnp.float32),
            pltpu.VMEM((channels // LANES, frames * TALL * wide, LANES), jnp.float32),
            pltpu.VMEM((groups, frames, TALL, wide, channels), jnp.bfloat16),
            pltpu.VMEM((groups, 2, *edge), jnp.bfloat16),
            pltpu.VMEM((groups, 2, 2, *corner), jnp.float32),
            pltpu.VMEM((frames, pair, columns, channels), jnp.bfloat16),
            pltpu.VMEM((channels // LANES, frames * pair * columns, LANES), jnp.float32),
            pltpu.VMEM((edges, *edge), jnp.bfloat16),
            pltpu.VMEM((edges, *corner), jnp.float32),
            pltpu.SemaphoreType.DMA((groups, 2)),
            pltpu.SemaphoreType.DMA((groups, 2)),
            pltpu.SemaphoreType.DMA((groups, 2, 2)),
            pltpu.SemaphoreType.DMA((groups, 2, 2)),
            pltpu.SemaphoreType.DMA((TILES,)),
            pltpu.SemaphoreType.DMA((2 * edges + 2 * TILES,)),
            pltpu.SemaphoreType.DMA((groups, 9)),
            pltpu.SemaphoreType.DMA((groups, 2)),
            pltpu.SemaphoreType.DMA((3,)),
        ],
        compiler_params=pltpu.CompilerParams(
            collective_id=0, has_side_effects=True, vmem_limit_bytes=55040 * 2**10
        ),
        name="chain",
    )(clip_features, conv_kernels, norm_gains)


def solution(mesh):
    return jax.shard_map(
        on_device,
        mesh=mesh,
        in_specs=(P("tm", "space", None, None), P("section", None, None, None), P("section", None)),
        out_specs=P("section", "tm", "space", None, None),
        check_vma=False,
    )
```
